128 devices in a mesh: dp: 4 (over y_lo, core), expert: 32 (over y_hi, z, x).
Axes of the slice: x: 4, y: 4 (y_hi: 2, y_lo: 2; y = y_hi * 2 + y_lo), z: 4, core: 2. Of those that a mesh axis runs over, the one named last changes fastest.
Arguments:
- hidden_in: bfloat16 [1024, 4096], P(('dp', 'expert')), may hold values from -6 to 6
- router_weight: bfloat16 [4096, 64], replicated, may hold values from -0.09375 to 0.09375
- expert_gate: bfloat16 [4096, 49152], P(None, ('dp', 'expert')), may hold values from -0.09375 to 0.09375
- expert_up: bfloat16 [4096, 49152], P(None, ('dp', 'expert')), may hold values from -0.09375 to 0.09375
- expert_down: bfloat16 [49152, 4096], P(('dp', 'expert')), may hold values from -0.21875 to 0.21875
- expert_ids: int32 [1024, 8], P(('dp', 'expert')), may hold values from 0 to 63, all different within a row; in each aligned block of 8 rows (0 to 7, 8 to 15, ...) at most 2 rows name the same one
- segment_ids: int32 [4, 256], P('dp'), may hold values from 0 to 31, never falling along the last dimension, each value on 1 to 16 neighbouring positions
- draft_gain: bfloat16 [4096], replicated, may hold values from 0.5 to 1.5
- draft_gate: bfloat16 [4096, 8192], P(None, 'expert'), may hold values from -0.09375 to 0.09375
- draft_up: bfloat16 [4096, 8192], P(None, 'expert'), may hold values from -0.09375 to 0.09375
- draft_down: bfloat16 [8192, 4096], P('expert'), may hold values from -0.0625 to 0.0625
Outputs:
- draft_out: bfloat16 [1024, 4096], P(('dp', 'expert'))
- grad_gate: float32 [4096, 8192], P('dp', 'expert')
- grad_up: float32 [4096, 8192], P('dp', 'expert')
- grad_down: float32 [8192, 4096], P('expert', 'dp')
The draws below stay inside these ranges and needn't reach their ends.
Inputs may be any that keep to these rules, and one draw needn't show every extreme that they name: `expert_ids`: each row names 8 different experts. Among the 8 rows of one device no expert is named more than 2 times, and in every draw some device names some expert exactly 2 times. `segment_ids`: within a batch row the numbers never fall; each document has 1 to 16 tokens and one has exactly 16.
All inputs are finite; a program needn't handle non-finite values.
Results may differ from the reference program's by a relative error of at most 0.035.
Values may be sent and summed in bfloat16 or wider, within the bound.
No kernel may reach another device: no remote copies, remote signals or barrier semaphores. Data moves between devices by JAX's collectives and lax.ppermute only.
A program may use at most 128 MiB of HBM per device.

```python
import math
import jax
import jax.numpy as jnp
import numpy as np
from jax import lax

D = 4096
FF_E = 768
FFD = 8192
TOP = 8
STEPS = 3
TOK_DEV = 8
EXPERTS = 64
CAP = 2
ROWS = 256
BATCHES = 4
TOKENS = 1024
N_EXPERT = 32


def shard_levels(key, dims, shards, smallest, high):
    factor_of = 1.0
    for dim, blocks in shards:
        draws = jax.random.uniform(jax.random.fold_in(jax.random.fold_in(key, 6), dim), (blocks,), jnp.float32, smallest / len(shards), high / len(shards))
        factor_of = factor_of * jnp.repeat(jnp.exp(draws), dims[dim] // blocks).reshape((-1,) + (1,) * (len(dims) - 1 - dim))
    return factor_of


def length_profile(amount, total, bound, skew):
    loads = [(1 << 20) // math.isqrt(rank ** skew) + 1 for rank in range(2, amount + 1)]
    rest, holding = total - bound - (amount - 1), [1] * (amount - 1)
    while rest > 0:
        candidates = [i for i in range(amount - 1) if holding[i] < bound]
        mass, remaining = sum([loads[i] for i in candidates]), rest
        for i in candidates:
            addition = min(bound - holding[i], max(1, remaining * loads[i] // mass), rest)
            holding[i] = holding[i] + addition
            rest = rest - addition
    return np.array([bound] + holding)


def uneven(rng, number_of, total, bound, slope):
    if number_of == 2:
        one = jax.random.randint(rng, (), max(1, total - bound), min(bound, total - 1) + 1)
        return jnp.stack([one, total - one])
    lengths = jnp.asarray(length_profile(number_of, total, bound, slope), jnp.int32)
    twos = (number_of - 1) // 2
    source_of, receiver = lengths[1:1 + 2 * twos:2], lengths[2:2 + 2 * twos:2]
    margin = jnp.minimum(source_of - 1, bound - receiver)
    shifted = jax.random.randint(jax.random.fold_in(rng, 1), (twos,), 0, 1 << 20) % (margin + 1)
    lengths = lengths.at[1:1 + 2 * twos:2].set(source_of - shifted).at[2:2 + 2 * twos:2].set(receiver + shifted)
    return lengths[jax.random.permutation(jax.random.fold_in(rng, 2), number_of)]


def routed_block(rng, own, number, rows, count, top, reach, lean):
    ranking = jax.random.permutation(rng, count)
    heavy_load, usual = load_shares(count, rows * top, reach, lean, True), load_shares(count, rows * top, reach, lean, False)
    places = jnp.arange(count)

    def named(tallies, rotation):
        used = int((tallies > 0).sum())
        fixed = max(1, used // 4)
        passed = fixed + (places - fixed + rotation * (used - fixed)) % max(1, count - fixed)
        return jnp.zeros((count,), jnp.int32).at[ranking[jnp.where(places < fixed, places, passed)]].set(jnp.asarray(tallies, jnp.int32))

    tallies = jnp.where(number % 4 == 0, named(heavy_load, number // 4), named(usual, number - number // 4 - 1))
    mixed = jax.random.permutation(jax.random.fold_in(own, 3), count)
    giver, receiver = mixed[0:count // 2 * 2:2], mixed[1:count // 2 * 2:2]
    margin = jnp.minimum(tallies[giver] - 1, reach - tallies[receiver]) // 2
    margin = jnp.where((giver == ranking[0]) | (receiver == ranking[0]) | (tallies[receiver] == 0), 0, jnp.maximum(margin, 0))
    passed = jax.random.randint(jax.random.fold_in(own, 4), (count // 2,), 0, 1 << 20) % (margin + 1)
    tallies = tallies.at[giver].add(-passed).at[receiver].add(passed)
    members = jnp.searchsorted(jnp.cumsum(tallies), jnp.arange(rows * top), side="right").astype(jnp.int32)
    listing = members.reshape(top, rows).T
    listing = listing[jax.random.permutation(jax.random.fold_in(own, 1), rows)]
    rotation = jax.random.randint(jax.random.fold_in(own, 2), (rows, 1), 0, top)
    return jnp.take_along_axis(listing, (jnp.arange(top)[None, :] + rotation) % top, axis=1)


def load_shares(count, total, reach, lean, full):
    portions = [(1 << 20) // math.isqrt(grade ** lean) + 1 for grade in range(1, count + 1)]
    largest = reach if full else min(reach, max(-(-total // count), total * portions[0] // sum(portions)))
    least = 1 if total - largest >= count - 1 else 0
    counts, rest = [largest] + [least] * (count - 1), total - largest - least * (count - 1)
    while rest > 0:
        movable = [i for i in range(1, count) if counts[i] < largest] or [i for i in range(1, count) if counts[i] < reach]
        pool, left = sum([portions[i] for i in movable]), rest
        for i in movable:
            more = min(reach - counts[i], max(1, left * portions[i] // pool), rest)
            counts[i] = counts[i] + more
            rest = rest - more
    return np.array(counts)


def noise(key, shape, spread, bound, split=(), held_as=jnp.bfloat16):
    array = jax.random.normal(key, shape, jnp.float32) * spread
    if len(split) > 0:
        array = shard_levels(key, shape, split, -0.22, 0.18) * array
    return jnp.clip(array, min=-bound, max=bound).astype(held_as)


def setup_inputs(seed: int = 0) -> dict:
    arg_keys = jax.random.split(jax.random.key(seed), 12)
    hidden_in = noise(arg_keys[0], (TOKENS, D), 1.0, 6.0, ((0, 128),))
    router_weight = noise(arg_keys[1], (D, EXPERTS), D ** -0.5, 0.09375)
    expert_gate = noise(arg_keys[2], (D, EXPERTS * FF_E), D ** -0.5, 0.09375, ((1, 128),))
    expert_up = noise(arg_keys[3], (D, EXPERTS * FF_E), D ** -0.5, 0.09375, ((1, 128),))
    expert_down = noise(arg_keys[4], (EXPERTS * FF_E, D), FF_E ** -0.5, 0.21875, ((0, 128),))
    expert_ids_keys = jax.random.split(jax.random.fold_in(arg_keys[5], 1), TOKENS // TOK_DEV)
    expert_ids_turns = jax.random.permutation(jax.random.fold_in(arg_keys[5], 3), TOKENS // TOK_DEV)
    expert_ids = jax.vmap(lambda own, number: routed_block(jax.random.fold_in(arg_keys[5], 2), own, number, TOK_DEV, EXPERTS, TOP, CAP, 2))(expert_ids_keys, expert_ids_turns).reshape((TOKENS, TOP))
    segment_ids = jax.vmap(lambda own: jnp.searchsorted(jnp.cumsum(uneven(own, ROWS // TOK_DEV, ROWS, 2 * TOK_DEV, 2)), jnp.arange(ROWS), side="right"))(jax.random.split(arg_keys[6], BATCHES)).reshape((BATCHES, ROWS)).astype(jnp.int32)
    draft_gain = jnp.clip(1.0 + 0.1 * jax.random.normal(arg_keys[7], (D,), jnp.float32), 0.5, 1.5).astype(jnp.bfloat16)
    draft_gate = noise(arg_keys[8], (D, FFD), D ** -0.5, 0.09375, ((1, 32),))
    draft_up = noise(arg_keys[9], (D, FFD), D ** -0.5, 0.09375, ((1, 32),))
    draft_down = noise(arg_keys[10], (FFD, D), FFD ** -0.5, 0.0625, ((0, 32),))
    return dict(hidden_in=hidden_in, router_weight=router_weight, expert_gate=expert_gate, expert_up=expert_up, expert_down=expert_down, expert_ids=expert_ids, segment_ids=segment_ids, draft_gain=draft_gain, draft_gate=draft_gate, draft_up=draft_up, draft_down=draft_down)


EPSILON = 1e-06

def normalize(incoming):
    as_float = incoming.astype(jnp.float32)
    inv_rms = lax.rsqrt(lax.optimization_barrier(jnp.mean(as_float * as_float, axis=-1, keepdims=True)) + EPSILON)
    return (as_float, inv_rms)

def silu_terms(gate_pre):
    sigmoid_v = jax.nn.sigmoid(gate_pre)
    return (gate_pre * sigmoid_v, sigmoid_v * (1.0 + gate_pre * (1.0 - sigmoid_v)))

def contract_rows(left_side, right_side):
    return lax.dot_general(left_side, right_side, (((0,), (0,)), ((), ())), preferred_element_type=jnp.float32)

def contract_cols(left_side, right_side):
    return lax.dot_general(left_side, right_side, (((1,), (1,)), ((), ())), preferred_element_type=jnp.float32)

def group_sum(operand_pairs):
    group_width = operand_pairs[0][0].shape[1] // N_EXPERT
    row_count = operand_pairs[0][0].shape[0]
    out_cols = operand_pairs[0][1].shape[1]

    def add_group(group_index, running):
        col_start = jnp.asarray(group_index).astype(jnp.int32) * group_width
        group_term = jnp.zeros((row_count, out_cols), jnp.float32)
        for left_side, right_side in operand_pairs:
            left_piece = lax.dynamic_slice_in_dim(left_side, col_start, group_width, 1)
            right_piece = lax.dynamic_slice_in_dim(right_side, col_start, group_width, 0)
            group_term = group_term + jnp.dot(left_piece, right_piece, preferred_element_type=jnp.float32)
        return running + lax.optimization_barrier(group_term.astype(jnp.bfloat16)).astype(jnp.float32)
    return lax.fori_loop(0, N_EXPERT, add_group, jnp.zeros((row_count, out_cols), jnp.float32))

def reference(hidden_in, router_weight, expert_gate, expert_up, expert_down, expert_ids, segment_ids, draft_gain, draft_gate, draft_up, draft_down):
    as_float, inv_rms = normalize(hidden_in)
    normed = (as_float * inv_rms).astype(jnp.bfloat16)
    logits = jnp.dot(normed, router_weight, preferred_element_type=jnp.float32)
    chosen = jnp.take_along_axis(logits, expert_ids, axis=1)
    weights = jnp.exp(chosen)
    route_probs = weights / lax.optimization_barrier(jnp.sum(weights, axis=1, keepdims=True))
    blocks = TOKENS // TOK_DEV
    pair_count = TOK_DEV * TOP
    flat_ids = expert_ids.reshape(blocks, pair_count).astype(jnp.int32)
    one_hot = (flat_ids[:, :, None] == jnp.arange(EXPERTS, dtype=jnp.int32)[None, None, :]).astype(jnp.int32)
    position = lax.optimization_barrier(jnp.sum(jnp.cumsum(one_hot, axis=1) * one_hot, axis=2)) - 1
    slot_index = (jnp.arange(blocks, dtype=jnp.int32)[:, None] * CAP + position).astype(jnp.int32)
    source_rows = (jnp.arange(blocks, dtype=jnp.int32)[:, None] * TOK_DEV + jnp.arange(pair_count, dtype=jnp.int32)[None, :] // TOP).astype(jnp.int32)
    expert_lists = jnp.zeros((EXPERTS, blocks * CAP, D), jnp.bfloat16).at[flat_ids, slot_index].set(normed[source_rows])
    half_width = FF_E // 2
    gate_stack = expert_gate.reshape(D, EXPERTS, FF_E).transpose(1, 0, 2)
    up_stack = expert_up.reshape(D, EXPERTS, FF_E).transpose(1, 0, 2)
    down_stack = expert_down.reshape(EXPERTS, FF_E, D)

    def run_expert(operands):
        slot_rows, w_gate, w_up, w_down = operands
        running = jnp.zeros((slot_rows.shape[0], D), jnp.float32)
        for half_index in range(2):
            lower = half_index * half_width
            upper = lower + half_width
            gate_pre = jnp.dot(slot_rows, w_gate[:, lower:upper], preferred_element_type=jnp.float32)
            up_pre = jnp.dot(slot_rows, w_up[:, lower:upper], preferred_element_type=jnp.float32)
            expert_act = (jax.nn.silu(gate_pre) * up_pre).astype(jnp.bfloat16)
            piece_out = jnp.dot(expert_act, w_down[lower:upper], preferred_element_type=jnp.float32).astype(jnp.bfloat16)
            running = running + lax.optimization_barrier(piece_out).astype(jnp.float32)
        return running
    outputs = lax.map(run_expert, (expert_lists, gate_stack, up_stack, down_stack))
    picked = outputs[flat_ids, slot_index].reshape(TOKENS, TOP, D)
    moe_out = lax.optimization_barrier(jnp.sum(route_probs[:, :, None] * picked, axis=1))
    top_state = (as_float + moe_out).astype(jnp.bfloat16)
    norm_gain = draft_gain.astype(jnp.float32)
    batch_rows = top_state.reshape(BATCHES, ROWS, D)
    high_pad = jnp.concatenate([batch_rows, jnp.zeros((BATCHES, STEPS, D), jnp.bfloat16)], axis=1)
    seg_pad = jnp.concatenate([segment_ids, jnp.full((BATCHES, STEPS), -1, jnp.int32)], axis=1)
    loss_scale = 1.0 / math.sqrt(TOKENS)
    draft_state = top_state
    saved_steps = []
    for step_index in range(STEPS):
        floats_in, inv_in = normalize(draft_state)
        draft_norm = (floats_in * inv_in * norm_gain).astype(jnp.bfloat16)
        gate_pre = jnp.dot(draft_norm, draft_gate, preferred_element_type=jnp.float32)
        up_pre = jnp.dot(draft_norm, draft_up, preferred_element_type=jnp.float32)
        draft_act = (jax.nn.silu(gate_pre) * up_pre).astype(jnp.bfloat16)
        summed = group_sum(((draft_act, draft_down),))
        new_state = (floats_in + summed).astype(jnp.bfloat16)
        saved_steps.append((draft_state, draft_norm, gate_pre, up_pre, draft_act, new_state))
        draft_state = new_state
    draft_out = draft_state
    grad_gate = jnp.zeros((D, FFD), jnp.float32)
    grad_up = jnp.zeros((D, FFD), jnp.float32)
    grad_down = jnp.zeros((FFD, D), jnp.float32)
    carried = jnp.zeros((TOKENS, D), jnp.float32)
    gate_t = draft_gate.T
    up_t = draft_up.T
    for step_index in reversed(range(STEPS)):
        state_in, draft_norm, gate_pre, up_pre, draft_act, state_out = saved_steps[step_index]
        ahead = step_index + 1
        target_rows = high_pad[:, ahead:ahead + ROWS].reshape(TOKENS, D)
        same_doc = (seg_pad[:, ahead:ahead + ROWS] == segment_ids).reshape(TOKENS, 1)
        grad_state = carried + loss_scale * jnp.where(same_doc, state_out.astype(jnp.float32) - target_rows.astype(jnp.float32), 0.0)
        grad_round = grad_state.astype(jnp.bfloat16)
        grad_down = grad_down + contract_rows(draft_act, grad_round)
        grad_act = contract_cols(grad_round, draft_down)
        silu_value, silu_slope = silu_terms(gate_pre)
        grad_gate_pre = (grad_act * up_pre * silu_slope).astype(jnp.bfloat16)
        grad_up_pre = (grad_act * silu_value).astype(jnp.bfloat16)
        grad_gate = grad_gate + contract_rows(draft_norm, grad_gate_pre)
        grad_up = grad_up + contract_rows(draft_norm, grad_up_pre)
        grad_norm = group_sum(((grad_gate_pre, gate_t), (grad_up_pre, up_t)))
        floats_in, inv_in = normalize(state_in)
        weighted = grad_norm * norm_gain
        grad_in = inv_in * weighted - floats_in * inv_in * inv_in * inv_in * lax.optimization_barrier(jnp.mean(floats_in * weighted, axis=-1, keepdims=True))
        carried = grad_state + grad_in
    return (draft_out, grad_gate, grad_up, grad_down)
```

```python
import math

import jax
import jax.numpy as jnp
from jax import lax
from jax.sharding import Mesh, PartitionSpec as P

STEPS = 3
EPSILON = 1e-06

ALL = ("y_lo", "core", "y_hi", "z", "x")
ROW = ("y_hi", "z", "x")
PLANE = ("z", "x")
REPLICAS = ("y_lo", "core", "y_hi")


def normalize(incoming):
    as_float = incoming.astype(jnp.float32)
    inv_rms = lax.rsqrt(jnp.mean(as_float * as_float, axis=-1, keepdims=True) + EPSILON)
    return (as_float, inv_rms)


def silu_terms(gate_pre):
    sigmoid_v = jax.nn.sigmoid(gate_pre)
    return (gate_pre * sigmoid_v, sigmoid_v * (1.0 + gate_pre * (1.0 - sigmoid_v)))


def contract_rows(left_side, right_side):
    return lax.dot_general(
        left_side, right_side, (((0,), (0,)), ((), ())), preferred_element_type=jnp.float32
    )


def contract_cols(left_side, right_side):
    return lax.dot_general(
        left_side, right_side, (((1,), (1,)), ((), ())), preferred_element_type=jnp.float32
    )


def expert_half(slot_rows, w_gate, w_up, w_down):
    flat_rows = slot_rows.reshape(-1, slot_rows.shape[-1])
    gate_pre = jnp.dot(flat_rows, w_gate, preferred_element_type=jnp.float32)
    up_pre = jnp.dot(flat_rows, w_up, preferred_element_type=jnp.float32)
    expert_act = (jax.nn.silu(gate_pre) * up_pre).astype(jnp.bfloat16)
    piece_out = jnp.dot(expert_act, w_down, preferred_element_type=jnp.float32).astype(jnp.bfloat16)
    return piece_out.reshape(slot_rows.shape)


def spread(incoming):
    members = lax.axis_size("z") * lax.axis_size("x")
    copies = jnp.broadcast_to(incoming[None], (members,) + incoming.shape)
    gathered = lax.all_to_all(copies, PLANE, split_axis=0, concat_axis=0, tiled=True)
    return gathered.reshape((-1, incoming.shape[-1]))


def collect(incoming):
    members = lax.axis_size("z") * lax.axis_size("x")
    parts = incoming.astype(jnp.bfloat16).reshape((members, -1, incoming.shape[-1]))
    received = lax.all_to_all(parts, PLANE, split_axis=0, concat_axis=0, tiled=True)
    return jnp.sum(received.astype(jnp.float32), axis=0)


def other_block(weight):
    half = weight.shape[0] // 2
    core = lax.axis_index("core")
    mine = lax.dynamic_slice_in_dim(weight, core * half, half, 0)
    fetched = lax.ppermute(mine, ("y_lo", "y_hi"), [(0, 3), (3, 0), (1, 2), (2, 1)])
    swapped = lax.ppermute(fetched, "core", [(0, 1), (1, 0)])
    first = jnp.where(core == 0, fetched, swapped)
    second = jnp.where(core == 0, swapped, fetched)
    return jnp.concatenate([first, second], axis=0)


def on_device(
    hidden_in,
    router_weight,
    expert_gate,
    expert_up,
    expert_down,
    expert_ids,
    segment_ids,
    draft_gain,
    draft_gate,
    draft_up,
    draft_down,
):
    tok_rows = hidden_in.shape[0]
    model_width = hidden_in.shape[1]
    top_count = expert_ids.shape[1]
    experts = router_weight.shape[1]
    capacity = 2 * ((tok_rows * top_count + experts - 1) // experts)
    token_count = tok_rows * lax.axis_size(ALL)
    gates = (draft_gate, other_block(draft_gate))
    ups = (draft_up, other_block(draft_up))
    downs = (draft_down, other_block(draft_down))
    as_float, inv_rms = normalize(hidden_in)
    normed = (as_float * inv_rms).astype(jnp.bfloat16)
    logits = jnp.dot(normed, router_weight, preferred_element_type=jnp.float32)
    chosen = jnp.take_along_axis(logits, expert_ids, axis=1)
    weights = jnp.exp(chosen)
    route_probs = weights / jnp.sum(weights, axis=1, keepdims=True)
    flat_ids = expert_ids.reshape(-1)
    one_hot = (flat_ids[:, None] == jnp.arange(experts, dtype=jnp.int32)[None, :]).astype(jnp.int32)
    position = jnp.sum(jnp.cumsum(one_hot, axis=0) * one_hot, axis=1) - 1
    slot_index = flat_ids * capacity + position
    slot_range = jnp.arange(experts * capacity, dtype=jnp.int32)
    picker = (slot_range[:, None] == slot_index[None, :]).astype(jnp.bfloat16)
    repeated = jnp.repeat(normed, top_count, axis=0)
    send_rows = jnp.dot(picker, repeated, preferred_element_type=jnp.float32).astype(jnp.bfloat16)
    send_rows = send_rows.reshape(experts, capacity, model_width)
    placed = (slot_index[:, None] == slot_range[None, :]).astype(jnp.float32)
    mixer = jnp.sum(
        (placed * route_probs.reshape(-1)[:, None]).reshape(
            tok_rows, top_count, experts * capacity
        ),
        axis=1,
    )
    doubled = jnp.broadcast_to(send_rows[:, None], (experts, 2, capacity, model_width)).reshape(
        2 * experts, capacity, model_width
    )
    half_parts = expert_half(
        lax.all_to_all(doubled, ALL, split_axis=0, concat_axis=0, tiled=True),
        expert_gate,
        expert_up,
        expert_down,
    )
    returned = lax.all_to_all(half_parts, ALL, split_axis=0, concat_axis=0, tiled=True)
    results = jnp.sum(
        returned.reshape(experts, 2, capacity, model_width).astype(jnp.float32), axis=1
    )
    results = results.reshape(experts * capacity, model_width)
    moe_out = jnp.dot(
        mixer, results, precision=lax.Precision.HIGHEST, preferred_element_type=jnp.float32
    )
    top_state = (as_float + moe_out).astype(jnp.bfloat16)
    norm_gain = draft_gain.astype(jnp.float32)
    segments = segment_ids[0]
    row_size = lax.axis_size(ROW)
    row_start = lax.axis_index(ROW) * tok_rows
    seg_pad = jnp.concatenate([segments, jnp.full((STEPS,), -1, jnp.int32)], axis=0)
    own_segments = lax.dynamic_slice_in_dim(segments, row_start, tok_rows, 0)
    loss_scale = 1.0 / math.sqrt(token_count)
    following = lax.ppermute(
        top_state, ROW, [(i, (i + row_size - 1) % row_size) for i in range(row_size)]
    )
    high_pad = jnp.concatenate([top_state, following], axis=0)
    draft_state = top_state
    saved_steps = []
    for step_index in range(STEPS):
        floats_in, inv_in = normalize(draft_state)
        draft_norm = spread((floats_in * inv_in * norm_gain).astype(jnp.bfloat16))
        pres = [
            (
                jnp.dot(draft_norm, gate, preferred_element_type=jnp.float32),
                jnp.dot(draft_norm, up, preferred_element_type=jnp.float32),
            )
            for gate, up in zip(gates, ups)
        ]
        acts = [(jax.nn.silu(gate_pre) * up_pre).astype(jnp.bfloat16) for gate_pre, up_pre in pres]
        summed = collect(
            jnp.dot(acts[0], downs[0], preferred_element_type=jnp.float32)
            + jnp.dot(acts[1], downs[1], preferred_element_type=jnp.float32)
        )
        new_state = (floats_in + summed).astype(jnp.bfloat16)
        saved_steps.append((draft_state, draft_norm, pres, acts, new_state))
        draft_state = new_state
    carried = jnp.zeros((tok_rows, model_width), jnp.float32)
    norms, grad_rows, act_lists, gate_lists, up_lists = [], [], [], [], []
    for step_index in reversed(range(STEPS)):
        state_in, draft_norm, pres, acts, state_out = saved_steps[step_index]
        ahead = step_index + 1
        target_rows = high_pad[ahead : ahead + tok_rows]
        same_doc = lax.dynamic_slice_in_dim(seg_pad, row_start + ahead, tok_rows, 0) == own_segments
        grad_state = carried + loss_scale * jnp.where(
            same_doc[:, None], state_out.astype(jnp.float32) - target_rows.astype(jnp.float32), 0.0
        )
        grad_full = spread(grad_state.astype(jnp.bfloat16))
        gate_grads, up_grads = [], []
        for (gate_pre, up_pre), down in zip(pres, downs):
            grad_act = contract_cols(grad_full, down)
            silu_value, silu_slope = silu_terms(gate_pre)
            gate_grads.append((grad_act * up_pre * silu_slope).astype(jnp.bfloat16))
            up_grads.append((grad_act * silu_value).astype(jnp.bfloat16))
        norms.append(draft_norm)
        grad_rows.append(grad_full)
        act_lists.append(acts)
        gate_lists.append(gate_grads)
        up_lists.append(up_grads)
        if step_index == 0:
            break
        grad_norm = collect(
            contract_cols(gate_grads[0], gates[0])
            + contract_cols(up_grads[0], ups[0])
            + contract_cols(gate_grads[1], gates[1])
            + contract_cols(up_grads[1], ups[1])
        )
        floats_in, inv_in = normalize(state_in)
        weighted = grad_norm * norm_gain
        grad_in = inv_in * weighted - floats_in * inv_in * inv_in * inv_in * jnp.mean(
            floats_in * weighted, axis=-1, keepdims=True
        )
        carried = grad_state + grad_in
    y_hi = lax.axis_index("y_hi")

    def in_order(lists):
        own = jnp.concatenate([pair[0] for pair in lists], axis=0)
        other = jnp.concatenate([pair[1] for pair in lists], axis=0)
        return [jnp.where(y_hi == 0, own, other), jnp.where(y_hi == 0, other, own)]

    quarters = lax.axis_size("y_lo") * lax.axis_size("core")
    width = model_width // quarters
    all_norms = jnp.concatenate(norms, axis=0)
    all_grads = jnp.concatenate(grad_rows, axis=0)

    def reduced(parts):
        received = lax.all_to_all(parts, REPLICAS, split_axis=0, concat_axis=0, tiled=True)
        return jnp.sum(received.astype(jnp.float32), axis=0)

    def by_model(lists):
        blocks = [contract_rows(all_norms, block).astype(jnp.bfloat16) for block in in_order(lists)]
        blocks = [block.reshape(quarters, 1, width, -1) for block in blocks]
        return jnp.concatenate(blocks, axis=1).reshape(2 * quarters, width, -1)

    down_blocks = in_order(act_lists)
    down_parts = jnp.stack(
        [
            contract_rows(block, all_grads[:, q * width : (q + 1) * width]).astype(jnp.bfloat16)
            for q in range(quarters)
            for block in down_blocks
        ],
        axis=0,
    )
    grad_down = reduced(down_parts)
    grad_gate = reduced(by_model(gate_lists))
    grad_up = reduced(by_model(up_lists))
    return (draft_state, grad_gate, grad_up, grad_down)


def solution(mesh):
    fine = Mesh(mesh.devices.reshape(2, 2, 2, 4, 4), ALL)
    dp = ("y_lo", "core")
    return jax.shard_map(
        on_device,
        mesh=fine,
        in_specs=(
            P(ALL, None),
            P(),
            P(None, ALL),
            P(None, ALL),
            P(ALL, None),
            P(ALL, None),
            P(dp, None),
            P(),
            P(None, ROW),
            P(None, ROW),
            P(ROW, None),
        ),
        out_specs=(
            P(ALL, None),
            P(dp, ROW),
            P(dp, ROW),
            P(ROW, dp),
        ),
        check_vma=False,
    )
```

```python
import math

import jax
import jax.numpy as jnp
from jax import lax
from jax.sharding import Mesh, PartitionSpec as P

STEPS = 3
EPSILON = 1e-06

ALL = ("y_lo", "core", "y_hi", "z", "x")
ROW = ("y_hi", "z", "x")
PLANE = ("z", "x")
SWAP = [(0, 1), (1, 0)]


def normalize(incoming):
    as_float = incoming.astype(jnp.float32)
    inv_rms = lax.rsqrt(jnp.mean(as_float * as_float, axis=-1, keepdims=True) + EPSILON)
    return (as_float, inv_rms)


def silu_terms(gate_pre):
    sigmoid_v = jax.nn.sigmoid(gate_pre)
    return (gate_pre * sigmoid_v, sigmoid_v * (1.0 + gate_pre * (1.0 - sigmoid_v)))


def contract_rows(left_side, right_side):
    return lax.dot_general(
        left_side, right_side, (((0,), (0,)), ((), ())), preferred_element_type=jnp.float32
    )


def contract_cols(left_side, right_side):
    return lax.dot_general(
        left_side, right_side, (((1,), (1,)), ((), ())), preferred_element_type=jnp.float32
    )


def expert_half(slot_rows, w_gate, w_up, w_down):
    flat_rows = slot_rows.reshape(-1, slot_rows.shape[-1])
    gate_pre = jnp.dot(flat_rows, w_gate, preferred_element_type=jnp.float32)
    up_pre = jnp.dot(flat_rows, w_up, preferred_element_type=jnp.float32)
    expert_act = (jax.nn.silu(gate_pre) * up_pre).astype(jnp.bfloat16)
    piece_out = jnp.dot(expert_act, w_down, preferred_element_type=jnp.float32).astype(jnp.bfloat16)
    return piece_out.reshape(slot_rows.shape)


def spread(incoming):
    members = lax.axis_size("z") * lax.axis_size("x")
    copies = jnp.broadcast_to(incoming[None], (members,) + incoming.shape)
    gathered = lax.all_to_all(copies, PLANE, split_axis=0, concat_axis=0, tiled=True)
    return gathered.reshape((-1, incoming.shape[-1]))


def collect(incoming):
    members = lax.axis_size("z") * lax.axis_size("x")
    parts = incoming.astype(jnp.bfloat16).reshape((members, -1, incoming.shape[-1]))
    received = lax.all_to_all(parts, PLANE, split_axis=0, concat_axis=0, tiled=True)
    return jnp.sum(received.astype(jnp.float32), axis=0)


def halves(incoming):
    width = incoming.shape[1] // 2
    y_lo = lax.axis_index("y_lo")
    own = lax.dynamic_slice_in_dim(incoming, y_lo * width, width, 1)
    far = lax.dynamic_slice_in_dim(incoming, (1 - y_lo) * width, width, 1)
    return own, far


def exchange(own_half, far_half, own_block, far_block):
    def pack(half, block):
        return jnp.concatenate([half, block], axis=1)

    def swap(rows, mask):
        return lax.ppermute(rows, ("y_lo", "y_hi"), [(i, i ^ mask) for i in range(4)])

    return jnp.concatenate(
        [
            pack(own_half, own_block),
            swap(pack(own_half, far_block), 1),
            swap(pack(far_half, own_block), 2),
            swap(pack(far_half, far_block), 3),
        ],
        axis=0,
    )


def other_block(weight):
    half = weight.shape[0] // 2
    core = lax.axis_index("core")
    mine = lax.dynamic_slice_in_dim(weight, core * half, half, 0)
    fetched = lax.ppermute(mine, ("y_lo", "y_hi"), [(0, 3), (3, 0), (1, 2), (2, 1)])
    swapped = lax.ppermute(fetched, "core", SWAP)
    first = jnp.where(core == 0, fetched, swapped)
    second = jnp.where(core == 0, swapped, fetched)
    return jnp.concatenate([first, second], axis=0)


def on_device(
    hidden_in,
    router_weight,
    expert_gate,
    expert_up,
    expert_down,
    expert_ids,
    segment_ids,
    draft_gain,
    draft_gate,
    draft_up,
    draft_down,
):
    tok_rows = hidden_in.shape[0]
    model_width = hidden_in.shape[1]
    top_count = expert_ids.shape[1]
    experts = router_weight.shape[1]
    capacity = 2 * ((tok_rows * top_count + experts - 1) // experts)
    token_count = tok_rows * lax.axis_size(ALL)
    gates = (draft_gate, other_block(draft_gate))
    ups = (draft_up, other_block(draft_up))
    downs = (draft_down, other_block(draft_down))
    as_float, inv_rms = normalize(hidden_in)
    normed = (as_float * inv_rms).astype(jnp.bfloat16)
    logits = jnp.dot(normed, router_weight, preferred_element_type=jnp.float32)
    chosen = jnp.take_along_axis(logits, expert_ids, axis=1)
    weights = jnp.exp(chosen)
    route_probs = weights / jnp.sum(weights, axis=1, keepdims=True)
    flat_ids = expert_ids.reshape(-1)
    one_hot = (flat_ids[:, None] == jnp.arange(experts, dtype=jnp.int32)[None, :]).astype(jnp.int32)
    position = jnp.sum(jnp.cumsum(one_hot, axis=0) * one_hot, axis=1) - 1
    slot_index = flat_ids * capacity + position
    slot_range = jnp.arange(experts * capacity, dtype=jnp.int32)
    picker = (slot_range[:, None] == slot_index[None, :]).astype(jnp.bfloat16)
    repeated = jnp.repeat(normed, top_count, axis=0)
    send_rows = jnp.dot(picker, repeated, preferred_element_type=jnp.float32).astype(jnp.bfloat16)
    send_rows = send_rows.reshape(experts, capacity, model_width)
    placed = (slot_index[:, None] == slot_range[None, :]).astype(jnp.float32)
    mixer = jnp.sum(
        (placed * route_probs.reshape(-1)[:, None]).reshape(
            tok_rows, top_count, experts * capacity
        ),
        axis=1,
    )
    doubled = jnp.broadcast_to(send_rows[:, None], (experts, 2, capacity, model_width)).reshape(
        2 * experts, capacity, model_width
    )
    half_parts = expert_half(
        lax.all_to_all(doubled, ALL, split_axis=0, concat_axis=0, tiled=True),
        expert_gate,
        expert_up,
        expert_down,
    )
    returned = lax.all_to_all(half_parts, ALL, split_axis=0, concat_axis=0, tiled=True)
    results = jnp.sum(
        returned.reshape(experts, 2, capacity, model_width).astype(jnp.float32), axis=1
    )
    results = results.reshape(experts * capacity, model_width)
    moe_out = jnp.dot(
        mixer, results, precision=lax.Precision.HIGHEST, preferred_element_type=jnp.float32
    )
    top_state = (as_float + moe_out).astype(jnp.bfloat16)
    norm_gain = draft_gain.astype(jnp.float32)
    segments = segment_ids[0]
    row_size = lax.axis_size(ROW)
    row_start = lax.axis_index(ROW) * tok_rows
    seg_pad = jnp.concatenate([segments, jnp.full((STEPS,), -1, jnp.int32)], axis=0)
    own_segments = lax.dynamic_slice_in_dim(segments, row_start, tok_rows, 0)
    loss_scale = 1.0 / math.sqrt(token_count)
    following = lax.ppermute(
        top_state, ROW, [(i, (i + row_size - 1) % row_size) for i in range(row_size)]
    )
    high_pad = jnp.concatenate([top_state, following], axis=0)
    draft_state = top_state
    saved_steps, forward_rows = [], []
    for step_index in range(STEPS):
        floats_in, inv_in = normalize(draft_state)
        draft_norm = spread((floats_in * inv_in * norm_gain).astype(jnp.bfloat16))
        pres = [
            (
                jnp.dot(draft_norm, gate, preferred_element_type=jnp.float32),
                jnp.dot(draft_norm, up, preferred_element_type=jnp.float32),
            )
            for gate, up in zip(gates, ups)
        ]
        acts = [(jax.nn.silu(gate_pre) * up_pre).astype(jnp.bfloat16) for gate_pre, up_pre in pres]
        summed = collect(
            jnp.dot(acts[0], downs[0], preferred_element_type=jnp.float32)
            + jnp.dot(acts[1], downs[1], preferred_element_type=jnp.float32)
        )
        new_state = (floats_in + summed).astype(jnp.bfloat16)
        saved_steps.append((draft_state, draft_norm, pres, acts, new_state))
        if step_index < STEPS - 1:
            forward_rows.append(exchange(*halves(draft_norm), *acts))
        draft_state = new_state
    carried = jnp.zeros((tok_rows, model_width), jnp.float32)
    shares = []
    units = draft_gate.shape[1]
    half_width = model_width // 2
    for step_index in reversed(range(STEPS)):
        state_in, draft_norm, pres, acts, state_out = saved_steps[step_index]
        ahead = step_index + 1
        target_rows = high_pad[ahead : ahead + tok_rows]
        same_doc = lax.dynamic_slice_in_dim(seg_pad, row_start + ahead, tok_rows, 0) == own_segments
        grad_state = carried + loss_scale * jnp.where(
            same_doc[:, None], state_out.astype(jnp.float32) - target_rows.astype(jnp.float32), 0.0
        )
        grad_full = spread(grad_state.astype(jnp.bfloat16))
        gate_grads, up_grads = [], []
        for (gate_pre, up_pre), down in zip(pres, downs):
            grad_act = contract_cols(grad_full, down)
            silu_value, silu_slope = silu_terms(gate_pre)
            gate_grads.append((grad_act * up_pre * silu_slope).astype(jnp.bfloat16))
            up_grads.append((grad_act * silu_value).astype(jnp.bfloat16))
        gate_up_rows = [jnp.concatenate(pair, axis=1) for pair in zip(gate_grads, up_grads)]
        if step_index == STEPS - 1:
            norm_own, norm_far = halves(draft_norm)
            grad_own, grad_far = halves(grad_full)
            rows = exchange(
                jnp.concatenate([norm_own, grad_own], axis=1),
                jnp.concatenate([norm_far, grad_far], axis=1),
                *[jnp.concatenate(pair, axis=1) for pair in zip(acts, gate_up_rows)],
            )
            wide, grads, blocks = jnp.split(rows, [half_width, 2 * half_width], axis=1)
            act_rows, gate_rows, up_rows = jnp.split(blocks, 3, axis=1)
        else:
            wide, act_rows = jnp.split(forward_rows[step_index], [half_width], axis=1)
            rows = exchange(*halves(grad_full), *gate_up_rows)
            grads, gate_rows, up_rows = jnp.split(rows, [half_width, half_width + units], axis=1)
        shares.append((wide, grads, act_rows, gate_rows, up_rows))
        if step_index == 0:
            break
        grad_norm = collect(
            contract_cols(gate_grads[0], gates[0])
            + contract_cols(up_grads[0], ups[0])
            + contract_cols(gate_grads[1], gates[1])
            + contract_cols(up_grads[1], ups[1])
        )
        floats_in, inv_in = normalize(state_in)
        weighted = grad_norm * norm_gain
        grad_in = inv_in * weighted - floats_in * inv_in * inv_in * inv_in * jnp.mean(
            floats_in * weighted, axis=-1, keepdims=True
        )
        carried = grad_state + grad_in
    gate_up = sum(
        contract_rows(wide, jnp.concatenate([gate_rows, up_rows], axis=1))
        for wide, _, _, gate_rows, up_rows in shares
    )
    down = sum(contract_rows(act_rows, grads) for _, grads, act_rows, _, _ in shares)
    core = lax.axis_index("core")
    quarter = gate_up.shape[0] // 2

    def add_cores(partial, axis):
        mine = lax.dynamic_slice_in_dim(partial, core * quarter, quarter, axis)
        sent = lax.dynamic_slice_in_dim(partial, (1 - core) * quarter, quarter, axis)
        return mine + lax.ppermute(sent.astype(jnp.bfloat16), "core", SWAP).astype(jnp.float32)

    grad_down = add_cores(down, 1)
    grad_gate_up = add_cores(gate_up, 0)
    grad_gate = grad_gate_up[:, :units]
    grad_up = grad_gate_up[:, units:]
    return (draft_state, grad_gate, grad_up, grad_down)


def solution(mesh):
    fine = Mesh(mesh.devices.reshape(2, 2, 2, 4, 4), ALL)
    dp = ("y_lo", "core")
    return jax.shard_map(
        on_device,
        mesh=fine,
        in_specs=(
            P(ALL, None),
            P(),
            P(None, ALL),
            P(None, ALL),
            P(ALL, None),
            P(ALL, None),
            P(dp, None),
            P(),
            P(None, ROW),
            P(None, ROW),
            P(ROW, None),
        ),
        out_specs=(
            P(ALL, None),
            P(dp, ROW),
            P(dp, ROW),
            P(ROW, dp),
        ),
        check_vma=False,
    )
```

```python
import math

import jax
import jax.numpy as jnp
from jax import lax
from jax.sharding import Mesh, PartitionSpec as P

STEPS = 3
EPSILON = 1e-06

ALL = ("y_lo", "core", "y_hi", "z", "x")
ROW = ("y_hi", "z", "x")
PLANE = ("z", "x")
SWAP = [(0, 1), (1, 0)]


def normalize(incoming):
    as_float = incoming.astype(jnp.float32)
    inv_rms = lax.rsqrt(jnp.mean(as_float * as_float, axis=-1, keepdims=True) + EPSILON)
    return (as_float, inv_rms)


def silu_terms(gate_pre):
    sigmoid_v = jax.nn.sigmoid(gate_pre)
    return (gate_pre * sigmoid_v, sigmoid_v * (1.0 + gate_pre * (1.0 - sigmoid_v)))


def contract_rows(left_side, right_side):
    return lax.dot_general(
        left_side, right_side, (((0,), (0,)), ((), ())), preferred_element_type=jnp.float32
    )


def contract_cols(left_side, right_side):
    return lax.dot_general(
        left_side, right_side, (((1,), (1,)), ((), ())), preferred_element_type=jnp.float32
    )


def expert_half(slot_rows, w_gate, w_up, w_down):
    flat_rows = slot_rows.reshape(-1, slot_rows.shape[-1])
    gate_pre = jnp.dot(flat_rows, w_gate, preferred_element_type=jnp.float32)
    up_pre = jnp.dot(flat_rows, w_up, preferred_element_type=jnp.float32)
    expert_act = (jax.nn.silu(gate_pre) * up_pre).astype(jnp.bfloat16)
    piece_out = jnp.dot(expert_act, w_down, preferred_element_type=jnp.float32).astype(jnp.bfloat16)
    return piece_out.reshape(slot_rows.shape)


def spread(incoming, beside):
    members = lax.axis_size("z") * lax.axis_size("x")
    copies = jnp.broadcast_to(incoming[None], (members,) + incoming.shape)
    gathered = lax.all_to_all(copies, PLANE, split_axis=0, concat_axis=0, tiled=True)
    gathered = gathered.reshape((-1, incoming.shape[-1]))
    return gathered if beside is None else beside.beside_gather(gathered)


def collect(incoming, beside):
    members = lax.axis_size("z") * lax.axis_size("x")
    parts = incoming.astype(jnp.bfloat16).reshape((members, -1, incoming.shape[-1]))
    received = lax.all_to_all(parts, PLANE, split_axis=0, concat_axis=0, tiled=True)
    return jnp.sum(beside.beside_sum(received).astype(jnp.float32), axis=0)


def halves(incoming):
    width = incoming.shape[1] // 2
    y_lo = lax.axis_index("y_lo")
    own = lax.dynamic_slice_in_dim(incoming, y_lo * width, width, 1)
    far = lax.dynamic_slice_in_dim(incoming, (1 - y_lo) * width, width, 1)
    return own, far


def swap(rows, mask):
    return lax.ppermute(rows, ("y_lo", "y_hi"), [(i, i ^ mask) for i in range(4)])


def pack(half, block):
    return jnp.concatenate([half, block], axis=1)


class Exchange:
    def __init__(self, own_half, far_half, own_block, far_block):
        self.rows = [pack(own_half, own_block), swap(pack(own_half, far_block), 1)]
        self.later = [pack(far_half, own_block), pack(far_half, far_block)]

    def beside_sum(self, received):
        received, self.rows[1], *self.later = lax.optimization_barrier(
            (received, self.rows[1], *self.later)
        )
        self.rows += [swap(self.later[0], 2), swap(self.later[1], 3)]
        return received

    def beside_gather(self, gathered):
        gathered, *self.rows[2:] = lax.optimization_barrier((gathered, *self.rows[2:]))
        return gathered

    def gathered(self):
        return jnp.concatenate(self.rows, axis=0)


def fetch_half(weight):
    half = weight.shape[0] // 2
    core = lax.axis_index("core")
    mine = lax.dynamic_slice_in_dim(weight, core * half, half, 0)
    return lax.ppermute(mine, ("y_lo", "y_hi"), [(0, 3), (3, 0), (1, 2), (2, 1)])


def both_halves(fetched):
    core = lax.axis_index("core")
    swapped = lax.ppermute(fetched, "core", SWAP)
    first = jnp.where(core == 0, fetched, swapped)
    second = jnp.where(core == 0, swapped, fetched)
    return jnp.concatenate([first, second], axis=0)


def on_device(
    hidden_in,
    router_weight,
    expert_gate,
    expert_up,
    expert_down,
    expert_ids,
    segment_ids,
    draft_gain,
    draft_gate,
    draft_up,
    draft_down,
):
    tok_rows = hidden_in.shape[0]
    model_width = hidden_in.shape[1]
    top_count = expert_ids.shape[1]
    experts = router_weight.shape[1]
    capacity = 2 * ((tok_rows * top_count + experts - 1) // experts)
    token_count = tok_rows * lax.axis_size(ALL)
    fetches = [fetch_half(weight) for weight in (draft_gate, draft_up, draft_down)]
    as_float, inv_rms = normalize(hidden_in)
    normed = (as_float * inv_rms).astype(jnp.bfloat16)
    logits = jnp.dot(normed, router_weight, preferred_element_type=jnp.float32)
    chosen = jnp.take_along_axis(logits, expert_ids, axis=1)
    weights = jnp.exp(chosen)
    route_probs = weights / jnp.sum(weights, axis=1, keepdims=True)
    flat_ids = expert_ids.reshape(-1)
    one_hot = (flat_ids[:, None] == jnp.arange(experts, dtype=jnp.int32)[None, :]).astype(jnp.int32)
    position = jnp.sum(jnp.cumsum(one_hot, axis=0) * one_hot, axis=1) - 1
    slot_index = flat_ids * capacity + position
    slot_range = jnp.arange(experts * capacity, dtype=jnp.int32)
    picker = (slot_range[:, None] == slot_index[None, :]).astype(jnp.bfloat16)
    repeated = jnp.repeat(normed, top_count, axis=0)
    send_rows = jnp.dot(picker, repeated, preferred_element_type=jnp.float32).astype(jnp.bfloat16)
    send_rows = send_rows.reshape(experts, capacity, model_width)
    placed = (slot_index[:, None] == slot_range[None, :]).astype(jnp.float32)
    mixer = jnp.sum(
        (placed * route_probs.reshape(-1)[:, None]).reshape(
            tok_rows, top_count, experts * capacity
        ),
        axis=1,
    )
    doubled = jnp.broadcast_to(send_rows[:, None], (experts, 2, capacity, model_width)).reshape(
        2 * experts, capacity, model_width
    )
    arrived = lax.all_to_all(doubled, ALL, split_axis=0, concat_axis=0, tiled=True)
    arrived, fetches[0] = lax.optimization_barrier((arrived, fetches[0]))
    half_parts = expert_half(arrived, expert_gate, expert_up, expert_down)
    half_parts, fetches[1] = lax.optimization_barrier((half_parts, fetches[1]))
    returned = lax.all_to_all(half_parts, ALL, split_axis=0, concat_axis=0, tiled=True)
    results = jnp.sum(
        returned.reshape(experts, 2, capacity, model_width).astype(jnp.float32), axis=1
    )
    results = results.reshape(experts * capacity, model_width)
    moe_out = jnp.dot(
        mixer, results, precision=lax.Precision.HIGHEST, preferred_element_type=jnp.float32
    )
    top_state = (as_float + moe_out).astype(jnp.bfloat16)
    top_state, *fetches = lax.optimization_barrier((top_state, *fetches))
    gates, ups, downs = [
        (weight, both_halves(fetched))
        for weight, fetched in zip((draft_gate, draft_up, draft_down), fetches)
    ]
    norm_gain = draft_gain.astype(jnp.float32)
    segments = segment_ids[0]
    row_size = lax.axis_size(ROW)
    row_start = lax.axis_index(ROW) * tok_rows
    seg_pad = jnp.concatenate([segments, jnp.full((STEPS,), -1, jnp.int32)], axis=0)
    own_segments = lax.dynamic_slice_in_dim(segments, row_start, tok_rows, 0)
    loss_scale = 1.0 / math.sqrt(token_count)
    following = lax.ppermute(
        top_state, ROW, [(i, (i + row_size - 1) % row_size) for i in range(row_size)]
    )
    high_pad = jnp.concatenate([top_state, following], axis=0)
    draft_state = top_state
    saved_steps, forward_rows = [], []
    latest = None
    for step_index in range(STEPS):
        floats_in, inv_in = normalize(draft_state)
        draft_norm = spread((floats_in * inv_in * norm_gain).astype(jnp.bfloat16), latest)
        pres = [
            (
                jnp.dot(draft_norm, gate, preferred_element_type=jnp.float32),
                jnp.dot(draft_norm, up, preferred_element_type=jnp.float32),
            )
            for gate, up in zip(gates, ups)
        ]
        acts = [(jax.nn.silu(gate_pre) * up_pre).astype(jnp.bfloat16) for gate_pre, up_pre in pres]
        partial = jnp.dot(acts[0], downs[0], preferred_element_type=jnp.float32) + jnp.dot(
            acts[1], downs[1], preferred_element_type=jnp.float32
        )
        latest = Exchange(*halves(draft_norm), *acts)
        forward_rows.append(latest)
        summed = collect(partial, latest)
        new_state = (floats_in + summed).astype(jnp.bfloat16)
        saved_steps.append((draft_state, draft_norm, pres, acts, new_state))
        draft_state = new_state
    carried = jnp.zeros((tok_rows, model_width), jnp.float32)
    backward_rows = []
    units = draft_gate.shape[1]
    half_width = model_width // 2
    for step_index in reversed(range(STEPS)):
        state_in, draft_norm, pres, acts, state_out = saved_steps[step_index]
        ahead = step_index + 1
        target_rows = high_pad[ahead : ahead + tok_rows]
        same_doc = lax.dynamic_slice_in_dim(seg_pad, row_start + ahead, tok_rows, 0) == own_segments
        grad_state = carried + loss_scale * jnp.where(
            same_doc[:, None], state_out.astype(jnp.float32) - target_rows.astype(jnp.float32), 0.0
        )
        grad_full = spread(grad_state.astype(jnp.bfloat16), latest)
        if step_index == 0:
            own_half, far_half = halves(grad_full)
            grad_shares = [own_half, swap(own_half, 1), swap(far_half, 2), swap(far_half, 3)]
        gate_grads, up_grads = [], []
        for (gate_pre, up_pre), down in zip(pres, downs):
            grad_act = contract_cols(grad_full, down)
            silu_value, silu_slope = silu_terms(gate_pre)
            gate_grads.append((grad_act * up_pre * silu_slope).astype(jnp.bfloat16))
            up_grads.append((grad_act * silu_value).astype(jnp.bfloat16))
        gate_up_rows = [jnp.concatenate(pair, axis=1) for pair in zip(gate_grads, up_grads)]
        if step_index == 0:
            block_shares = [swap(gate_up_rows[i % 2], i) if i else gate_up_rows[0] for i in range(4)]
            break
        latest = Exchange(*halves(grad_full), *gate_up_rows)
        backward_rows.append(latest)
        partial = (
            contract_cols(gate_grads[0], gates[0])
            + contract_cols(up_grads[0], ups[0])
            + contract_cols(gate_grads[1], gates[1])
            + contract_cols(up_grads[1], ups[1])
        )
        grad_norm = collect(partial, latest)
        floats_in, inv_in = normalize(state_in)
        weighted = grad_norm * norm_gain
        grad_in = inv_in * weighted - floats_in * inv_in * inv_in * inv_in * jnp.mean(
            floats_in * weighted, axis=-1, keepdims=True
        )
        carried = grad_state + grad_in
    backward_shares = [jnp.split(rows.gathered(), [half_width], axis=1) for rows in backward_rows]
    backward_shares.append(
        [jnp.concatenate(grad_shares, axis=0), jnp.concatenate(block_shares, axis=0)]
    )
    gate_up, down = 0.0, 0.0
    for rows, (grads, gate_up_rows) in zip(reversed(forward_rows), backward_shares):
        wide, act_rows = jnp.split(rows.gathered(), [half_width], axis=1)
        gate_up = gate_up + contract_rows(wide, gate_up_rows)
        down = down + contract_rows(act_rows, grads)
    core = lax.axis_index("core")
    quarter = gate_up.shape[0] // 2

    def add_cores(partial, axis):
        mine = lax.dynamic_slice_in_dim(partial, core * quarter, quarter, axis)
        sent = lax.dynamic_slice_in_dim(partial, (1 - core) * quarter, quarter, axis)
        return mine + lax.ppermute(sent.astype(jnp.bfloat16), "core", SWAP).astype(jnp.float32)

    grad_down = add_cores(down, 1)
    grad_gate_up = add_cores(gate_up, 0)
    grad_gate = grad_gate_up[:, :units]
    grad_up = grad_gate_up[:, units:]
    return (draft_state, grad_gate, grad_up, grad_down)


def solution(mesh):
    fine = Mesh(mesh.devices.reshape(2, 2, 2, 4, 4), ALL)
    dp = ("y_lo", "core")
    return jax.shard_map(
        on_device,
        mesh=fine,
        in_specs=(
            P(ALL, None),
            P(),
            P(None, ALL),
            P(None, ALL),
            P(ALL, None),
            P(ALL, None),
            P(dp, None),
            P(),
            P(None, ROW),
            P(None, ROW),
            P(ROW, None),
        ),
        out_specs=(
            P(ALL, None),
            P(dp, ROW),
            P(dp, ROW),
            P(ROW, dp),
        ),
        check_vma=False,
    )
```

```python
import math

import jax
import jax.numpy as jnp
from jax import lax
from jax.experimental import pallas as pl
from jax.experimental.pallas import tpu as pltpu
from jax.sharding import Mesh, PartitionSpec as P

STEPS = 3
PARTS = 4
EPSILON = 1e-06

ALL = ("y_lo", "core", "y_hi", "z", "x")
ROW = ("y_hi", "z", "x")
PLANE = ("z", "x")
SWAP = [(0, 1), (1, 0)]


def normalize(incoming):
    as_float = incoming.astype(jnp.float32)
    inv_rms = lax.rsqrt(jnp.mean(as_float * as_float, axis=-1, keepdims=True) + EPSILON)
    return (as_float, inv_rms)


def silu_terms(gate_pre):
    sigmoid_v = jax.nn.sigmoid(gate_pre)
    return (gate_pre * sigmoid_v, sigmoid_v * (1.0 + gate_pre * (1.0 - sigmoid_v)))


def contract_rows(left_side, right_side):
    return lax.dot_general(
        left_side, right_side, (((0,), (0,)), ((), ())), preferred_element_type=jnp.float32
    )


def contract_cols(left_side, right_side):
    return lax.dot_general(
        left_side, right_side, (((1,), (1,)), ((), ())), preferred_element_type=jnp.float32
    )


def expert_kernel(x_ref, gate_hbm, up_hbm, down_hbm, out_ref, gate, up, down, wide, rows, sems):
    copies = [
        pltpu.make_async_copy(source, target, sems.at[i])
        for i, (source, target) in enumerate(((gate_hbm, gate), (up_hbm, up), (down_hbm, down)))
    ]
    for copy in copies:
        copy.start()
    sources, pieces, run = x_ref.shape
    capacity = rows.shape[0] // sources
    parts = pieces // capacity
    lanes = wide.shape[-1]
    for lane in range(run // lanes):
        columns = pl.ds(lane * lanes, lanes)
        wide[lane] = x_ref[:, :, columns].reshape(sources * pieces, lanes).astype(jnp.float32)
        for piece in range(pieces):
            slot, part = divmod(piece, parts)
            rows[
                pl.ds(slot * sources, sources), pl.ds(part * run + lane * lanes, lanes)
            ] = wide[lane, pl.ds(piece, sources, stride=pieces), :].astype(jnp.bfloat16)
    copies[0].wait()
    gate_pre = jnp.dot(rows[...], gate[...], preferred_element_type=jnp.float32)
    copies[1].wait()
    up_pre = jnp.dot(rows[...], up[...], preferred_element_type=jnp.float32)
    act = (gate_pre * jax.nn.sigmoid(gate_pre) * up_pre).astype(jnp.bfloat16)
    copies[2].wait()
    for part in range(parts):
        result = jnp.dot(
            act, down[:, pl.ds(part * run, run)], preferred_element_type=jnp.float32
        )
        for slot in range(capacity):
            for lane in range(run // lanes):
                wide[lane, pl.ds(slot * parts + part, sources, stride=pieces), :] = result[
                    slot * sources : (slot + 1) * sources, lane * lanes : (lane + 1) * lanes
                ]
    for lane in range(run // lanes):
        out_ref[:, :, pl.ds(lane * lanes, lanes)] = (
            wide[lane].astype(jnp.bfloat16).reshape(sources, pieces, lanes)
        )


def expert_half(arrived, w_gate, w_up, w_down, capacity):
    sources, pieces, run = arrived.shape
    width = w_gate.shape[0]
    whole = pl.BlockSpec(memory_space=pltpu.VMEM)
    far = pl.BlockSpec(memory_space=pl.ANY)
    return pl.pallas_call(
        expert_kernel,
        out_shape=jax.ShapeDtypeStruct(arrived.shape, jnp.bfloat16),
        in_specs=[whole, far, far, far],
        out_specs=whole,
        scratch_shapes=[
            pltpu.VMEM(w_gate.shape, jnp.bfloat16),
            pltpu.VMEM(w_up.shape, jnp.bfloat16),
            pltpu.VMEM(w_down.shape, jnp.bfloat16),
            pltpu.VMEM((run // 128, sources * pieces, 128), jnp.float32),
            pltpu.VMEM((sources * capacity, width), jnp.bfloat16),
            pltpu.SemaphoreType.DMA((3,)),
        ],
        compiler_params=pltpu.CompilerParams(vmem_limit_bytes=36 * 1024 * 1024),
        cost_estimate=pl.CostEstimate(
            flops=6 * sources * capacity * width * w_gate.shape[1],
            bytes_accessed=3 * w_gate.size * 2,
            transcendentals=0,
        ),
    )(arrived, w_gate, w_up, w_down)


def spread(incoming, beside):
    members = lax.axis_size("z") * lax.axis_size("x")
    copies = jnp.broadcast_to(incoming[None], (members,) + incoming.shape)
    gathered = lax.all_to_all(copies, PLANE, split_axis=0, concat_axis=0, tiled=True)
    gathered = gathered.reshape((-1, incoming.shape[-1]))
    return gathered if beside is None else beside.beside_gather(gathered)


def collect(incoming, beside):
    members = lax.axis_size("z") * lax.axis_size("x")
    parts = incoming.astype(jnp.bfloat16).reshape((members, -1, incoming.shape[-1]))
    received = lax.all_to_all(parts, PLANE, split_axis=0, concat_axis=0, tiled=True)
    return jnp.sum(beside.beside_sum(received).astype(jnp.float32), axis=0)


def halves(incoming):
    width = incoming.shape[1] // 2
    y_lo = lax.axis_index("y_lo")
    own = lax.dynamic_slice_in_dim(incoming, y_lo * width, width, 1)
    far = lax.dynamic_slice_in_dim(incoming, (1 - y_lo) * width, width, 1)
    return own, far


def swap(rows, mask):
    return lax.ppermute(rows, ("y_lo", "y_hi"), [(i, i ^ mask) for i in range(4)])


def pack(half, block):
    return jnp.concatenate([half, block], axis=1)


class Exchange:
    def __init__(self, own_half, far_half, own_block, far_block):
        self.rows = [pack(own_half, own_block), swap(pack(own_half, far_block), 1)]
        self.later = [pack(far_half, own_block), pack(far_half, far_block)]

    def beside_sum(self, received):
        received, self.rows[1], *self.later = lax.optimization_barrier(
            (received, self.rows[1], *self.later)
        )
        self.rows += [swap(self.later[0], 2), swap(self.later[1], 3)]
        return received

    def beside_gather(self, gathered):
        gathered, *self.rows[2:] = lax.optimization_barrier((gathered, *self.rows[2:]))
        return gathered

    def gathered(self):
        return jnp.concatenate(self.rows, axis=0)


def fetch_half(weight):
    half = weight.shape[0] // 2
    core = lax.axis_index("core")
    mine = lax.dynamic_slice_in_dim(weight, core * half, half, 0)
    return lax.ppermute(mine, ("y_lo", "y_hi"), [(0, 3), (3, 0), (1, 2), (2, 1)])


def both_halves(fetched):
    core = lax.axis_index("core")
    swapped = lax.ppermute(fetched, "core", SWAP)
    first = jnp.where(core == 0, fetched, swapped)
    second = jnp.where(core == 0, swapped, fetched)
    return jnp.concatenate([first, second], axis=0)


def on_device(
    hidden_in,
    router_weight,
    expert_gate,
    expert_up,
    expert_down,
    expert_ids,
    segment_ids,
    draft_gain,
    draft_gate,
    draft_up,
    draft_down,
):
    tok_rows = hidden_in.shape[0]
    model_width = hidden_in.shape[1]
    top_count = expert_ids.shape[1]
    experts = router_weight.shape[1]
    capacity = 2 * ((tok_rows * top_count + experts - 1) // experts)
    token_count = tok_rows * lax.axis_size(ALL)
    fetches = [fetch_half(weight) for weight in (draft_gate, draft_up, draft_down)]
    as_float, inv_rms = normalize(hidden_in)
    normed = (as_float * inv_rms).astype(jnp.bfloat16)
    logits = jnp.dot(normed, router_weight, preferred_element_type=jnp.float32)
    chosen = jnp.take_along_axis(logits, expert_ids, axis=1)
    weights = jnp.exp(chosen)
    route_probs = weights / jnp.sum(weights, axis=1, keepdims=True)
    flat_ids = expert_ids.reshape(-1)
    choice_range = jnp.arange(flat_ids.shape[0], dtype=jnp.int32)
    earlier = (flat_ids[:, None] == flat_ids[None, :]) & (
        choice_range[None, :] < choice_range[:, None]
    )
    slots = flat_ids * capacity + jnp.sum(earlier.astype(jnp.int32), axis=1)
    lines = experts * 2 * capacity * PARTS
    line = jnp.arange(lines, dtype=jnp.int32)
    line_slot = line // (2 * capacity * PARTS) * capacity + line // PARTS % capacity
    piece_slots = jnp.repeat(slots.reshape(tok_rows, top_count), PARTS, axis=0)
    piece_probs = jnp.repeat(route_probs, PARTS, axis=0)
    piece_part = jnp.arange(tok_rows * PARTS, dtype=jnp.int32) % PARTS
    same_part = piece_part[:, None] == (line % PARTS)[None, :]
    hits = [same_part & (piece_slots[:, k : k + 1] == line_slot[None, :]) for k in range(top_count)]
    picker = sum(hit.astype(jnp.float32) for hit in hits).astype(jnp.bfloat16)
    mixer = sum(jnp.where(hit, piece_probs[:, k : k + 1], 0.0) for k, hit in enumerate(hits))
    pieces = normed.reshape(tok_rows * PARTS, model_width // PARTS)
    doubled = contract_rows(picker, pieces).astype(jnp.bfloat16)
    doubled = doubled.reshape(2 * experts, capacity * PARTS, model_width // PARTS)
    arrived = lax.all_to_all(doubled, ALL, split_axis=0, concat_axis=0, tiled=True)
    arrived, fetches[0] = lax.optimization_barrier((arrived, fetches[0]))
    half_parts = expert_half(arrived, expert_gate, expert_up, expert_down, capacity)
    returned = lax.all_to_all(half_parts, ALL, split_axis=0, concat_axis=0, tiled=True)
    returned = returned.reshape(lines, model_width // PARTS)
    first = mixer.astype(jnp.bfloat16)
    rest = mixer - first.astype(jnp.float32)
    second = rest.astype(jnp.bfloat16)
    third = (rest - second.astype(jnp.float32)).astype(jnp.bfloat16)
    mixed = jnp.dot(
        jnp.concatenate([first, second, third], axis=0),
        returned,
        preferred_element_type=jnp.float32,
    )
    moe_out = jnp.sum(mixed.reshape(3, tok_rows * PARTS, -1), axis=0).reshape(tok_rows, model_width)
    top_state = (as_float + moe_out).astype(jnp.bfloat16)
    top_state, fetches[1] = lax.optimization_barrier((top_state, fetches[1]))
    gates, ups = [
        (weight, both_halves(fetched)) for weight, fetched in zip((draft_gate, draft_up), fetches)
    ]
    norm_gain = draft_gain.astype(jnp.float32)
    segments = segment_ids[0]
    row_size = lax.axis_size(ROW)
    row_start = lax.axis_index(ROW) * tok_rows
    seg_pad = jnp.concatenate([segments, jnp.full((STEPS,), -1, jnp.int32)], axis=0)
    own_segments = lax.dynamic_slice_in_dim(segments, row_start, tok_rows, 0)
    loss_scale = 1.0 / math.sqrt(token_count)
    following = lax.ppermute(
        top_state, ROW, [(i, (i + row_size - 1) % row_size) for i in range(row_size)]
    )
    high_pad = jnp.concatenate([top_state, following], axis=0)
    draft_state = top_state
    saved_steps, forward_rows = [], []
    latest = None
    for step_index in range(STEPS):
        floats_in, inv_in = normalize(draft_state)
        draft_norm = spread((floats_in * inv_in * norm_gain).astype(jnp.bfloat16), latest)
        if step_index == 0:
            draft_norm, fetches[2] = lax.optimization_barrier((draft_norm, fetches[2]))
            downs = (draft_down, both_halves(fetches[2]))
        pres = [
            (
                jnp.dot(draft_norm, gate, preferred_element_type=jnp.float32),
                jnp.dot(draft_norm, up, preferred_element_type=jnp.float32),
            )
            for gate, up in zip(gates, ups)
        ]
        acts = [(jax.nn.silu(gate_pre) * up_pre).astype(jnp.bfloat16) for gate_pre, up_pre in pres]
        partial = jnp.dot(acts[0], downs[0], preferred_element_type=jnp.float32) + jnp.dot(
            acts[1], downs[1], preferred_element_type=jnp.float32
        )
        partial, norm_rows, *act_rows = lax.optimization_barrier((partial, draft_norm, *acts))
        latest = Exchange(*halves(norm_rows), *act_rows)
        forward_rows.append(latest)
        summed = collect(partial, latest)
        new_state = (floats_in + summed).astype(jnp.bfloat16)
        saved_steps.append((draft_state, draft_norm, pres, acts, new_state))
        draft_state = new_state
    carried = jnp.zeros((tok_rows, model_width), jnp.float32)
    backward_rows = []
    units = draft_gate.shape[1]
    half_width = model_width // 2
    for step_index in reversed(range(STEPS)):
        state_in, draft_norm, pres, acts, state_out = saved_steps[step_index]
        ahead = step_index + 1
        target_rows = high_pad[ahead : ahead + tok_rows]
        same_doc = lax.dynamic_slice_in_dim(seg_pad, row_start + ahead, tok_rows, 0) == own_segments
        grad_state = carried + loss_scale * jnp.where(
            same_doc[:, None], state_out.astype(jnp.float32) - target_rows.astype(jnp.float32), 0.0
        )
        grad_full = spread(grad_state.astype(jnp.bfloat16), latest)
        if step_index == 0:
            own_half, far_half = halves(grad_full)
            grad_shares = [own_half, swap(own_half, 1), swap(far_half, 2), swap(far_half, 3)]
        gate_grads, up_grads = [], []
        for (gate_pre, up_pre), down in zip(pres, downs):
            grad_act = contract_cols(grad_full, down)
            silu_value, silu_slope = silu_terms(gate_pre)
            gate_grads.append((grad_act * up_pre * silu_slope).astype(jnp.bfloat16))
            up_grads.append((grad_act * silu_value).astype(jnp.bfloat16))
        gate_up_rows = [jnp.concatenate(pair, axis=1) for pair in zip(gate_grads, up_grads)]
        if step_index == 0:
            block_shares = [swap(gate_up_rows[i % 2], i) if i else gate_up_rows[0] for i in range(4)]
            break
        partial = (
            contract_cols(gate_grads[0], gates[0])
            + contract_cols(up_grads[0], ups[0])
            + contract_cols(gate_grads[1], gates[1])
            + contract_cols(up_grads[1], ups[1])
        )
        partial, grad_rows, *gate_up_rows = lax.optimization_barrier(
            (partial, grad_full, *gate_up_rows)
        )
        latest = Exchange(*halves(grad_rows), *gate_up_rows)
        backward_rows.append(latest)
        grad_norm = collect(partial, latest)
        floats_in, inv_in = normalize(state_in)
        weighted = grad_norm * norm_gain
        grad_in = inv_in * weighted - floats_in * inv_in * inv_in * inv_in * jnp.mean(
            floats_in * weighted, axis=-1, keepdims=True
        )
        carried = grad_state + grad_in
    backward_shares = [jnp.split(rows.gathered(), [half_width], axis=1) for rows in backward_rows]
    backward_shares.append(
        [jnp.concatenate(grad_shares, axis=0), jnp.concatenate(block_shares, axis=0)]
    )
    gate_up, down = 0.0, 0.0
    for rows, (grads, gate_up_rows) in zip(reversed(forward_rows), backward_shares):
        wide, act_rows = jnp.split(rows.gathered(), [half_width], axis=1)
        gate_up = gate_up + contract_rows(wide, gate_up_rows)
        down = down + contract_rows(act_rows, grads)
    core = lax.axis_index("core")
    quarter = gate_up.shape[0] // 2

    def add_cores(partial, axis):
        mine = lax.dynamic_slice_in_dim(partial, core * quarter, quarter, axis)
        sent = lax.dynamic_slice_in_dim(partial, (1 - core) * quarter, quarter, axis)
        return mine + lax.ppermute(sent.astype(jnp.bfloat16), "core", SWAP).astype(jnp.float32)

    grad_down = add_cores(down, 1)
    grad_gate_up = add_cores(gate_up, 0)
    grad_gate = grad_gate_up[:, :units]
    grad_up = grad_gate_up[:, units:]
    return (draft_state, grad_gate, grad_up, grad_down)


def solution(mesh):
    fine = Mesh(mesh.devices.reshape(2, 2, 2, 4, 4), ALL)
    dp = ("y_lo", "core")
    return jax.shard_map(
        on_device,
        mesh=fine,
        in_specs=(
            P(ALL, None),
            P(),
            P(None, ALL),
            P(None, ALL),
            P(ALL, None),
            P(ALL, None),
            P(dp, None),
            P(),
            P(None, ROW),
            P(None, ROW),
            P(ROW, None),
        ),
        out_specs=(
            P(ALL, None),
            P(dp, ROW),
            P(dp, ROW),
            P(ROW, dp),
        ),
        check_vma=False,
    )
```

```python
import math

import jax
import jax.numpy as jnp
from jax import lax
from jax.experimental import pallas as pl
from jax.experimental.pallas import tpu as pltpu
from jax.sharding import Mesh, PartitionSpec as P

STEPS = 3
PARTS = 4
EPSILON = 1e-06

ALL = ("y_lo", "core", "y_hi", "z", "x")
ROW = ("y_hi", "z", "x")
PLANE = ("z", "x")
SWAP = [(0, 1), (1, 0)]


def normalize(incoming):
    as_float = incoming.astype(jnp.float32)
    inv_rms = lax.rsqrt(jnp.mean(as_float * as_float, axis=-1, keepdims=True) + EPSILON)
    return (as_float, inv_rms)


def silu_terms(gate_pre):
    sigmoid_v = jax.nn.sigmoid(gate_pre)
    return (gate_pre * sigmoid_v, sigmoid_v * (1.0 + gate_pre * (1.0 - sigmoid_v)))


def contract_rows(left_side, right_side):
    return lax.dot_general(
        left_side, right_side, (((0,), (0,)), ((), ())), preferred_element_type=jnp.float32
    )


def contract_cols(left_side, right_side):
    return lax.dot_general(
        left_side, right_side, (((1,), (1,)), ((), ())), preferred_element_type=jnp.float32
    )


def expert_kernel(x_ref, gate_hbm, up_hbm, down_hbm, out_ref, gate, up, down, wide, rows, sems):
    copies = [
        pltpu.make_async_copy(source, target, sems.at[i])
        for i, (source, target) in enumerate(((gate_hbm, gate), (up_hbm, up), (down_hbm, down)))
    ]
    for copy in copies:
        copy.start()
    sources, pieces, run = x_ref.shape
    capacity = rows.shape[0] // sources
    parts = pieces // capacity
    lanes = wide.shape[-1]
    for lane in range(run // lanes):
        columns = pl.ds(lane * lanes, lanes)
        wide[lane] = x_ref[:, :, columns].reshape(sources * pieces, lanes).astype(jnp.float32)
        for piece in range(pieces):
            slot, part = divmod(piece, parts)
            rows[
                pl.ds(slot * sources, sources), pl.ds(part * run + lane * lanes, lanes)
            ] = wide[lane, pl.ds(piece, sources, stride=pieces), :].astype(jnp.bfloat16)
    copies[0].wait()
    gate_pre = jnp.dot(rows[...], gate[...], preferred_element_type=jnp.float32)
    copies[1].wait()
    up_pre = jnp.dot(rows[...], up[...], preferred_element_type=jnp.float32)
    act = (gate_pre * jax.nn.sigmoid(gate_pre) * up_pre).astype(jnp.bfloat16)
    copies[2].wait()
    for part in range(parts):
        result = jnp.dot(
            act, down[:, pl.ds(part * run, run)], preferred_element_type=jnp.float32
        )
        for slot in range(capacity):
            for lane in range(run // lanes):
                wide[lane, pl.ds(slot * parts + part, sources, stride=pieces), :] = result[
                    slot * sources : (slot + 1) * sources, lane * lanes : (lane + 1) * lanes
                ]
    for lane in range(run // lanes):
        out_ref[:, :, pl.ds(lane * lanes, lanes)] = (
            wide[lane].astype(jnp.bfloat16).reshape(sources, pieces, lanes)
        )


def expert_half(arrived, w_gate, w_up, w_down, capacity):
    sources, pieces, run = arrived.shape
    width = w_gate.shape[0]
    whole = pl.BlockSpec(memory_space=pltpu.VMEM)
    far = pl.BlockSpec(memory_space=pl.ANY)
    return pl.pallas_call(
        expert_kernel,
        out_shape=jax.ShapeDtypeStruct(arrived.shape, jnp.bfloat16),
        in_specs=[whole, far, far, far],
        out_specs=whole,
        scratch_shapes=[
            pltpu.VMEM(w_gate.shape, jnp.bfloat16),
            pltpu.VMEM(w_up.shape, jnp.bfloat16),
            pltpu.VMEM(w_down.shape, jnp.bfloat16),
            pltpu.VMEM((run // 128, sources * pieces, 128), jnp.float32),
            pltpu.VMEM((sources * capacity, width), jnp.bfloat16),
            pltpu.SemaphoreType.DMA((3,)),
        ],
        compiler_params=pltpu.CompilerParams(vmem_limit_bytes=56 * 1024 * 1024),
        cost_estimate=pl.CostEstimate(
            flops=6 * sources * capacity * width * w_gate.shape[1],
            bytes_accessed=3 * w_gate.size * 2,
            transcendentals=0,
        ),
    )(arrived, w_gate, w_up, w_down)


def spread(incoming, beside):
    members = lax.axis_size("z") * lax.axis_size("x")
    copies = jnp.broadcast_to(incoming[None], (members,) + incoming.shape)
    gathered = lax.all_to_all(copies, PLANE, split_axis=0, concat_axis=0, tiled=True)
    gathered = gathered.reshape((-1, incoming.shape[-1]))
    return gathered if beside is None else beside.beside_gather(gathered)


def collect(incoming, beside):
    members = lax.axis_size("z") * lax.axis_size("x")
    parts = incoming.astype(jnp.bfloat16).reshape((members, -1, incoming.shape[-1]))
    received = lax.all_to_all(parts, PLANE, split_axis=0, concat_axis=0, tiled=True)
    return jnp.sum(beside.beside_sum(received).astype(jnp.float32), axis=0)


def halves(incoming):
    width = incoming.shape[1] // 2
    y_lo = lax.axis_index("y_lo")
    own = lax.dynamic_slice_in_dim(incoming, y_lo * width, width, 1)
    far = lax.dynamic_slice_in_dim(incoming, (1 - y_lo) * width, width, 1)
    return own, far


def swap(rows, mask):
    return lax.ppermute(rows, ("y_lo", "y_hi"), [(i, i ^ mask) for i in range(4)])


def pack_kernel(y_lo_ref, wide_ref, *refs):
    blocks, outs = refs[:-4], refs[-4:]
    half = wide_ref.shape[1] // 2
    for mask, out in enumerate(outs):
        start = pl.multiple_of((y_lo_ref[0] ^ (mask // 2)) * half, half)
        out[:, :half] = wide_ref[:, pl.ds(start, half)]
        width = half
        for block in blocks:
            size = block.shape[1] // 2
            first = mask % 2 * size
            out[:, width : width + size] = block[:, first : first + size]
            width += size


def packs(wide, blocks):
    rows = wide.shape[0]
    width = (wide.shape[1] + sum(block.shape[1] for block in blocks)) // 2
    whole = pl.BlockSpec(memory_space=pltpu.VMEM)
    out = jax.ShapeDtypeStruct((rows, width), jnp.bfloat16)
    return pl.pallas_call(
        pack_kernel,
        out_shape=[out] * 4,
        in_specs=[pl.BlockSpec(memory_space=pltpu.SMEM)] + [whole] * (1 + len(blocks)),
        out_specs=[whole] * 4,
        compiler_params=pltpu.CompilerParams(vmem_limit_bytes=16 * 1024 * 1024),
        cost_estimate=pl.CostEstimate(
            flops=0, bytes_accessed=12 * rows * width, transcendentals=0
        ),
    )(lax.axis_index("y_lo").astype(jnp.int32).reshape(1), wide, *blocks)


class Exchange:
    def __init__(self, wide, blocks):
        own, far_y_hi, *self.later = packs(wide, blocks)
        self.rows = [own, swap(far_y_hi, 1)]

    def beside_sum(self, received):
        received, self.rows[1], *self.later = lax.optimization_barrier(
            (received, self.rows[1], *self.later)
        )
        self.rows += [swap(self.later[0], 2), swap(self.later[1], 3)]
        return received

    def beside_gather(self, gathered):
        gathered, *self.rows[2:] = lax.optimization_barrier((gathered, *self.rows[2:]))
        return gathered

    def gathered(self):
        return jnp.concatenate(self.rows, axis=0)


def fetch_half(weight):
    half = weight.shape[0] // 2
    core = lax.axis_index("core")
    mine = lax.dynamic_slice_in_dim(weight, core * half, half, 0)
    return lax.ppermute(mine, ("y_lo", "y_hi"), [(0, 3), (3, 0), (1, 2), (2, 1)])


def both_halves(fetched):
    core = lax.axis_index("core")
    swapped = lax.ppermute(fetched, "core", SWAP)
    first = jnp.where(core == 0, fetched, swapped)
    second = jnp.where(core == 0, swapped, fetched)
    return jnp.concatenate([first, second], axis=0)


def on_device(
    hidden_in,
    router_weight,
    expert_gate,
    expert_up,
    expert_down,
    expert_ids,
    segment_ids,
    draft_gain,
    draft_gate,
    draft_up,
    draft_down,
):
    tok_rows = hidden_in.shape[0]
    model_width = hidden_in.shape[1]
    top_count = expert_ids.shape[1]
    experts = router_weight.shape[1]
    capacity = 2 * ((tok_rows * top_count + experts - 1) // experts)
    token_count = tok_rows * lax.axis_size(ALL)
    fetches = [fetch_half(weight) for weight in (draft_gate, draft_up, draft_down)]
    as_float, inv_rms = normalize(hidden_in)
    normed = (as_float * inv_rms).astype(jnp.bfloat16)
    logits = jnp.dot(normed, router_weight, preferred_element_type=jnp.float32)
    chosen = jnp.take_along_axis(logits, expert_ids, axis=1)
    weights = jnp.exp(chosen)
    route_probs = weights / jnp.sum(weights, axis=1, keepdims=True)
    flat_ids = expert_ids.reshape(-1)
    choice_range = jnp.arange(flat_ids.shape[0], dtype=jnp.int32)
    earlier = (flat_ids[:, None] == flat_ids[None, :]) & (
        choice_range[None, :] < choice_range[:, None]
    )
    slots = flat_ids * capacity + jnp.sum(earlier.astype(jnp.int32), axis=1)
    lines = experts * 2 * capacity * PARTS
    line = jnp.arange(lines, dtype=jnp.int32)
    line_slot = line // (2 * capacity * PARTS) * capacity + line // PARTS % capacity
    piece_slots = jnp.repeat(slots.reshape(tok_rows, top_count), PARTS, axis=0)
    piece_probs = jnp.repeat(route_probs, PARTS, axis=0)
    piece_part = jnp.arange(tok_rows * PARTS, dtype=jnp.int32) % PARTS
    same_part = piece_part[:, None] == (line % PARTS)[None, :]
    hits = [same_part & (piece_slots[:, k : k + 1] == line_slot[None, :]) for k in range(top_count)]
    picker = sum(hit.astype(jnp.float32) for hit in hits).astype(jnp.bfloat16)
    mixer = sum(jnp.where(hit, piece_probs[:, k : k + 1], 0.0) for k, hit in enumerate(hits))
    pieces = normed.reshape(tok_rows * PARTS, model_width // PARTS)
    doubled = contract_rows(picker, pieces).astype(jnp.bfloat16)
    doubled = doubled.reshape(2 * experts, capacity * PARTS, model_width // PARTS)
    arrived = lax.all_to_all(doubled, ALL, split_axis=0, concat_axis=0, tiled=True)
    arrived, fetches[0] = lax.optimization_barrier((arrived, fetches[0]))
    half_parts = expert_half(arrived, expert_gate, expert_up, expert_down, capacity)
    half_parts, fetches[1] = lax.optimization_barrier((half_parts, fetches[1]))
    returned = lax.all_to_all(half_parts, ALL, split_axis=0, concat_axis=0, tiled=True)
    returned = returned.reshape(lines, model_width // PARTS)
    first = mixer.astype(jnp.bfloat16)
    rest = mixer - first.astype(jnp.float32)
    second = rest.astype(jnp.bfloat16)
    third = (rest - second.astype(jnp.float32)).astype(jnp.bfloat16)
    mixed = jnp.dot(
        jnp.concatenate([first, second, third], axis=0),
        returned,
        preferred_element_type=jnp.float32,
    )
    moe_out = jnp.sum(mixed.reshape(3, tok_rows * PARTS, -1), axis=0).reshape(tok_rows, model_width)
    top_state = (as_float + moe_out).astype(jnp.bfloat16)
    top_state, *fetches[:2] = lax.optimization_barrier((top_state, *fetches[:2]))
    gates, ups = [
        (weight, both_halves(fetched)) for weight, fetched in zip((draft_gate, draft_up), fetches)
    ]
    norm_gain = draft_gain.astype(jnp.float32)
    segments = segment_ids[0]
    row_size = lax.axis_size(ROW)
    row_start = lax.axis_index(ROW) * tok_rows
    seg_pad = jnp.concatenate([segments, jnp.full((STEPS,), -1, jnp.int32)], axis=0)
    own_segments = lax.dynamic_slice_in_dim(segments, row_start, tok_rows, 0)
    loss_scale = 1.0 / math.sqrt(token_count)
    following = lax.ppermute(
        top_state, ROW, [(i, (i + row_size - 1) % row_size) for i in range(row_size)]
    )
    high_pad = jnp.concatenate([top_state, following], axis=0)
    draft_state = top_state
    saved_steps, forward_rows = [], []
    latest = None
    for step_index in range(STEPS):
        floats_in, inv_in = normalize(draft_state)
        draft_norm = spread((floats_in * inv_in * norm_gain).astype(jnp.bfloat16), latest)
        if step_index == 0:
            draft_norm, fetches[2] = lax.optimization_barrier((draft_norm, fetches[2]))
            downs = (draft_down, both_halves(fetches[2]))
        pres = [
            (
                jnp.dot(draft_norm, gate, preferred_element_type=jnp.float32),
                jnp.dot(draft_norm, up, preferred_element_type=jnp.float32),
            )
            for gate, up in zip(gates, ups)
        ]
        acts = [(jax.nn.silu(gate_pre) * up_pre).astype(jnp.bfloat16) for gate_pre, up_pre in pres]
        partial = jnp.dot(acts[0], downs[0], preferred_element_type=jnp.float32) + jnp.dot(
            acts[1], downs[1], preferred_element_type=jnp.float32
        )
        partial, norm_rows, act_rows = lax.optimization_barrier(
            (partial, draft_norm, jnp.concatenate(acts, axis=1))
        )
        latest = Exchange(norm_rows, [act_rows])
        forward_rows.append(latest)
        summed = collect(partial, latest)
        new_state = (floats_in + summed).astype(jnp.bfloat16)
        saved_steps.append((draft_state, draft_norm, pres, acts, new_state))
        draft_state = new_state
    carried = jnp.zeros((tok_rows, model_width), jnp.float32)
    backward_rows = []
    units = draft_gate.shape[1]
    half_width = model_width // 2
    for step_index in reversed(range(STEPS)):
        state_in, draft_norm, pres, acts, state_out = saved_steps[step_index]
        ahead = step_index + 1
        target_rows = high_pad[ahead : ahead + tok_rows]
        same_doc = lax.dynamic_slice_in_dim(seg_pad, row_start + ahead, tok_rows, 0) == own_segments
        grad_state = carried + loss_scale * jnp.where(
            same_doc[:, None], state_out.astype(jnp.float32) - target_rows.astype(jnp.float32), 0.0
        )
        grad_full = spread(grad_state.astype(jnp.bfloat16), latest)
        if step_index == 0:
            own_half, far_half = halves(grad_full)
            grad_shares = [own_half, swap(own_half, 1), swap(far_half, 2), swap(far_half, 3)]
        gate_grads, up_grads = [], []
        for (gate_pre, up_pre), down in zip(pres, downs):
            grad_act = contract_cols(grad_full, down)
            silu_value, silu_slope = silu_terms(gate_pre)
            gate_grads.append((grad_act * up_pre * silu_slope).astype(jnp.bfloat16))
            up_grads.append((grad_act * silu_value).astype(jnp.bfloat16))
        if step_index == 0:
            gate_up_rows = [jnp.concatenate(pair, axis=1) for pair in zip(gate_grads, up_grads)]
            block_shares = [swap(gate_up_rows[i % 2], i) if i else gate_up_rows[0] for i in range(4)]
            break
        partial = (
            contract_cols(gate_grads[0], gates[0])
            + contract_cols(up_grads[0], ups[0])
            + contract_cols(gate_grads[1], gates[1])
            + contract_cols(up_grads[1], ups[1])
        )
        partial, grad_rows, gate_rows, up_rows = lax.optimization_barrier(
            (
                partial,
                grad_full,
                jnp.concatenate(gate_grads, axis=1),
                jnp.concatenate(up_grads, axis=1),
            )
        )
        latest = Exchange(grad_rows, [gate_rows, up_rows])
        backward_rows.append(latest)
        grad_norm = collect(partial, latest)
        floats_in, inv_in = normalize(state_in)
        weighted = grad_norm * norm_gain
        grad_in = inv_in * weighted - floats_in * inv_in * inv_in * inv_in * jnp.mean(
            floats_in * weighted, axis=-1, keepdims=True
        )
        carried = grad_state + grad_in
    backward_shares = [jnp.split(rows.gathered(), [half_width], axis=1) for rows in backward_rows]
    backward_shares.append(
        [jnp.concatenate(grad_shares, axis=0), jnp.concatenate(block_shares, axis=0)]
    )
    gate_up, down = 0.0, 0.0
    for rows, (grads, gate_up_rows) in zip(reversed(forward_rows), backward_shares):
        wide, act_rows = jnp.split(rows.gathered(), [half_width], axis=1)
        gate_up = gate_up + contract_rows(wide, gate_up_rows)
        down = down + contract_rows(act_rows, grads)
    core = lax.axis_index("core")
    quarter = gate_up.shape[0] // 2

    def add_cores(partial, axis):
        mine = lax.dynamic_slice_in_dim(partial, core * quarter, quarter, axis)
        sent = lax.dynamic_slice_in_dim(partial, (1 - core) * quarter, quarter, axis)
        return mine, lax.ppermute(sent.astype(jnp.bfloat16), "core", SWAP)

    mine, received = add_cores(gate_up, 0)
    grad_gate = mine[:, :units] + received[:, :units].astype(jnp.float32)
    grad_up = mine[:, units:] + received[:, units:].astype(jnp.float32)
    mine, received = add_cores(down, 1)
    grad_down = mine + received.astype(jnp.float32)
    return (draft_state, grad_gate, grad_up, grad_down)


def solution(mesh):
    fine = Mesh(mesh.devices.reshape(2, 2, 2, 4, 4), ALL)
    dp = ("y_lo", "core")
    return jax.shard_map(
        on_device,
        mesh=fine,
        in_specs=(
            P(ALL, None),
            P(),
            P(None, ALL),
            P(None, ALL),
            P(ALL, None),
            P(ALL, None),
            P(dp, None),
            P(),
            P(None, ROW),
            P(None, ROW),
            P(ROW, None),
        ),
        out_specs=(
            P(ALL, None),
            P(dp, ROW),
            P(dp, ROW),
            P(ROW, dp),
        ),
        check_vma=False,
    )
```

```python
import math

import jax
import jax.numpy as jnp
from jax import lax
from jax.experimental import pallas as pl
from jax.experimental.pallas import tpu as pltpu
from jax.sharding import Mesh, PartitionSpec as P

STEPS = 3
PARTS = 4
EPSILON = 1e-06

ALL = ("y_lo", "core", "y_hi", "z", "x")
ROW = ("y_hi", "z", "x")
PLANE = ("z", "x")
SWAP = [(0, 1), (1, 0)]


def normalize(incoming):
    as_float = incoming.astype(jnp.float32)
    inv_rms = lax.rsqrt(jnp.mean(as_float * as_float, axis=-1, keepdims=True) + EPSILON)
    return (as_float, inv_rms)


def silu_terms(gate_pre):
    sigmoid_v = jax.nn.sigmoid(gate_pre)
    return (gate_pre * sigmoid_v, sigmoid_v * (1.0 + gate_pre * (1.0 - sigmoid_v)))


def contract_rows(left_side, right_side):
    return lax.dot_general(
        left_side, right_side, (((0,), (0,)), ((), ())), preferred_element_type=jnp.float32
    )


def contract_cols(left_side, right_side):
    return lax.dot_general(
        left_side, right_side, (((1,), (1,)), ((), ())), preferred_element_type=jnp.float32
    )


def expert_kernel(x_ref, gate_hbm, up_hbm, down_hbm, out_ref, gate, up, down, wide, rows, sems):
    copies = [
        pltpu.make_async_copy(source, target, sems.at[i])
        for i, (source, target) in enumerate(((gate_hbm, gate), (up_hbm, up), (down_hbm, down)))
    ]
    for copy in copies:
        copy.start()
    sources, pieces, run = x_ref.shape
    capacity = rows.shape[0] // sources
    parts = pieces // capacity
    lanes = wide.shape[-1]
    for lane in range(run // lanes):
        columns = pl.ds(lane * lanes, lanes)
        wide[lane] = x_ref[:, :, columns].reshape(sources * pieces, lanes).astype(jnp.float32)
        for piece in range(pieces):
            slot, part = divmod(piece, parts)
            rows[
                pl.ds(slot * sources, sources), pl.ds(part * run + lane * lanes, lanes)
            ] = wide[lane, pl.ds(piece, sources, stride=pieces), :].astype(jnp.bfloat16)
    copies[0].wait()
    gate_pre = jnp.dot(rows[...], gate[...], preferred_element_type=jnp.float32)
    copies[1].wait()
    up_pre = jnp.dot(rows[...], up[...], preferred_element_type=jnp.float32)
    act = (gate_pre * jax.nn.sigmoid(gate_pre) * up_pre).astype(jnp.bfloat16)
    copies[2].wait()
    for part in range(parts):
        result = jnp.dot(
            act, down[:, pl.ds(part * run, run)], preferred_element_type=jnp.float32
        )
        for slot in range(capacity):
            for lane in range(run // lanes):
                wide[lane, pl.ds(slot * parts + part, sources, stride=pieces), :] = result[
                    slot * sources : (slot + 1) * sources, lane * lanes : (lane + 1) * lanes
                ]
    for lane in range(run // lanes):
        out_ref[:, :, pl.ds(lane * lanes, lanes)] = (
            wide[lane].astype(jnp.bfloat16).reshape(sources, pieces, lanes)
        )


def expert_half(arrived, w_gate, w_up, w_down, capacity):
    sources, pieces, run = arrived.shape
    width = w_gate.shape[0]
    whole = pl.BlockSpec(memory_space=pltpu.VMEM)
    far = pl.BlockSpec(memory_space=pl.ANY)
    return pl.pallas_call(
        expert_kernel,
        out_shape=jax.ShapeDtypeStruct(arrived.shape, jnp.bfloat16),
        in_specs=[whole, far, far, far],
        out_specs=whole,
        scratch_shapes=[
            pltpu.VMEM(w_gate.shape, jnp.bfloat16),
            pltpu.VMEM(w_up.shape, jnp.bfloat16),
            pltpu.VMEM(w_down.shape, jnp.bfloat16),
            pltpu.VMEM((run // 128, sources * pieces, 128), jnp.float32),
            pltpu.VMEM((sources * capacity, width), jnp.bfloat16),
            pltpu.SemaphoreType.DMA((3,)),
        ],
        compiler_params=pltpu.CompilerParams(vmem_limit_bytes=56 * 1024 * 1024),
        cost_estimate=pl.CostEstimate(
            flops=6 * sources * capacity * width * w_gate.shape[1],
            bytes_accessed=3 * w_gate.size * 2,
            transcendentals=0,
        ),
    )(arrived, w_gate, w_up, w_down)


def spread(incoming, beside):
    members = lax.axis_size("z") * lax.axis_size("x")
    copies = jnp.broadcast_to(incoming[None], (members,) + incoming.shape)
    gathered = lax.all_to_all(copies, PLANE, split_axis=0, concat_axis=0, tiled=True)
    gathered = gathered.reshape((-1, incoming.shape[-1]))
    return gathered if beside is None else beside.beside_gather(gathered)


def collect(incoming, beside):
    members = lax.axis_size("z") * lax.axis_size("x")
    parts = incoming.astype(jnp.bfloat16).reshape((members, -1, incoming.shape[-1]))
    received = lax.all_to_all(parts, PLANE, split_axis=0, concat_axis=0, tiled=True)
    return jnp.sum(beside.beside_sum(received).astype(jnp.float32), axis=0)


def halves(incoming):
    width = incoming.shape[1] // 2
    y_lo = lax.axis_index("y_lo")
    own = lax.dynamic_slice_in_dim(incoming, y_lo * width, width, 1)
    far = lax.dynamic_slice_in_dim(incoming, (1 - y_lo) * width, width, 1)
    return own, far


def swap(rows, mask):
    return lax.ppermute(rows, ("y_lo", "y_hi"), [(i, i ^ mask) for i in range(4)])


def pack_kernel(y_lo_ref, wide_ref, *refs):
    blocks, outs = refs[:-4], refs[-4:]
    half = wide_ref.shape[1] // 2
    for mask, out in enumerate(outs):
        start = pl.multiple_of((y_lo_ref[0] ^ (mask // 2)) * half, half)
        out[:, :half] = wide_ref[:, pl.ds(start, half)]
        width = half
        for block in blocks:
            size = block.shape[1] // 2
            first = mask % 2 * size
            out[:, width : width + size] = block[:, first : first + size]
            width += size


def packs(wide, blocks):
    rows = wide.shape[0]
    width = (wide.shape[1] + sum(block.shape[1] for block in blocks)) // 2
    whole = pl.BlockSpec(memory_space=pltpu.VMEM)
    out = jax.ShapeDtypeStruct((rows, width), jnp.bfloat16)
    return pl.pallas_call(
        pack_kernel,
        out_shape=[out] * 4,
        in_specs=[pl.BlockSpec(memory_space=pltpu.SMEM)] + [whole] * (1 + len(blocks)),
        out_specs=[whole] * 4,
        compiler_params=pltpu.CompilerParams(vmem_limit_bytes=8 * 1024 * 1024),
        cost_estimate=pl.CostEstimate(
            flops=0, bytes_accessed=12 * rows * width, transcendentals=0
        ),
    )(lax.axis_index("y_lo").astype(jnp.int32).reshape(1), wide, *blocks)


class Exchange:
    def __init__(self, packed):
        own, far_y_hi, *self.later = packed
        self.rows = [own, swap(far_y_hi, 1)]

    def beside_sum(self, received):
        received, self.rows[1], *self.later = lax.optimization_barrier(
            (received, self.rows[1], *self.later)
        )
        self.rows += [swap(self.later[0], 2), swap(self.later[1], 3)]
        return received

    def beside_gather(self, gathered):
        gathered, *self.rows[2:] = lax.optimization_barrier((gathered, *self.rows[2:]))
        return gathered

    def gathered(self):
        return jnp.concatenate(self.rows, axis=0)


def fetch_half(weight):
    half = weight.shape[0] // 2
    core = lax.axis_index("core")
    mine = lax.dynamic_slice_in_dim(weight, core * half, half, 0)
    return lax.ppermute(mine, ("y_lo", "y_hi"), [(0, 3), (3, 0), (1, 2), (2, 1)])


def both_halves(fetched):
    core = lax.axis_index("core")
    swapped = lax.ppermute(fetched, "core", SWAP)
    first = jnp.where(core == 0, fetched, swapped)
    second = jnp.where(core == 0, swapped, fetched)
    return jnp.concatenate([first, second], axis=0)


def on_device(
    hidden_in,
    router_weight,
    expert_gate,
    expert_up,
    expert_down,
    expert_ids,
    segment_ids,
    draft_gain,
    draft_gate,
    draft_up,
    draft_down,
):
    tok_rows = hidden_in.shape[0]
    model_width = hidden_in.shape[1]
    top_count = expert_ids.shape[1]
    experts = router_weight.shape[1]
    capacity = 2 * ((tok_rows * top_count + experts - 1) // experts)
    token_count = tok_rows * lax.axis_size(ALL)
    fetches = [fetch_half(weight) for weight in (draft_gate, draft_up, draft_down)]
    as_float, inv_rms = normalize(hidden_in)
    normed = (as_float * inv_rms).astype(jnp.bfloat16)
    logits = jnp.dot(normed, router_weight, preferred_element_type=jnp.float32)
    chosen = jnp.take_along_axis(logits, expert_ids, axis=1)
    weights = jnp.exp(chosen)
    route_probs = weights / jnp.sum(weights, axis=1, keepdims=True)
    flat_ids = expert_ids.reshape(-1)
    choice_range = jnp.arange(flat_ids.shape[0], dtype=jnp.int32)
    earlier = (flat_ids[:, None] == flat_ids[None, :]) & (
        choice_range[None, :] < choice_range[:, None]
    )
    slots = flat_ids * capacity + jnp.sum(earlier.astype(jnp.int32), axis=1)
    lines = experts * 2 * capacity * PARTS
    line = jnp.arange(lines, dtype=jnp.int32)
    line_slot = line // (2 * capacity * PARTS) * capacity + line // PARTS % capacity
    piece_slots = jnp.repeat(slots.reshape(tok_rows, top_count), PARTS, axis=0)
    piece_probs = jnp.repeat(route_probs, PARTS, axis=0)
    piece_part = jnp.arange(tok_rows * PARTS, dtype=jnp.int32) % PARTS
    same_part = piece_part[:, None] == (line % PARTS)[None, :]
    hits = [same_part & (piece_slots[:, k : k + 1] == line_slot[None, :]) for k in range(top_count)]
    picker = sum(hit.astype(jnp.float32) for hit in hits).astype(jnp.bfloat16)
    mixer = sum(jnp.where(hit, piece_probs[:, k : k + 1], 0.0) for k, hit in enumerate(hits))
    pieces = normed.reshape(tok_rows * PARTS, model_width // PARTS)
    doubled = contract_rows(picker, pieces).astype(jnp.bfloat16)
    doubled = doubled.reshape(2 * experts, capacity * PARTS, model_width // PARTS)
    arrived = lax.all_to_all(doubled, ALL, split_axis=0, concat_axis=0, tiled=True)
    arrived, fetches[0] = lax.optimization_barrier((arrived, fetches[0]))
    half_parts = expert_half(arrived, expert_gate, expert_up, expert_down, capacity)
    half_parts, fetches[1] = lax.optimization_barrier((half_parts, fetches[1]))
    returned = lax.all_to_all(half_parts, ALL, split_axis=0, concat_axis=0, tiled=True)
    gate_up_weight = jnp.concatenate(
        [draft_gate, draft_up, both_halves(fetches[0]), both_halves(fetches[1])], axis=1
    )
    returned, gate_up_weight = lax.optimization_barrier((returned, gate_up_weight))
    returned = returned.reshape(lines, model_width // PARTS)
    first = mixer.astype(jnp.bfloat16)
    rest = mixer - first.astype(jnp.float32)
    second = rest.astype(jnp.bfloat16)
    third = (rest - second.astype(jnp.float32)).astype(jnp.bfloat16)
    mixed = jnp.dot(
        jnp.concatenate([first, second, third], axis=0),
        returned,
        preferred_element_type=jnp.float32,
    )
    moe_out = jnp.sum(mixed.reshape(3, tok_rows * PARTS, -1), axis=0).reshape(tok_rows, model_width)
    top_state = (as_float + moe_out).astype(jnp.bfloat16)
    units = draft_gate.shape[1]
    half_width = model_width // 2
    norm_gain = draft_gain.astype(jnp.float32)
    segments = segment_ids[0]
    row_size = lax.axis_size(ROW)
    row_start = lax.axis_index(ROW) * tok_rows
    seg_pad = jnp.concatenate([segments, jnp.full((STEPS,), -1, jnp.int32)], axis=0)
    own_segments = lax.dynamic_slice_in_dim(segments, row_start, tok_rows, 0)
    loss_scale = 1.0 / math.sqrt(token_count)
    following = lax.ppermute(
        top_state, ROW, [(i, (i + row_size - 1) % row_size) for i in range(row_size)]
    )
    high_pad = jnp.concatenate([top_state, following], axis=0)
    draft_state = top_state
    saved_steps, forward_rows = [], []
    latest = None
    for step_index in range(STEPS):
        floats_in, inv_in = normalize(draft_state)
        draft_norm = spread((floats_in * inv_in * norm_gain).astype(jnp.bfloat16), latest)
        if step_index == 0:
            draft_norm, fetches[2] = lax.optimization_barrier((draft_norm, fetches[2]))
            down_weight = jnp.concatenate([draft_down, both_halves(fetches[2])], axis=0)
        pres = jnp.split(
            jnp.dot(draft_norm, gate_up_weight, preferred_element_type=jnp.float32), 4, axis=1
        )
        acts = jnp.concatenate(
            [jax.nn.silu(pres[0]) * pres[1], jax.nn.silu(pres[2]) * pres[3]], axis=1
        ).astype(jnp.bfloat16)
        packed = packs(draft_norm, [acts])
        acts, *packed = lax.optimization_barrier((acts, *packed))
        partial = jnp.dot(acts, down_weight, preferred_element_type=jnp.float32)
        latest = Exchange(packed)
        forward_rows.append(latest)
        summed = collect(partial, latest)
        new_state = (floats_in + summed).astype(jnp.bfloat16)
        saved_steps.append((draft_state, pres, new_state))
        draft_state = new_state
    carried = jnp.zeros((tok_rows, model_width), jnp.float32)
    backward_rows = []
    for step_index in reversed(range(STEPS)):
        state_in, pres, state_out = saved_steps[step_index]
        ahead = step_index + 1
        target_rows = high_pad[ahead : ahead + tok_rows]
        same_doc = lax.dynamic_slice_in_dim(seg_pad, row_start + ahead, tok_rows, 0) == own_segments
        grad_state = carried + loss_scale * jnp.where(
            same_doc[:, None], state_out.astype(jnp.float32) - target_rows.astype(jnp.float32), 0.0
        )
        own_rows = grad_state.astype(jnp.bfloat16)
        grad_full = spread(own_rows, latest)
        if step_index == 0:
            own_half, far_half = halves(own_rows)
            others = [swap(own_half, 1), swap(far_half, 2), swap(far_half, 3)]
            grad_full, *others = lax.optimization_barrier((grad_full, *others))
            other_grads = spread(jnp.concatenate(others, axis=0), None)
        grad_act = jnp.split(contract_cols(grad_full, down_weight), 2, axis=1)
        gate_up_grads = []
        for block, block_grad in enumerate(grad_act):
            silu_value, silu_slope = silu_terms(pres[2 * block])
            gate_up_grads.append(block_grad * pres[2 * block + 1] * silu_slope)
            gate_up_grads.append(block_grad * silu_value)
        gate_up_grads = jnp.concatenate(gate_up_grads, axis=1).astype(jnp.bfloat16)
        if step_index == 0:
            own_block, far_block = jnp.split(gate_up_grads, 2, axis=1)
            gate_up_shares = [own_block, swap(far_block, 1), swap(own_block, 2), swap(far_block, 3)]
            break
        packed = packs(grad_full, [gate_up_grads])
        gate_up_grads, *packed = lax.optimization_barrier((gate_up_grads, *packed))
        partial = contract_cols(gate_up_grads, gate_up_weight)
        latest = Exchange(packed)
        backward_rows.append(latest)
        grad_norm = collect(partial, latest)
        floats_in, inv_in = normalize(state_in)
        weighted = grad_norm * norm_gain
        grad_in = inv_in * weighted - floats_in * inv_in * inv_in * inv_in * jnp.mean(
            floats_in * weighted, axis=-1, keepdims=True
        )
        carried = grad_state + grad_in
    gate_up, down = 0.0, 0.0
    for forward, backward in zip(reversed(forward_rows), backward_rows):
        wide, act_rows = jnp.split(forward.gathered(), [half_width], axis=1)
        grads, gate_up_rows = jnp.split(backward.gathered(), [half_width], axis=1)
        gate_up = gate_up + contract_rows(wide, gate_up_rows)
        down = down + contract_rows(act_rows, grads)
    wide = jnp.concatenate([rows[:, :half_width] for rows in forward_rows[0].rows], axis=0)
    gate_up = gate_up + contract_rows(wide, jnp.concatenate(gate_up_shares, axis=0))
    own_acts, *other_acts = [rows[:, half_width:] for rows in forward_rows[0].rows]
    other_acts = jnp.stack([acts.reshape(-1, tok_rows, units) for acts in other_acts], axis=1)
    down = down + contract_rows(own_acts, halves(grad_full)[0])
    down = down + contract_rows(other_acts.reshape(-1, units), other_grads)
    core = lax.axis_index("core")
    quarter = gate_up.shape[0] // 2

    def add_cores(partial, axis):
        mine = lax.dynamic_slice_in_dim(partial, core * quarter, quarter, axis)
        sent = lax.dynamic_slice_in_dim(partial, (1 - core) * quarter, quarter, axis)
        return mine, lax.ppermute(sent.astype(jnp.bfloat16), "core", SWAP)

    mine, received = add_cores(gate_up, 0)
    grad_gate = mine[:, :units] + received[:, :units].astype(jnp.float32)
    grad_up = mine[:, units:] + received[:, units:].astype(jnp.float32)
    mine, received = add_cores(down, 1)
    grad_down = mine + received.astype(jnp.float32)
    return (draft_state, grad_gate, grad_up, grad_down)


def solution(mesh):
    fine = Mesh(mesh.devices.reshape(2, 2, 2, 4, 4), ALL)
    dp = ("y_lo", "core")
    return jax.shard_map(
        on_device,
        mesh=fine,
        in_specs=(
            P(ALL, None),
            P(),
            P(None, ALL),
            P(None, ALL),
            P(ALL, None),
            P(ALL, None),
            P(dp, None),
            P(),
            P(None, ROW),
            P(None, ROW),
            P(ROW, None),
        ),
        out_specs=(
            P(ALL, None),
            P(dp, ROW),
            P(dp, ROW),
            P(ROW, dp),
        ),
        check_vma=False,
    )
```

```python
import functools
import math

import jax
import jax.numpy as jnp
from jax import lax
from jax.experimental import pallas as pl
from jax.experimental.pallas import tpu as pltpu
from jax.sharding import Mesh, PartitionSpec as P

STEPS = 3
PARTS = 4
EPSILON = 1e-06

ALL = ("y_lo", "core", "y_hi", "z", "x")
ROW = ("y_hi", "z", "x")
PLANE = ("z", "x")
SWAP = [(0, 1), (1, 0)]


def normalize(incoming):
    as_float = incoming.astype(jnp.float32)
    inv_rms = lax.rsqrt(jnp.mean(as_float * as_float, axis=-1, keepdims=True) + EPSILON)
    return (as_float, inv_rms)


def silu_terms(gate_pre):
    sigmoid_v = jax.nn.sigmoid(gate_pre)
    return (gate_pre * sigmoid_v, sigmoid_v * (1.0 + gate_pre * (1.0 - sigmoid_v)))


def contract_rows(left_side, right_side):
    return lax.dot_general(
        left_side, right_side, (((0,), (0,)), ((), ())), preferred_element_type=jnp.float32
    )


def contract_cols(left_side, right_side):
    return lax.dot_general(
        left_side, right_side, (((1,), (1,)), ((), ())), preferred_element_type=jnp.float32
    )


def expert_kernel(x_ref, gate_hbm, up_hbm, down_hbm, out_ref, gate, up, down, wide, rows, sems):
    copies = [
        pltpu.make_async_copy(source, target, sems.at[i])
        for i, (source, target) in enumerate(((gate_hbm, gate), (up_hbm, up), (down_hbm, down)))
    ]
    for copy in copies:
        copy.start()
    sources, pieces, run = x_ref.shape
    capacity = rows.shape[0] // sources
    parts = pieces // capacity
    lanes = wide.shape[-1]
    for lane in range(run // lanes):
        columns = pl.ds(lane * lanes, lanes)
        wide[lane] = x_ref[:, :, columns].reshape(sources * pieces, lanes).astype(jnp.float32)
        for piece in range(pieces):
            slot, part = divmod(piece, parts)
            rows[
                pl.ds(slot * sources, sources), pl.ds(part * run + lane * lanes, lanes)
            ] = wide[lane, pl.ds(piece, sources, stride=pieces), :].astype(jnp.bfloat16)
    copies[0].wait()
    gate_pre = jnp.dot(rows[...], gate[...], preferred_element_type=jnp.float32)
    copies[1].wait()
    up_pre = jnp.dot(rows[...], up[...], preferred_element_type=jnp.float32)
    act = (gate_pre * jax.nn.sigmoid(gate_pre) * up_pre).astype(jnp.bfloat16)
    copies[2].wait()
    for part in range(parts):
        result = jnp.dot(
            act, down[:, pl.ds(part * run, run)], preferred_element_type=jnp.float32
        )
        for slot in range(capacity):
            for lane in range(run // lanes):
                wide[lane, pl.ds(slot * parts + part, sources, stride=pieces), :] = result[
                    slot * sources : (slot + 1) * sources, lane * lanes : (lane + 1) * lanes
                ]
    for lane in range(run // lanes):
        out_ref[:, :, pl.ds(lane * lanes, lanes)] = (
            wide[lane].astype(jnp.bfloat16).reshape(sources, pieces, lanes)
        )


def expert_half(arrived, w_gate, w_up, w_down, capacity):
    sources, pieces, run = arrived.shape
    width = w_gate.shape[0]
    whole = pl.BlockSpec(memory_space=pltpu.VMEM)
    far = pl.BlockSpec(memory_space=pl.ANY)
    return pl.pallas_call(
        expert_kernel,
        out_shape=jax.ShapeDtypeStruct(arrived.shape, jnp.bfloat16),
        in_specs=[whole, far, far, far],
        out_specs=whole,
        scratch_shapes=[
            pltpu.VMEM(w_gate.shape, jnp.bfloat16),
            pltpu.VMEM(w_up.shape, jnp.bfloat16),
            pltpu.VMEM(w_down.shape, jnp.bfloat16),
            pltpu.VMEM((run // 128, sources * pieces, 128), jnp.float32),
            pltpu.VMEM((sources * capacity, width), jnp.bfloat16),
            pltpu.SemaphoreType.DMA((3,)),
        ],
        compiler_params=pltpu.CompilerParams(vmem_limit_bytes=56 * 1024 * 1024),
        cost_estimate=pl.CostEstimate(
            flops=6 * sources * capacity * width * w_gate.shape[1],
            bytes_accessed=3 * w_gate.size * 2,
            transcendentals=0,
        ),
    )(arrived, w_gate, w_up, w_down)


def spread(incoming, beside):
    members = lax.axis_size("z") * lax.axis_size("x")
    copies = jnp.broadcast_to(incoming[None], (members,) + incoming.shape)
    gathered = lax.all_to_all(copies, PLANE, split_axis=0, concat_axis=0, tiled=True)
    gathered = gathered.reshape((-1, incoming.shape[-1]))
    return gathered if beside is None else beside.beside_gather(gathered)


def collect(incoming, beside):
    members = lax.axis_size("z") * lax.axis_size("x")
    parts = incoming.astype(jnp.bfloat16).reshape((members, -1, incoming.shape[-1]))
    received = lax.all_to_all(parts, PLANE, split_axis=0, concat_axis=0, tiled=True)
    return jnp.sum(beside.beside_sum(received).astype(jnp.float32), axis=0)


def halves(incoming):
    width = incoming.shape[1] // 2
    y_lo = lax.axis_index("y_lo")
    own = lax.dynamic_slice_in_dim(incoming, y_lo * width, width, 1)
    far = lax.dynamic_slice_in_dim(incoming, (1 - y_lo) * width, width, 1)
    return own, far


def swap(rows, mask):
    return lax.ppermute(rows, ("y_lo", "y_hi"), [(i, i ^ mask) for i in range(4)])


def pack_kernel(y_lo_ref, wide_ref, *refs):
    blocks, outs = refs[:-4], refs[-4:]
    half = wide_ref.shape[1] // 2
    for mask, out in enumerate(outs):
        start = pl.multiple_of((y_lo_ref[0] ^ (mask // 2)) * half, half)
        out[:, :half] = wide_ref[:, pl.ds(start, half)]
        width = half
        for block in blocks:
            size = block.shape[1] // 2
            first = mask % 2 * size
            out[:, width : width + size] = block[:, first : first + size]
            width += size


def packs(wide, blocks):
    rows = wide.shape[0]
    width = (wide.shape[1] + sum(block.shape[1] for block in blocks)) // 2
    whole = pl.BlockSpec(memory_space=pltpu.VMEM)
    out = jax.ShapeDtypeStruct((rows, width), jnp.bfloat16)
    return pl.pallas_call(
        pack_kernel,
        out_shape=[out] * 4,
        in_specs=[pl.BlockSpec(memory_space=pltpu.SMEM)] + [whole] * (1 + len(blocks)),
        out_specs=[whole] * 4,
        compiler_params=pltpu.CompilerParams(vmem_limit_bytes=8 * 1024 * 1024),
        cost_estimate=pl.CostEstimate(
            flops=0, bytes_accessed=12 * rows * width, transcendentals=0
        ),
    )(lax.axis_index("y_lo").astype(jnp.int32).reshape(1), wide, *blocks)


class Exchange:
    def __init__(self, packed):
        own, far_y_hi, *self.later = packed
        self.rows = [own, swap(far_y_hi, 1)]

    def beside_sum(self, received):
        received, self.rows[1], *self.later = lax.optimization_barrier(
            (received, self.rows[1], *self.later)
        )
        self.rows += [swap(self.later[0], 2), swap(self.later[1], 3)]
        return received

    def beside_gather(self, gathered):
        gathered, *self.rows[2:] = lax.optimization_barrier((gathered, *self.rows[2:]))
        return gathered

    def gathered(self):
        return jnp.concatenate(self.rows, axis=0)


def fetch_half(weight):
    half = weight.shape[0] // 2
    core = lax.axis_index("core")
    mine = lax.dynamic_slice_in_dim(weight, core * half, half, 0)
    return lax.ppermute(mine, ("y_lo", "y_hi"), [(0, 3), (3, 0), (1, 2), (2, 1)])


def assemble_kernel(axis, core_ref, *refs):
    out, sems = refs[-2:]
    count = (len(refs) - 2) // 3
    size = refs[0].shape[axis]
    half = refs[count].shape[0]
    core = core_ref[0]
    places = []

    def place(source, block, start):
        rows = source.shape[0]
        if axis == 1:
            target = out.at[pl.ds(start, rows), pl.ds(block * size, size)]
        else:
            target = out.at[pl.ds(block * size + start, rows), :]
        places.append((source, target))

    for i in range(count):
        place(refs[i], i, 0)
        place(refs[count + i], count + i, pl.multiple_of(core * half, half))
        place(refs[2 * count + i], count + i, pl.multiple_of((1 - core) * half, half))
    copies = [
        pltpu.make_async_copy(source, target, sems.at[k])
        for k, (source, target) in enumerate(places)
    ]
    for copy in copies:
        copy.start()
    for copy in copies:
        copy.wait()


def assemble(owns, fetched, axis):
    swapped = [lax.ppermute(half, "core", SWAP) for half in fetched]
    shape = list(owns[0].shape)
    shape[axis] *= 2 * len(owns)
    far = pl.BlockSpec(memory_space=pl.ANY)
    parts = [*owns, *fetched, *swapped]
    return pl.pallas_call(
        functools.partial(assemble_kernel, axis),
        out_shape=jax.ShapeDtypeStruct(tuple(shape), jnp.bfloat16),
        in_specs=[pl.BlockSpec(memory_space=pltpu.SMEM)] + [far] * len(parts),
        out_specs=far,
        scratch_shapes=[pltpu.SemaphoreType.DMA((len(parts),))],
        cost_estimate=pl.CostEstimate(
            flops=0, bytes_accessed=4 * math.prod(shape), transcendentals=0
        ),
    )(lax.axis_index("core").astype(jnp.int32).reshape(1), *parts)


def on_device(
    hidden_in,
    router_weight,
    expert_gate,
    expert_up,
    expert_down,
    expert_ids,
    segment_ids,
    draft_gain,
    draft_gate,
    draft_up,
    draft_down,
):
    tok_rows = hidden_in.shape[0]
    model_width = hidden_in.shape[1]
    top_count = expert_ids.shape[1]
    experts = router_weight.shape[1]
    capacity = 2 * ((tok_rows * top_count + experts - 1) // experts)
    token_count = tok_rows * lax.axis_size(ALL)
    fetches = [fetch_half(weight) for weight in (draft_gate, draft_up, draft_down)]
    as_float, inv_rms = normalize(hidden_in)
    normed = (as_float * inv_rms).astype(jnp.bfloat16)
    logits = jnp.dot(normed, router_weight, preferred_element_type=jnp.float32)
    chosen = jnp.take_along_axis(logits, expert_ids, axis=1)
    weights = jnp.exp(chosen)
    route_probs = weights / jnp.sum(weights, axis=1, keepdims=True)
    flat_ids = expert_ids.reshape(-1)
    choice_range = jnp.arange(flat_ids.shape[0], dtype=jnp.int32)
    earlier = (flat_ids[:, None] == flat_ids[None, :]) & (
        choice_range[None, :] < choice_range[:, None]
    )
    slots = flat_ids * capacity + jnp.sum(earlier.astype(jnp.int32), axis=1)
    lines = experts * 2 * capacity * PARTS
    line = jnp.arange(lines, dtype=jnp.int32)
    line_slot = line // (2 * capacity * PARTS) * capacity + line // PARTS % capacity
    piece_slots = jnp.repeat(slots.reshape(tok_rows, top_count), PARTS, axis=0)
    piece_probs = jnp.repeat(route_probs, PARTS, axis=0)
    piece_part = jnp.arange(tok_rows * PARTS, dtype=jnp.int32) % PARTS
    same_part = piece_part[:, None] == (line % PARTS)[None, :]
    hits = [same_part & (piece_slots[:, k : k + 1] == line_slot[None, :]) for k in range(top_count)]
    picker = sum(hit.astype(jnp.float32) for hit in hits).astype(jnp.bfloat16)
    mixer = sum(jnp.where(hit, piece_probs[:, k : k + 1], 0.0) for k, hit in enumerate(hits))
    pieces = normed.reshape(tok_rows * PARTS, model_width // PARTS)
    doubled = contract_rows(picker, pieces).astype(jnp.bfloat16)
    doubled = doubled.reshape(2 * experts, capacity * PARTS, model_width // PARTS)
    arrived = lax.all_to_all(doubled, ALL, split_axis=0, concat_axis=0, tiled=True)
    arrived, fetches[0] = lax.optimization_barrier((arrived, fetches[0]))
    half_parts = expert_half(arrived, expert_gate, expert_up, expert_down, capacity)
    half_parts, fetches[1] = lax.optimization_barrier((half_parts, fetches[1]))
    returned = lax.all_to_all(half_parts, ALL, split_axis=0, concat_axis=0, tiled=True)
    gate_up_weight = assemble([draft_gate, draft_up], fetches[:2], 1)
    returned, gate_up_weight = lax.optimization_barrier((returned, gate_up_weight))
    returned = returned.reshape(lines, model_width // PARTS)
    first = mixer.astype(jnp.bfloat16)
    rest = mixer - first.astype(jnp.float32)
    second = rest.astype(jnp.bfloat16)
    third = (rest - second.astype(jnp.float32)).astype(jnp.bfloat16)
    mixed = jnp.dot(
        jnp.concatenate([first, second, third], axis=0),
        returned,
        preferred_element_type=jnp.float32,
    )
    moe_out = jnp.sum(mixed.reshape(3, tok_rows * PARTS, -1), axis=0).reshape(tok_rows, model_width)
    top_state = (as_float + moe_out).astype(jnp.bfloat16)
    units = draft_gate.shape[1]
    half_width = model_width // 2
    norm_gain = draft_gain.astype(jnp.float32)
    segments = segment_ids[0]
    row_size = lax.axis_size(ROW)
    row_start = lax.axis_index(ROW) * tok_rows
    seg_pad = jnp.concatenate([segments, jnp.full((STEPS,), -1, jnp.int32)], axis=0)
    own_segments = lax.dynamic_slice_in_dim(segments, row_start, tok_rows, 0)
    loss_scale = 1.0 / math.sqrt(token_count)
    following = lax.ppermute(
        top_state, ROW, [(i, (i + row_size - 1) % row_size) for i in range(row_size)]
    )
    high_pad = jnp.concatenate([top_state, following], axis=0)
    draft_state = top_state
    saved_steps, forward_rows = [], []
    latest = None
    for step_index in range(STEPS):
        floats_in, inv_in = normalize(draft_state)
        draft_norm = spread((floats_in * inv_in * norm_gain).astype(jnp.bfloat16), latest)
        if step_index == 0:
            draft_norm, fetches[2] = lax.optimization_barrier((draft_norm, fetches[2]))
            down_weight = assemble([draft_down], fetches[2:], 0)
        pres = jnp.split(
            jnp.dot(draft_norm, gate_up_weight, preferred_element_type=jnp.float32), 4, axis=1
        )
        acts = jnp.concatenate(
            [jax.nn.silu(pres[0]) * pres[1], jax.nn.silu(pres[2]) * pres[3]], axis=1
        ).astype(jnp.bfloat16)
        packed = packs(draft_norm, [acts])
        acts, *packed = lax.optimization_barrier((acts, *packed))
        partial = jnp.dot(acts, down_weight, preferred_element_type=jnp.float32)
        latest = Exchange(packed)
        forward_rows.append(latest)
        summed = collect(partial, latest)
        new_state = (floats_in + summed).astype(jnp.bfloat16)
        saved_steps.append((draft_state, pres, new_state))
        draft_state = new_state
    carried = jnp.zeros((tok_rows, model_width), jnp.float32)
    backward_rows = []
    for step_index in reversed(range(STEPS)):
        state_in, pres, state_out = saved_steps[step_index]
        ahead = step_index + 1
        target_rows = high_pad[ahead : ahead + tok_rows]
        same_doc = lax.dynamic_slice_in_dim(seg_pad, row_start + ahead, tok_rows, 0) == own_segments
        grad_state = carried + loss_scale * jnp.where(
            same_doc[:, None], state_out.astype(jnp.float32) - target_rows.astype(jnp.float32), 0.0
        )
        own_rows = grad_state.astype(jnp.bfloat16)
        grad_full = spread(own_rows, latest)
        if step_index == 0:
            own_half, far_half = halves(own_rows)
            others = [swap(own_half, 1), swap(far_half, 2), swap(far_half, 3)]
            grad_full, *others = lax.optimization_barrier((grad_full, *others))
            other_grads = spread(jnp.concatenate(others, axis=0), None)
        grad_act = jnp.split(contract_cols(grad_full, down_weight), 2, axis=1)
        gate_up_grads = []
        for block, block_grad in enumerate(grad_act):
            silu_value, silu_slope = silu_terms(pres[2 * block])
            gate_up_grads.append(block_grad * pres[2 * block + 1] * silu_slope)
            gate_up_grads.append(block_grad * silu_value)
        gate_up_grads = jnp.concatenate(gate_up_grads, axis=1).astype(jnp.bfloat16)
        if step_index == 0:
            own_block, far_block = jnp.split(gate_up_grads, 2, axis=1)
            gate_up_shares = [own_block, swap(far_block, 1), swap(own_block, 2), swap(far_block, 3)]
            break
        packed = packs(grad_full, [gate_up_grads])
        gate_up_grads, *packed = lax.optimization_barrier((gate_up_grads, *packed))
        partial = contract_cols(gate_up_grads, gate_up_weight)
        latest = Exchange(packed)
        backward_rows.append(latest)
        grad_norm = collect(partial, latest)
        floats_in, inv_in = normalize(state_in)
        weighted = grad_norm * norm_gain
        grad_in = inv_in * weighted - floats_in * inv_in * inv_in * inv_in * jnp.mean(
            floats_in * weighted, axis=-1, keepdims=True
        )
        carried = grad_state + grad_in
    gate_up, down = 0.0, 0.0
    for forward, backward in zip(reversed(forward_rows), backward_rows):
        wide, act_rows = jnp.split(forward.gathered(), [half_width], axis=1)
        grads, gate_up_rows = jnp.split(backward.gathered(), [half_width], axis=1)
        gate_up = gate_up + contract_rows(wide, gate_up_rows)
        down = down + contract_rows(act_rows, grads)
    wide = jnp.concatenate([rows[:, :half_width] for rows in forward_rows[0].rows], axis=0)
    gate_up = gate_up + contract_rows(wide, jnp.concatenate(gate_up_shares, axis=0))
    own_acts, *other_acts = [rows[:, half_width:] for rows in forward_rows[0].rows]
    other_acts = jnp.stack([acts.reshape(-1, tok_rows, units) for acts in other_acts], axis=1)
    down = down + contract_rows(own_acts, halves(grad_full)[0])
    down = down + contract_rows(other_acts.reshape(-1, units), other_grads)
    core = lax.axis_index("core")
    quarter = gate_up.shape[0] // 2

    def add_cores(partial, axis):
        mine = lax.dynamic_slice_in_dim(partial, core * quarter, quarter, axis)
        sent = lax.dynamic_slice_in_dim(partial, (1 - core) * quarter, quarter, axis)
        return mine, lax.ppermute(sent.astype(jnp.bfloat16), "core", SWAP)

    mine, received = add_cores(gate_up, 0)
    grad_gate = mine[:, :units] + received[:, :units].astype(jnp.float32)
    grad_up = mine[:, units:] + received[:, units:].astype(jnp.float32)
    mine, received = add_cores(down, 1)
    grad_down = mine + received.astype(jnp.float32)
    return (draft_state, grad_gate, grad_up, grad_down)


def solution(mesh):
    fine = Mesh(mesh.devices.reshape(2, 2, 2, 4, 4), ALL)
    dp = ("y_lo", "core")
    return jax.shard_map(
        on_device,
        mesh=fine,
        in_specs=(
            P(ALL, None),
            P(),
            P(None, ALL),
            P(None, ALL),
            P(ALL, None),
            P(ALL, None),
            P(dp, None),
            P(),
            P(None, ROW),
            P(None, ROW),
            P(ROW, None),
        ),
        out_specs=(
            P(ALL, None),
            P(dp, ROW),
            P(dp, ROW),
            P(ROW, dp),
        ),
        check_vma=False,
    )
```

```python
import functools
import math

import jax
import jax.numpy as jnp
from jax import lax
from jax.experimental import pallas as pl
from jax.experimental.pallas import tpu as pltpu
from jax.sharding import Mesh, PartitionSpec as P

STEPS = 3
PARTS = 4
EPSILON = 1e-06

ALL = ("y_lo", "core", "y_hi", "z", "x")
ROW = ("y_hi", "z", "x")
PLANE = ("z", "x")
SWAP = [(0, 1), (1, 0)]


def normalize(incoming):
    as_float = incoming.astype(jnp.float32)
    inv_rms = lax.rsqrt(jnp.mean(as_float * as_float, axis=-1, keepdims=True) + EPSILON)
    return (as_float, inv_rms)


def silu_terms(gate_pre):
    sigmoid_v = jax.nn.sigmoid(gate_pre)
    return (gate_pre * sigmoid_v, sigmoid_v * (1.0 + gate_pre * (1.0 - sigmoid_v)))


def contract_rows(left_side, right_side):
    return lax.dot_general(
        left_side, right_side, (((0,), (0,)), ((), ())), preferred_element_type=jnp.float32
    )


def contract_cols(left_side, right_side):
    return lax.dot_general(
        left_side, right_side, (((1,), (1,)), ((), ())), preferred_element_type=jnp.float32
    )


def expert_kernel(x_ref, gate_hbm, up_hbm, down_hbm, out_ref, gate, up, down, wide, rows, sems):
    copies = [
        pltpu.make_async_copy(source, target, sems.at[i])
        for i, (source, target) in enumerate(((gate_hbm, gate), (up_hbm, up), (down_hbm, down)))
    ]
    for copy in copies:
        copy.start()
    sources, pieces, run = x_ref.shape
    capacity = rows.shape[0] // sources
    parts = pieces // capacity
    lanes = wide.shape[-1]
    for lane in range(run // lanes):
        columns = pl.ds(lane * lanes, lanes)
        wide[lane] = x_ref[:, :, columns].reshape(sources * pieces, lanes).astype(jnp.float32)
        for piece in range(pieces):
            slot, part = divmod(piece, parts)
            rows[
                pl.ds(slot * sources, sources), pl.ds(part * run + lane * lanes, lanes)
            ] = wide[lane, pl.ds(piece, sources, stride=pieces), :].astype(jnp.bfloat16)
    copies[0].wait()
    gate_pre = jnp.dot(rows[...], gate[...], preferred_element_type=jnp.float32)
    copies[1].wait()
    up_pre = jnp.dot(rows[...], up[...], preferred_element_type=jnp.float32)
    act = (gate_pre * jax.nn.sigmoid(gate_pre) * up_pre).astype(jnp.bfloat16)
    copies[2].wait()
    for part in range(parts):
        result = jnp.dot(
            act, down[:, pl.ds(part * run, run)], preferred_element_type=jnp.float32
        )
        for slot in range(capacity):
            for lane in range(run // lanes):
                wide[lane, pl.ds(slot * parts + part, sources, stride=pieces), :] = result[
                    slot * sources : (slot + 1) * sources, lane * lanes : (lane + 1) * lanes
                ]
    for lane in range(run // lanes):
        out_ref[:, :, pl.ds(lane * lanes, lanes)] = (
            wide[lane].astype(jnp.bfloat16).reshape(sources, pieces, lanes)
        )


def expert_half(arrived, w_gate, w_up, w_down, capacity):
    sources, pieces, run = arrived.shape
    width = w_gate.shape[0]
    whole = pl.BlockSpec(memory_space=pltpu.VMEM)
    far = pl.BlockSpec(memory_space=pl.ANY)
    return pl.pallas_call(
        expert_kernel,
        out_shape=jax.ShapeDtypeStruct(arrived.shape, jnp.bfloat16),
        in_specs=[whole, far, far, far],
        out_specs=whole,
        scratch_shapes=[
            pltpu.VMEM(w_gate.shape, jnp.bfloat16),
            pltpu.VMEM(w_up.shape, jnp.bfloat16),
            pltpu.VMEM(w_down.shape, jnp.bfloat16),
            pltpu.VMEM((run // 128, sources * pieces, 128), jnp.float32),
            pltpu.VMEM((sources * capacity, width), jnp.bfloat16),
            pltpu.SemaphoreType.DMA((3,)),
        ],
        compiler_params=pltpu.CompilerParams(vmem_limit_bytes=56 * 1024 * 1024),
        cost_estimate=pl.CostEstimate(
            flops=6 * sources * capacity * width * w_gate.shape[1],
            bytes_accessed=3 * w_gate.size * 2,
            transcendentals=0,
        ),
    )(arrived, w_gate, w_up, w_down)


def spread(incoming, beside):
    members = lax.axis_size("z") * lax.axis_size("x")
    copies = jnp.broadcast_to(incoming[None], (members,) + incoming.shape)
    gathered = lax.all_to_all(copies, PLANE, split_axis=0, concat_axis=0, tiled=True)
    gathered = gathered.reshape((-1, incoming.shape[-1]))
    return gathered if beside is None else beside.beside_gather(gathered)


def collect(incoming, beside):
    members = lax.axis_size("z") * lax.axis_size("x")
    parts = incoming.astype(jnp.bfloat16).reshape((members, -1, incoming.shape[-1]))
    received = lax.all_to_all(parts, PLANE, split_axis=0, concat_axis=0, tiled=True)
    return jnp.sum(beside.beside_sum(received).astype(jnp.float32), axis=0)


def halves(incoming):
    width = incoming.shape[1] // 2
    y_lo = lax.axis_index("y_lo")
    own = lax.dynamic_slice_in_dim(incoming, y_lo * width, width, 1)
    far = lax.dynamic_slice_in_dim(incoming, (1 - y_lo) * width, width, 1)
    return own, far


def swap(rows, mask):
    return lax.ppermute(rows, ("y_lo", "y_hi"), [(i, i ^ mask) for i in range(4)])


def pack_kernel(y_lo_ref, wide_ref, *refs):
    blocks, outs = refs[:-4], refs[-4:]
    half = wide_ref.shape[1] // 2
    for mask, out in enumerate(outs):
        start = pl.multiple_of((y_lo_ref[0] ^ (mask // 2)) * half, half)
        out[:, :half] = wide_ref[:, pl.ds(start, half)]
        width = half
        for block in blocks:
            size = block.shape[1] // 2
            first = mask % 2 * size
            out[:, width : width + size] = block[:, first : first + size]
            width += size


def packs(wide, blocks):
    rows = wide.shape[0]
    width = (wide.shape[1] + sum(block.shape[1] for block in blocks)) // 2
    whole = pl.BlockSpec(memory_space=pltpu.VMEM)
    out = jax.ShapeDtypeStruct((rows, width), jnp.bfloat16)
    return pl.pallas_call(
        pack_kernel,
        out_shape=[out] * 4,
        in_specs=[pl.BlockSpec(memory_space=pltpu.SMEM)] + [whole] * (1 + len(blocks)),
        out_specs=[whole] * 4,
        compiler_params=pltpu.CompilerParams(vmem_limit_bytes=8 * 1024 * 1024),
        cost_estimate=pl.CostEstimate(
            flops=0, bytes_accessed=12 * rows * width, transcendentals=0
        ),
    )(lax.axis_index("y_lo").astype(jnp.int32).reshape(1), wide, *blocks)


class Exchange:
    def __init__(self, packed):
        own, far_y_hi, *self.later = packed
        self.rows = [own, swap(far_y_hi, 1)]

    def beside_sum(self, received):
        received, self.rows[1], *self.later = lax.optimization_barrier(
            (received, self.rows[1], *self.later)
        )
        self.rows += [swap(self.later[0], 2), swap(self.later[1], 3)]
        return received

    def beside_gather(self, gathered):
        gathered, *self.rows[2:] = lax.optimization_barrier((gathered, *self.rows[2:]))
        return gathered

    def gathered(self):
        return jnp.concatenate(self.rows, axis=0)


def fetch_half(weight):
    half = weight.shape[0] // 2
    core = lax.axis_index("core")
    mine = lax.dynamic_slice_in_dim(weight, core * half, half, 0)
    return lax.ppermute(mine, ("y_lo", "y_hi"), [(0, 3), (3, 0), (1, 2), (2, 1)])


def assemble_kernel(axis, core_ref, *refs):
    out, sems = refs[-2:]
    count = (len(refs) - 2) // 3
    size = refs[0].shape[axis]
    half = refs[count].shape[0]
    core = core_ref[0]
    places = []

    def place(source, block, start):
        rows = source.shape[0]
        if axis == 1:
            target = out.at[pl.ds(start, rows), pl.ds(block * size, size)]
        else:
            target = out.at[pl.ds(block * size + start, rows), :]
        places.append((source, target))

    for i in range(count):
        place(refs[i], i, 0)
        place(refs[count + i], count + i, pl.multiple_of(core * half, half))
        place(refs[2 * count + i], count + i, pl.multiple_of((1 - core) * half, half))
    copies = [
        pltpu.make_async_copy(source, target, sems.at[k])
        for k, (source, target) in enumerate(places)
    ]
    for copy in copies:
        copy.start()
    for copy in copies:
        copy.wait()


def assemble(owns, fetched, axis):
    swapped = [lax.ppermute(half, "core", SWAP) for half in fetched]
    shape = list(owns[0].shape)
    shape[axis] *= 2 * len(owns)
    far = pl.BlockSpec(memory_space=pl.ANY)
    parts = [*owns, *fetched, *swapped]
    return pl.pallas_call(
        functools.partial(assemble_kernel, axis),
        out_shape=jax.ShapeDtypeStruct(tuple(shape), jnp.bfloat16),
        in_specs=[pl.BlockSpec(memory_space=pltpu.SMEM)] + [far] * len(parts),
        out_specs=pl.BlockSpec(memory_space=pltpu.VMEM),
        scratch_shapes=[pltpu.SemaphoreType.DMA((len(parts),))],
        compiler_params=pltpu.CompilerParams(vmem_limit_bytes=20 * 1024 * 1024),
        cost_estimate=pl.CostEstimate(
            flops=0, bytes_accessed=4 * math.prod(shape), transcendentals=0
        ),
    )(lax.axis_index("core").astype(jnp.int32).reshape(1), *parts)


def on_device(
    hidden_in,
    router_weight,
    expert_gate,
    expert_up,
    expert_down,
    expert_ids,
    segment_ids,
    draft_gain,
    draft_gate,
    draft_up,
    draft_down,
):
    tok_rows = hidden_in.shape[0]
    model_width = hidden_in.shape[1]
    top_count = expert_ids.shape[1]
    experts = router_weight.shape[1]
    capacity = 2 * ((tok_rows * top_count + experts - 1) // experts)
    token_count = tok_rows * lax.axis_size(ALL)
    fetches = [fetch_half(weight) for weight in (draft_gate, draft_up, draft_down)]
    as_float, inv_rms = normalize(hidden_in)
    normed = (as_float * inv_rms).astype(jnp.bfloat16)
    logits = jnp.dot(normed, router_weight, preferred_element_type=jnp.float32)
    chosen = jnp.take_along_axis(logits, expert_ids, axis=1)
    weights = jnp.exp(chosen)
    route_probs = weights / jnp.sum(weights, axis=1, keepdims=True)
    flat_ids = expert_ids.reshape(-1)
    choice_range = jnp.arange(flat_ids.shape[0], dtype=jnp.int32)
    earlier = (flat_ids[:, None] == flat_ids[None, :]) & (
        choice_range[None, :] < choice_range[:, None]
    )
    slots = flat_ids * capacity + jnp.sum(earlier.astype(jnp.int32), axis=1)
    lines = experts * 2 * capacity * PARTS
    line = jnp.arange(lines, dtype=jnp.int32)
    line_slot = line // (2 * capacity * PARTS) * capacity + line // PARTS % capacity
    piece_slots = jnp.repeat(slots.reshape(tok_rows, top_count), PARTS, axis=0)
    piece_probs = jnp.repeat(route_probs, PARTS, axis=0)
    piece_part = jnp.arange(tok_rows * PARTS, dtype=jnp.int32) % PARTS
    same_part = piece_part[:, None] == (line % PARTS)[None, :]
    hits = [same_part & (piece_slots[:, k : k + 1] == line_slot[None, :]) for k in range(top_count)]
    picker = sum(hit.astype(jnp.float32) for hit in hits).astype(jnp.bfloat16)
    mixer = sum(jnp.where(hit, piece_probs[:, k : k + 1], 0.0) for k, hit in enumerate(hits))
    pieces = normed.reshape(tok_rows * PARTS, model_width // PARTS)
    doubled = contract_rows(picker, pieces).astype(jnp.bfloat16)
    doubled = doubled.reshape(2 * experts, capacity * PARTS, model_width // PARTS)
    arrived = lax.all_to_all(doubled, ALL, split_axis=0, concat_axis=0, tiled=True)
    arrived, fetches[0] = lax.optimization_barrier((arrived, fetches[0]))
    half_parts = expert_half(arrived, expert_gate, expert_up, expert_down, capacity)
    half_parts, fetches[1] = lax.optimization_barrier((half_parts, fetches[1]))
    returned = lax.all_to_all(half_parts, ALL, split_axis=0, concat_axis=0, tiled=True)
    gate_up_weight = assemble([draft_gate, draft_up], fetches[:2], 1)
    returned, gate_up_weight = lax.optimization_barrier((returned, gate_up_weight))
    returned = returned.reshape(lines, model_width // PARTS)
    first = mixer.astype(jnp.bfloat16)
    rest = mixer - first.astype(jnp.float32)
    second = rest.astype(jnp.bfloat16)
    third = (rest - second.astype(jnp.float32)).astype(jnp.bfloat16)
    mixed = jnp.dot(
        jnp.concatenate([first, second, third], axis=0),
        returned,
        preferred_element_type=jnp.float32,
    )
    moe_out = jnp.sum(mixed.reshape(3, tok_rows * PARTS, -1), axis=0).reshape(tok_rows, model_width)
    top_state = (as_float + moe_out).astype(jnp.bfloat16)
    units = draft_gate.shape[1]
    half_width = model_width // 2
    norm_gain = draft_gain.astype(jnp.float32)
    segments = segment_ids[0]
    row_size = lax.axis_size(ROW)
    row_start = lax.axis_index(ROW) * tok_rows
    seg_pad = jnp.concatenate([segments, jnp.full((STEPS,), -1, jnp.int32)], axis=0)
    own_segments = lax.dynamic_slice_in_dim(segments, row_start, tok_rows, 0)
    loss_scale = 1.0 / math.sqrt(token_count)
    following = lax.ppermute(
        top_state, ROW, [(i, (i + row_size - 1) % row_size) for i in range(row_size)]
    )
    high_pad = jnp.concatenate([top_state, following], axis=0)
    draft_state = top_state
    saved_steps, forward_rows = [], []
    latest = None
    for step_index in range(STEPS):
        floats_in, inv_in = normalize(draft_state)
        draft_norm = spread((floats_in * inv_in * norm_gain).astype(jnp.bfloat16), latest)
        if step_index == 0:
            draft_norm, fetches[2] = lax.optimization_barrier((draft_norm, fetches[2]))
            down_weight = assemble([draft_down], fetches[2:], 0)
        pres = jnp.split(
            jnp.dot(draft_norm, gate_up_weight, preferred_element_type=jnp.float32), 4, axis=1
        )
        acts = jnp.concatenate(
            [jax.nn.silu(pres[0]) * pres[1], jax.nn.silu(pres[2]) * pres[3]], axis=1
        ).astype(jnp.bfloat16)
        packed = packs(draft_norm, [acts])
        acts, *packed = lax.optimization_barrier((acts, *packed))
        partial = jnp.dot(acts, down_weight, preferred_element_type=jnp.float32)
        latest = Exchange(packed)
        forward_rows.append(latest)
        summed = collect(partial, latest)
        new_state = (floats_in + summed).astype(jnp.bfloat16)
        saved_steps.append((draft_state, pres, new_state))
        draft_state = new_state
    carried = jnp.zeros((tok_rows, model_width), jnp.float32)
    backward_rows = []
    for step_index in reversed(range(STEPS)):
        state_in, pres, state_out = saved_steps[step_index]
        ahead = step_index + 1
        target_rows = high_pad[ahead : ahead + tok_rows]
        same_doc = lax.dynamic_slice_in_dim(seg_pad, row_start + ahead, tok_rows, 0) == own_segments
        grad_state = carried + loss_scale * jnp.where(
            same_doc[:, None], state_out.astype(jnp.float32) - target_rows.astype(jnp.float32), 0.0
        )
        own_rows = grad_state.astype(jnp.bfloat16)
        grad_full = spread(own_rows, latest)
        if step_index == 0:
            own_half, far_half = halves(own_rows)
            others = [swap(own_half, 1), swap(far_half, 2), swap(far_half, 3)]
            grad_full, *others = lax.optimization_barrier((grad_full, *others))
            other_grads = spread(jnp.concatenate(others, axis=0), None)
        grad_act = jnp.split(contract_cols(grad_full, down_weight), 2, axis=1)
        gate_up_grads = []
        for block, block_grad in enumerate(grad_act):
            silu_value, silu_slope = silu_terms(pres[2 * block])
            gate_up_grads.append(block_grad * pres[2 * block + 1] * silu_slope)
            gate_up_grads.append(block_grad * silu_value)
        gate_up_grads = jnp.concatenate(gate_up_grads, axis=1).astype(jnp.bfloat16)
        if step_index == 0:
            own_block, far_block = jnp.split(gate_up_grads, 2, axis=1)
            gate_up_shares = [own_block, swap(far_block, 1), swap(own_block, 2), swap(far_block, 3)]
            break
        packed = packs(grad_full, [gate_up_grads])
        gate_up_grads, *packed = lax.optimization_barrier((gate_up_grads, *packed))
        partial = contract_cols(gate_up_grads, gate_up_weight)
        latest = Exchange(packed)
        backward_rows.append(latest)
        grad_norm = collect(partial, latest)
        floats_in, inv_in = normalize(state_in)
        weighted = grad_norm * norm_gain
        grad_in = inv_in * weighted - floats_in * inv_in * inv_in * inv_in * jnp.mean(
            floats_in * weighted, axis=-1, keepdims=True
        )
        carried = grad_state + grad_in
    gate_up, down = 0.0, 0.0
    for forward, backward in zip(reversed(forward_rows), backward_rows):
        wide, act_rows = jnp.split(forward.gathered(), [half_width], axis=1)
        grads, gate_up_rows = jnp.split(backward.gathered(), [half_width], axis=1)
        gate_up = gate_up + contract_rows(wide, gate_up_rows)
        down = down + contract_rows(act_rows, grads)
    wide = jnp.concatenate([rows[:, :half_width] for rows in forward_rows[0].rows], axis=0)
    gate_up = gate_up + contract_rows(wide, jnp.concatenate(gate_up_shares, axis=0))
    own_acts, *other_acts = [rows[:, half_width:] for rows in forward_rows[0].rows]
    other_acts = jnp.stack([acts.reshape(-1, tok_rows, units) for acts in other_acts], axis=1)
    down = down + contract_rows(own_acts, halves(grad_full)[0])
    down = down + contract_rows(other_acts.reshape(-1, units), other_grads)
    core = lax.axis_index("core")
    quarter = gate_up.shape[0] // 2

    def add_cores(partial, axis):
        mine = lax.dynamic_slice_in_dim(partial, core * quarter, quarter, axis)
        sent = lax.dynamic_slice_in_dim(partial, (1 - core) * quarter, quarter, axis)
        return mine, lax.ppermute(sent.astype(jnp.bfloat16), "core", SWAP)

    mine, received = add_cores(gate_up, 0)
    grad_gate = mine[:, :units] + received[:, :units].astype(jnp.float32)
    grad_up = mine[:, units:] + received[:, units:].astype(jnp.float32)
    mine, received = add_cores(down, 1)
    grad_down = mine + received.astype(jnp.float32)
    return (draft_state, grad_gate, grad_up, grad_down)


def solution(mesh):
    fine = Mesh(mesh.devices.reshape(2, 2, 2, 4, 4), ALL)
    dp = ("y_lo", "core")
    return jax.shard_map(
        on_device,
        mesh=fine,
        in_specs=(
            P(ALL, None),
            P(),
            P(None, ALL),
            P(None, ALL),
            P(ALL, None),
            P(ALL, None),
            P(dp, None),
            P(),
            P(None, ROW),
            P(None, ROW),
            P(ROW, None),
        ),
        out_specs=(
            P(ALL, None),
            P(dp, ROW),
            P(dp, ROW),
            P(ROW, dp),
        ),
        check_vma=False,
    )
```

```python
import functools
import math

import jax
import jax.numpy as jnp
from jax import lax
from jax.experimental import pallas as pl
from jax.experimental.pallas import tpu as pltpu
from jax.sharding import Mesh, PartitionSpec as P

STEPS = 3
PARTS = 4
EPSILON = 1e-06

ALL = ("y_lo", "core", "y_hi", "z", "x")
ROW = ("y_hi", "z", "x")
PLANE = ("z", "x")
SWAP = [(0, 1), (1, 0)]


def normalize(incoming):
    as_float = incoming.astype(jnp.float32)
    inv_rms = lax.rsqrt(jnp.mean(as_float * as_float, axis=-1, keepdims=True) + EPSILON)
    return (as_float, inv_rms)


def silu_terms(gate_pre):
    sigmoid_v = jax.nn.sigmoid(gate_pre)
    return (gate_pre * sigmoid_v, sigmoid_v * (1.0 + gate_pre * (1.0 - sigmoid_v)))


def contract_rows(left_side, right_side):
    return lax.dot_general(
        left_side, right_side, (((0,), (0,)), ((), ())), preferred_element_type=jnp.float32
    )


def contract_cols(left_side, right_side):
    return lax.dot_general(
        left_side, right_side, (((1,), (1,)), ((), ())), preferred_element_type=jnp.float32
    )


def expert_kernel(x_ref, gate_hbm, up_hbm, down_hbm, out_ref, gate, up, down, wide, rows, sems):
    copies = [
        pltpu.make_async_copy(source, target, sems.at[i])
        for i, (source, target) in enumerate(((gate_hbm, gate), (up_hbm, up), (down_hbm, down)))
    ]
    for copy in copies:
        copy.start()
    sources, pieces, run = x_ref.shape
    capacity = rows.shape[0] // sources
    parts = pieces // capacity
    lanes = wide.shape[-1]
    for lane in range(run // lanes):
        columns = pl.ds(lane * lanes, lanes)
        wide[lane] = x_ref[:, :, columns].reshape(sources * pieces, lanes).astype(jnp.float32)
        for piece in range(pieces):
            slot, part = divmod(piece, parts)
            rows[
                pl.ds(slot * sources, sources), pl.ds(part * run + lane * lanes, lanes)
            ] = wide[lane, pl.ds(piece, sources, stride=pieces), :].astype(jnp.bfloat16)
    copies[0].wait()
    gate_pre = jnp.dot(rows[...], gate[...], preferred_element_type=jnp.float32)
    copies[1].wait()
    up_pre = jnp.dot(rows[...], up[...], preferred_element_type=jnp.float32)
    act = (gate_pre * jax.nn.sigmoid(gate_pre) * up_pre).astype(jnp.bfloat16)
    copies[2].wait()
    for part in range(parts):
        result = jnp.dot(
            act, down[:, pl.ds(part * run, run)], preferred_element_type=jnp.float32
        )
        for slot in range(capacity):
            for lane in range(run // lanes):
                wide[lane, pl.ds(slot * parts + part, sources, stride=pieces), :] = result[
                    slot * sources : (slot + 1) * sources, lane * lanes : (lane + 1) * lanes
                ]
    for lane in range(run // lanes):
        out_ref[:, :, pl.ds(lane * lanes, lanes)] = (
            wide[lane].astype(jnp.bfloat16).reshape(sources, pieces, lanes)
        )


def expert_half(arrived, w_gate, w_up, w_down, capacity):
    sources, pieces, run = arrived.shape
    width = w_gate.shape[0]
    whole = pl.BlockSpec(memory_space=pltpu.VMEM)
    far = pl.BlockSpec(memory_space=pl.ANY)
    return pl.pallas_call(
        expert_kernel,
        out_shape=jax.ShapeDtypeStruct(arrived.shape, jnp.bfloat16),
        in_specs=[whole, far, far, far],
        out_specs=whole,
        scratch_shapes=[
            pltpu.VMEM(w_gate.shape, jnp.bfloat16),
            pltpu.VMEM(w_up.shape, jnp.bfloat16),
            pltpu.VMEM(w_down.shape, jnp.bfloat16),
            pltpu.VMEM((run // 128, sources * pieces, 128), jnp.float32),
            pltpu.VMEM((sources * capacity, width), jnp.bfloat16),
            pltpu.SemaphoreType.DMA((3,)),
        ],
        compiler_params=pltpu.CompilerParams(vmem_limit_bytes=56 * 1024 * 1024),
        cost_estimate=pl.CostEstimate(
            flops=6 * sources * capacity * width * w_gate.shape[1],
            bytes_accessed=3 * w_gate.size * 2,
            transcendentals=0,
        ),
    )(arrived, w_gate, w_up, w_down)


def spread(incoming, beside):
    members = lax.axis_size("z") * lax.axis_size("x")
    copies = jnp.broadcast_to(incoming[None], (members,) + incoming.shape)
    gathered = lax.all_to_all(copies, PLANE, split_axis=0, concat_axis=0, tiled=True)
    gathered = gathered.reshape((-1, incoming.shape[-1]))
    return gathered if beside is None else beside.beside_gather(gathered)


def collect(incoming, beside):
    members = lax.axis_size("z") * lax.axis_size("x")
    parts = incoming.astype(jnp.bfloat16).reshape((members, -1, incoming.shape[-1]))
    received = lax.all_to_all(parts, PLANE, split_axis=0, concat_axis=0, tiled=True)
    return jnp.sum(beside.beside_sum(received).astype(jnp.float32), axis=0)


def halves(incoming):
    width = incoming.shape[1] // 2
    y_lo = lax.axis_index("y_lo")
    own = lax.dynamic_slice_in_dim(incoming, y_lo * width, width, 1)
    far = lax.dynamic_slice_in_dim(incoming, (1 - y_lo) * width, width, 1)
    return own, far


def swap(rows, mask):
    return lax.ppermute(rows, ("y_lo", "y_hi"), [(i, i ^ mask) for i in range(4)])


def pack_kernel(y_lo_ref, wide_ref, own_ref, far_ref, *outs):
    half = wide_ref.shape[1] // 2
    for mask, out in enumerate(outs):
        start = pl.multiple_of((y_lo_ref[0] ^ (mask // 2)) * half, half)
        out[:, :half] = wide_ref[:, pl.ds(start, half)]
        out[:, half:] = (far_ref if mask % 2 else own_ref)[...]


def packs(wide, own, far):
    rows = wide.shape[0]
    width = wide.shape[1] // 2 + own.shape[1]
    whole = pl.BlockSpec(memory_space=pltpu.VMEM)
    out = jax.ShapeDtypeStruct((rows, width), jnp.bfloat16)
    return pl.pallas_call(
        pack_kernel,
        out_shape=[out] * 4,
        in_specs=[pl.BlockSpec(memory_space=pltpu.SMEM)] + [whole] * 3,
        out_specs=[whole] * 4,
        compiler_params=pltpu.CompilerParams(vmem_limit_bytes=8 * 1024 * 1024),
        cost_estimate=pl.CostEstimate(
            flops=0, bytes_accessed=12 * rows * width, transcendentals=0
        ),
    )(lax.axis_index("y_lo").astype(jnp.int32).reshape(1), wide, own, far)


class Exchange:
    def __init__(self, packed):
        own, far_y_hi, *self.later = packed
        self.rows = [own, swap(far_y_hi, 1)]

    def beside_sum(self, received):
        received, self.rows[1], *self.later = lax.optimization_barrier(
            (received, self.rows[1], *self.later)
        )
        self.rows += [swap(self.later[0], 2), swap(self.later[1], 3)]
        return received

    def beside_gather(self, gathered):
        gathered, *self.rows[2:] = lax.optimization_barrier((gathered, *self.rows[2:]))
        return gathered

    def gathered(self):
        return jnp.concatenate(self.rows, axis=0)


def fetch_half(weight):
    half = weight.shape[0] // 2
    core = lax.axis_index("core")
    mine = lax.dynamic_slice_in_dim(weight, core * half, half, 0)
    return lax.ppermute(mine, ("y_lo", "y_hi"), [(0, 3), (3, 0), (1, 2), (2, 1)])


def assemble_kernel(core_ref, *refs):
    *refs, own_out, far_out, sems = refs
    count = len(refs) // 3
    half = refs[count].shape[0]
    core = core_ref[0]
    copies = []

    def place(source, out, start, block):
        rows, size = source.shape
        target = out.at[pl.ds(start, rows), pl.ds(block * size, size)]
        copies.append(pltpu.make_async_copy(source, target, sems.at[len(copies)]))

    for i in range(count):
        place(refs[i], own_out, 0, i)
        place(refs[count + i], far_out, pl.multiple_of(core * half, half), i)
        place(refs[2 * count + i], far_out, pl.multiple_of((1 - core) * half, half), i)
    for copy in copies:
        copy.start()
    for copy in copies:
        copy.wait()


def assemble(owns, fetched):
    swapped = [lax.ppermute(half, "core", SWAP) for half in fetched]
    rows, size = owns[0].shape
    out = jax.ShapeDtypeStruct((rows, size * len(owns)), jnp.bfloat16)
    far = pl.BlockSpec(memory_space=pl.ANY)
    parts = [*owns, *fetched, *swapped]
    return pl.pallas_call(
        assemble_kernel,
        out_shape=[out] * 2,
        in_specs=[pl.BlockSpec(memory_space=pltpu.SMEM)] + [far] * len(parts),
        out_specs=[pl.BlockSpec(memory_space=pltpu.VMEM)] * 2,
        scratch_shapes=[pltpu.SemaphoreType.DMA((len(parts),))],
        compiler_params=pltpu.CompilerParams(vmem_limit_bytes=20 * 1024 * 1024),
        cost_estimate=pl.CostEstimate(
            flops=0, bytes_accessed=8 * rows * size * len(owns), transcendentals=0
        ),
    )(lax.axis_index("core").astype(jnp.int32).reshape(1), *parts)


def on_device(
    hidden_in,
    router_weight,
    expert_gate,
    expert_up,
    expert_down,
    expert_ids,
    segment_ids,
    draft_gain,
    draft_gate,
    draft_up,
    draft_down,
):
    tok_rows = hidden_in.shape[0]
    model_width = hidden_in.shape[1]
    top_count = expert_ids.shape[1]
    experts = router_weight.shape[1]
    capacity = 2 * ((tok_rows * top_count + experts - 1) // experts)
    token_count = tok_rows * lax.axis_size(ALL)
    fetches = [fetch_half(weight) for weight in (draft_gate, draft_up, draft_down)]
    as_float, inv_rms = normalize(hidden_in)
    normed = (as_float * inv_rms).astype(jnp.bfloat16)
    logits = jnp.dot(normed, router_weight, preferred_element_type=jnp.float32)
    chosen = jnp.take_along_axis(logits, expert_ids, axis=1)
    weights = jnp.exp(chosen)
    route_probs = weights / jnp.sum(weights, axis=1, keepdims=True)
    flat_ids = expert_ids.reshape(-1)
    choice_range = jnp.arange(flat_ids.shape[0], dtype=jnp.int32)
    earlier = (flat_ids[:, None] == flat_ids[None, :]) & (
        choice_range[None, :] < choice_range[:, None]
    )
    slots = flat_ids * capacity + jnp.sum(earlier.astype(jnp.int32), axis=1)
    lines = experts * 2 * capacity * PARTS
    line = jnp.arange(lines, dtype=jnp.int32)
    line_slot = line // (2 * capacity * PARTS) * capacity + line // PARTS % capacity
    piece_slots = jnp.repeat(slots.reshape(tok_rows, top_count), PARTS, axis=0)
    piece_probs = jnp.repeat(route_probs, PARTS, axis=0)
    piece_part = jnp.arange(tok_rows * PARTS, dtype=jnp.int32) % PARTS
    same_part = piece_part[:, None] == (line % PARTS)[None, :]
    hits = [same_part & (piece_slots[:, k : k + 1] == line_slot[None, :]) for k in range(top_count)]
    picker = sum(hit.astype(jnp.float32) for hit in hits).astype(jnp.bfloat16)
    mixer = sum(jnp.where(hit, piece_probs[:, k : k + 1], 0.0) for k, hit in enumerate(hits))
    pieces = normed.reshape(tok_rows * PARTS, model_width // PARTS)
    doubled = contract_rows(picker, pieces).astype(jnp.bfloat16)
    doubled = doubled.reshape(2 * experts, capacity * PARTS, model_width // PARTS)
    arrived = lax.all_to_all(doubled, ALL, split_axis=0, concat_axis=0, tiled=True)
    arrived, fetches[0] = lax.optimization_barrier((arrived, fetches[0]))
    half_parts = expert_half(arrived, expert_gate, expert_up, expert_down, capacity)
    half_parts, fetches[1] = lax.optimization_barrier((half_parts, fetches[1]))
    returned = lax.all_to_all(half_parts, ALL, split_axis=0, concat_axis=0, tiled=True)
    gate_ups = assemble([draft_gate, draft_up], fetches[:2])
    returned, *gate_ups = lax.optimization_barrier((returned, *gate_ups))
    returned = returned.reshape(lines, model_width // PARTS)
    first = mixer.astype(jnp.bfloat16)
    rest = mixer - first.astype(jnp.float32)
    second = rest.astype(jnp.bfloat16)
    third = (rest - second.astype(jnp.float32)).astype(jnp.bfloat16)
    mixed = jnp.dot(
        jnp.concatenate([first, second, third], axis=0),
        returned,
        preferred_element_type=jnp.float32,
    )
    moe_out = jnp.sum(mixed.reshape(3, tok_rows * PARTS, -1), axis=0).reshape(tok_rows, model_width)
    top_state = (as_float + moe_out).astype(jnp.bfloat16)
    units = draft_gate.shape[1]
    half_width = model_width // 2
    norm_gain = draft_gain.astype(jnp.float32)
    segments = segment_ids[0]
    row_size = lax.axis_size(ROW)
    row_start = lax.axis_index(ROW) * tok_rows
    seg_pad = jnp.concatenate([segments, jnp.full((STEPS,), -1, jnp.int32)], axis=0)
    own_segments = lax.dynamic_slice_in_dim(segments, row_start, tok_rows, 0)
    loss_scale = 1.0 / math.sqrt(token_count)
    following = lax.ppermute(
        top_state, ROW, [(i, (i + row_size - 1) % row_size) for i in range(row_size)]
    )
    high_pad = jnp.concatenate([top_state, following], axis=0)
    draft_state = top_state
    saved_steps, forward_rows = [], []
    latest = None
    for step_index in range(STEPS):
        floats_in, inv_in = normalize(draft_state)
        draft_norm = spread((floats_in * inv_in * norm_gain).astype(jnp.bfloat16), latest)
        if step_index == 0:
            draft_norm, fetches[2] = lax.optimization_barrier((draft_norm, fetches[2]))
            downs = assemble([draft_down], fetches[2:])
        pres, acts = [], []
        for gate_up in gate_ups:
            both = jnp.dot(draft_norm, gate_up, preferred_element_type=jnp.float32)
            gate_pre, up_pre = jnp.split(both, 2, axis=1)
            pres.append((gate_pre, up_pre))
            acts.append((jax.nn.silu(gate_pre) * up_pre).astype(jnp.bfloat16))
        packed = packs(draft_norm, *acts)
        own_acts, far_acts, *packed = lax.optimization_barrier((*acts, *packed))
        partial = jnp.dot(own_acts, downs[0], preferred_element_type=jnp.float32) + jnp.dot(
            far_acts, downs[1], preferred_element_type=jnp.float32
        )
        latest = Exchange(packed)
        forward_rows.append(latest)
        summed = collect(partial, latest)
        new_state = (floats_in + summed).astype(jnp.bfloat16)
        saved_steps.append((draft_state, pres, new_state))
        draft_state = new_state
    carried = jnp.zeros((tok_rows, model_width), jnp.float32)
    backward_rows = []
    for step_index in reversed(range(STEPS)):
        state_in, pres, state_out = saved_steps[step_index]
        ahead = step_index + 1
        target_rows = high_pad[ahead : ahead + tok_rows]
        same_doc = lax.dynamic_slice_in_dim(seg_pad, row_start + ahead, tok_rows, 0) == own_segments
        grad_state = carried + loss_scale * jnp.where(
            same_doc[:, None], state_out.astype(jnp.float32) - target_rows.astype(jnp.float32), 0.0
        )
        own_rows = grad_state.astype(jnp.bfloat16)
        grad_full = spread(own_rows, latest)
        if step_index == 0:
            own_half, far_half = halves(own_rows)
            others = [swap(own_half, 1), swap(far_half, 2), swap(far_half, 3)]
            grad_full, *others = lax.optimization_barrier((grad_full, *others))
            other_grads = spread(jnp.concatenate(others, axis=0), None)
        gate_up_grads = []
        for (gate_pre, up_pre), down in zip(pres, downs):
            grad_act = contract_cols(grad_full, down)
            silu_value, silu_slope = silu_terms(gate_pre)
            both = jnp.concatenate([grad_act * up_pre * silu_slope, grad_act * silu_value], axis=1)
            gate_up_grads.append(both.astype(jnp.bfloat16))
        if step_index == 0:
            own_block, far_block = gate_up_grads
            gate_up_shares = [own_block, swap(far_block, 1), swap(own_block, 2), swap(far_block, 3)]
            break
        packed = packs(grad_full, *gate_up_grads)
        own_grads, far_grads, *packed = lax.optimization_barrier((*gate_up_grads, *packed))
        partial = contract_cols(own_grads, gate_ups[0]) + contract_cols(far_grads, gate_ups[1])
        latest = Exchange(packed)
        backward_rows.append(latest)
        grad_norm = collect(partial, latest)
        floats_in, inv_in = normalize(state_in)
        weighted = grad_norm * norm_gain
        grad_in = inv_in * weighted - floats_in * inv_in * inv_in * inv_in * jnp.mean(
            floats_in * weighted, axis=-1, keepdims=True
        )
        carried = grad_state + grad_in
    gate_up, down = 0.0, 0.0
    for forward, backward in zip(reversed(forward_rows), backward_rows):
        wide, act_rows = jnp.split(forward.gathered(), [half_width], axis=1)
        grads, gate_up_rows = jnp.split(backward.gathered(), [half_width], axis=1)
        gate_up = gate_up + contract_rows(wide, gate_up_rows)
        down = down + contract_rows(act_rows, grads)
    wide = jnp.concatenate([rows[:, :half_width] for rows in forward_rows[0].rows], axis=0)
    gate_up = gate_up + contract_rows(wide, jnp.concatenate(gate_up_shares, axis=0))
    core = lax.axis_index("core")
    quarter = half_width // 2

    def add_cores(partial, axis):
        mine = lax.dynamic_slice_in_dim(partial, core * quarter, quarter, axis)
        sent = lax.dynamic_slice_in_dim(partial, (1 - core) * quarter, quarter, axis)
        return mine, lax.ppermute(sent.astype(jnp.bfloat16), "core", SWAP)

    mine, received = add_cores(gate_up, 0)
    grad_gate = mine[:, :units] + received[:, :units].astype(jnp.float32)
    grad_up = mine[:, units:] + received[:, units:].astype(jnp.float32)
    other_grads, grad_gate, grad_up = lax.optimization_barrier((other_grads, grad_gate, grad_up))
    own_acts, *other_acts = [rows[:, half_width:] for rows in forward_rows[0].rows]
    other_acts = jnp.stack([acts.reshape(-1, tok_rows, units) for acts in other_acts], axis=1)
    down = down + contract_rows(own_acts, halves(grad_full)[0])
    down = down + contract_rows(other_acts.reshape(-1, units), other_grads)
    mine, received = add_cores(down, 1)
    grad_down = mine + received.astype(jnp.float32)
    return (draft_state, grad_gate, grad_up, grad_down)


def solution(mesh):
    fine = Mesh(mesh.devices.reshape(2, 2, 2, 4, 4), ALL)
    dp = ("y_lo", "core")
    return jax.shard_map(
        on_device,
        mesh=fine,
        in_specs=(
            P(ALL, None),
            P(),
            P(None, ALL),
            P(None, ALL),
            P(ALL, None),
            P(ALL, None),
            P(dp, None),
            P(),
            P(None, ROW),
            P(None, ROW),
            P(ROW, None),
        ),
        out_specs=(
            P(ALL, None),
            P(dp, ROW),
            P(dp, ROW),
            P(ROW, dp),
        ),
        check_vma=False,
    )
```

```python
import functools
import math

import jax
import jax.numpy as jnp
from jax import lax
from jax.experimental import pallas as pl
from jax.experimental.layout import Layout, with_layout_constraint
from jax.experimental.pallas import tpu as pltpu
from jax.sharding import Mesh, PartitionSpec as P

STEPS = 3
PARTS = 4
EPSILON = 1e-06

ALL = ("y_lo", "core", "y_hi", "z", "x")
ROW = ("y_hi", "z", "x")
PLANE = ("z", "x")
SWAP = [(0, 1), (1, 0)]


def normalize(incoming):
    as_float = incoming.astype(jnp.float32)
    inv_rms = lax.rsqrt(jnp.mean(as_float * as_float, axis=-1, keepdims=True) + EPSILON)
    return (as_float, inv_rms)


def silu_terms(gate_pre):
    sigmoid_v = jax.nn.sigmoid(gate_pre)
    return (gate_pre * sigmoid_v, sigmoid_v * (1.0 + gate_pre * (1.0 - sigmoid_v)))


def contract_rows(left_side, right_side):
    return lax.dot_general(
        left_side, right_side, (((0,), (0,)), ((), ())), preferred_element_type=jnp.float32
    )


def contract_cols(left_side, right_side):
    return lax.dot_general(
        left_side, right_side, (((1,), (1,)), ((), ())), preferred_element_type=jnp.float32
    )


def expert_kernel(x_ref, gate_hbm, up_hbm, down_hbm, out_ref, gate, up, down, wide, rows, sems):
    copies = [
        pltpu.make_async_copy(source, target, sems.at[i])
        for i, (source, target) in enumerate(((gate_hbm, gate), (up_hbm, up), (down_hbm, down)))
    ]
    for copy in copies:
        copy.start()
    sources, pieces, run = x_ref.shape
    capacity = rows.shape[0] // sources
    parts = pieces // capacity
    lanes = wide.shape[-1]
    for lane in range(run // lanes):
        columns = pl.ds(lane * lanes, lanes)
        wide[lane] = x_ref[:, :, columns].reshape(sources * pieces, lanes).astype(jnp.float32)
        for piece in range(pieces):
            slot, part = divmod(piece, parts)
            rows[
                pl.ds(slot * sources, sources), pl.ds(part * run + lane * lanes, lanes)
            ] = wide[lane, pl.ds(piece, sources, stride=pieces), :].astype(jnp.bfloat16)
    copies[0].wait()
    gate_pre = jnp.dot(rows[...], gate[...], preferred_element_type=jnp.float32)
    copies[1].wait()
    up_pre = jnp.dot(rows[...], up[...], preferred_element_type=jnp.float32)
    act = (gate_pre * jax.nn.sigmoid(gate_pre) * up_pre).astype(jnp.bfloat16)
    copies[2].wait()
    for part in range(parts):
        result = jnp.dot(
            act, down[:, pl.ds(part * run, run)], preferred_element_type=jnp.float32
        )
        for slot in range(capacity):
            for lane in range(run // lanes):
                wide[lane, pl.ds(slot * parts + part, sources, stride=pieces), :] = result[
                    slot * sources : (slot + 1) * sources, lane * lanes : (lane + 1) * lanes
                ]
    for lane in range(run // lanes):
        out_ref[:, :, pl.ds(lane * lanes, lanes)] = (
            wide[lane].astype(jnp.bfloat16).reshape(sources, pieces, lanes)
        )


def expert_half(arrived, w_gate, w_up, w_down, capacity):
    sources, pieces, run = arrived.shape
    width = w_gate.shape[0]
    whole = pl.BlockSpec(memory_space=pltpu.VMEM)
    far = pl.BlockSpec(memory_space=pl.ANY)
    return pl.pallas_call(
        expert_kernel,
        out_shape=jax.ShapeDtypeStruct(arrived.shape, jnp.bfloat16),
        in_specs=[whole, far, far, far],
        out_specs=whole,
        scratch_shapes=[
            pltpu.VMEM(w_gate.shape, jnp.bfloat16),
            pltpu.VMEM(w_up.shape, jnp.bfloat16),
            pltpu.VMEM(w_down.shape, jnp.bfloat16),
            pltpu.VMEM((run // 128, sources * pieces, 128), jnp.float32),
            pltpu.VMEM((sources * capacity, width), jnp.bfloat16),
            pltpu.SemaphoreType.DMA((3,)),
        ],
        compiler_params=pltpu.CompilerParams(vmem_limit_bytes=56 * 1024 * 1024),
        cost_estimate=pl.CostEstimate(
            flops=6 * sources * capacity * width * w_gate.shape[1],
            bytes_accessed=3 * w_gate.size * 2,
            transcendentals=0,
        ),
    )(arrived, w_gate, w_up, w_down)


def spread(incoming, beside):
    members = lax.axis_size("z") * lax.axis_size("x")
    copies = jnp.broadcast_to(incoming[None], (members,) + incoming.shape)
    gathered = lax.all_to_all(copies, PLANE, split_axis=0, concat_axis=0, tiled=True)
    gathered = gathered.reshape((-1, incoming.shape[-1]))
    return gathered if beside is None else beside.beside_gather(gathered)


def collect(incoming, beside):
    members = lax.axis_size("z") * lax.axis_size("x")
    parts = incoming.astype(jnp.bfloat16).reshape((members, -1, incoming.shape[-1]))
    received = lax.all_to_all(parts, PLANE, split_axis=0, concat_axis=0, tiled=True)
    return jnp.sum(beside.beside_sum(received).astype(jnp.float32), axis=0)


def halves(incoming):
    width = incoming.shape[1] // 2
    y_lo = lax.axis_index("y_lo")
    own = lax.dynamic_slice_in_dim(incoming, y_lo * width, width, 1)
    far = lax.dynamic_slice_in_dim(incoming, (1 - y_lo) * width, width, 1)
    return own, far


def swap(rows, mask):
    return lax.ppermute(rows, ("y_lo", "y_hi"), [(i, i ^ mask) for i in range(4)])


def pack_kernel(y_lo_ref, wide_ref, *refs):
    blocks, outs = refs[:-4], refs[-4:]
    half = wide_ref.shape[1] // 2
    for mask, out in enumerate(outs):
        start = pl.multiple_of((y_lo_ref[0] ^ (mask // 2)) * half, half)
        out[:, :half] = wide_ref[:, pl.ds(start, half)]
        width = half
        for block in blocks:
            size = block.shape[1] // 2
            first = mask % 2 * size
            out[:, width : width + size] = block[:, first : first + size]
            width += size


def packs(wide, blocks):
    rows = wide.shape[0]
    width = (wide.shape[1] + sum(block.shape[1] for block in blocks)) // 2
    whole = pl.BlockSpec(memory_space=pltpu.VMEM)
    out = jax.ShapeDtypeStruct((rows, width), jnp.bfloat16)
    return pl.pallas_call(
        pack_kernel,
        out_shape=[out] * 4,
        in_specs=[pl.BlockSpec(memory_space=pltpu.SMEM)] + [whole] * (1 + len(blocks)),
        out_specs=[whole] * 4,
        compiler_params=pltpu.CompilerParams(vmem_limit_bytes=8 * 1024 * 1024),
        cost_estimate=pl.CostEstimate(
            flops=0, bytes_accessed=12 * rows * width, transcendentals=0
        ),
    )(lax.axis_index("y_lo").astype(jnp.int32).reshape(1), wide, *blocks)


class Exchange:
    def __init__(self, packed):
        own, far_y_hi, *self.later = packed
        self.rows = [own, swap(far_y_hi, 1)]

    def beside_sum(self, received):
        received, self.rows[1], *self.later = lax.optimization_barrier(
            (received, self.rows[1], *self.later)
        )
        self.rows += [swap(self.later[0], 2), swap(self.later[1], 3)]
        return received

    def beside_gather(self, gathered):
        gathered, *self.rows[2:] = lax.optimization_barrier((gathered, *self.rows[2:]))
        return gathered

    def gathered(self):
        return jnp.concatenate(self.rows, axis=0)


def fetch_half(weight):
    half = weight.shape[0] // 2
    core = lax.axis_index("core")
    mine = lax.dynamic_slice_in_dim(weight, core * half, half, 0)
    return lax.ppermute(mine, ("y_lo", "y_hi"), [(0, 3), (3, 0), (1, 2), (2, 1)])


def assemble_kernel(axis, core_ref, *refs):
    out, sems = refs[-2:]
    count = (len(refs) - 2) // 3
    size = refs[0].shape[axis]
    half = refs[count].shape[0]
    core = core_ref[0]
    places = []

    def place(source, block, start):
        rows = source.shape[0]
        if axis == 1:
            target = out.at[pl.ds(start, rows), pl.ds(block * size, size)]
        else:
            target = out.at[pl.ds(block * size + start, rows), :]
        places.append((source, target))

    for i in range(count):
        place(refs[i], i, 0)
        place(refs[count + i], count + i, pl.multiple_of(core * half, half))
        place(refs[2 * count + i], count + i, pl.multiple_of((1 - core) * half, half))
    copies = [
        pltpu.make_async_copy(source, target, sems.at[k])
        for k, (source, target) in enumerate(places)
    ]
    for copy in copies:
        copy.start()
    for copy in copies:
        copy.wait()


def assemble(owns, fetched, axis):
    swapped = [lax.ppermute(half, "core", SWAP) for half in fetched]
    shape = list(owns[0].shape)
    shape[axis] *= 2 * len(owns)
    far = pl.BlockSpec(memory_space=pl.ANY)
    parts = [*owns, *fetched, *swapped]
    return pl.pallas_call(
        functools.partial(assemble_kernel, axis),
        out_shape=jax.ShapeDtypeStruct(tuple(shape), jnp.bfloat16),
        in_specs=[pl.BlockSpec(memory_space=pltpu.SMEM)] + [far] * len(parts),
        out_specs=pl.BlockSpec(memory_space=pltpu.VMEM),
        scratch_shapes=[pltpu.SemaphoreType.DMA((len(parts),))],
        compiler_params=pltpu.CompilerParams(vmem_limit_bytes=20 * 1024 * 1024),
        cost_estimate=pl.CostEstimate(
            flops=0, bytes_accessed=4 * math.prod(shape), transcendentals=0
        ),
    )(lax.axis_index("core").astype(jnp.int32).reshape(1), *parts)


def on_device(
    hidden_in,
    router_weight,
    expert_gate,
    expert_up,
    expert_down,
    expert_ids,
    segment_ids,
    draft_gain,
    draft_gate,
    draft_up,
    draft_down,
):
    tok_rows = hidden_in.shape[0]
    model_width = hidden_in.shape[1]
    top_count = expert_ids.shape[1]
    experts = router_weight.shape[1]
    capacity = 2 * ((tok_rows * top_count + experts - 1) // experts)
    token_count = tok_rows * lax.axis_size(ALL)
    fetches = [fetch_half(weight) for weight in (draft_gate, draft_up)]
    as_float, inv_rms = normalize(hidden_in)
    normed = (as_float * inv_rms).astype(jnp.bfloat16)
    logits = jnp.dot(normed, router_weight, preferred_element_type=jnp.float32)
    chosen = jnp.take_along_axis(logits, expert_ids, axis=1)
    weights = jnp.exp(chosen)
    route_probs = weights / jnp.sum(weights, axis=1, keepdims=True)
    flat_ids = expert_ids.reshape(-1)
    choice_range = jnp.arange(flat_ids.shape[0], dtype=jnp.int32)
    earlier = (flat_ids[:, None] == flat_ids[None, :]) & (
        choice_range[None, :] < choice_range[:, None]
    )
    slots = flat_ids * capacity + jnp.sum(earlier.astype(jnp.int32), axis=1)
    lines = experts * 2 * capacity * PARTS
    line = jnp.arange(lines, dtype=jnp.int32)
    line_slot = line // (2 * capacity * PARTS) * capacity + line // PARTS % capacity
    piece_slots = jnp.repeat(slots.reshape(tok_rows, top_count), PARTS, axis=0)
    piece_probs = jnp.repeat(route_probs, PARTS, axis=0)
    piece_part = jnp.arange(tok_rows * PARTS, dtype=jnp.int32) % PARTS
    same_part = piece_part[:, None] == (line % PARTS)[None, :]
    hits = [same_part & (piece_slots[:, k : k + 1] == line_slot[None, :]) for k in range(top_count)]
    picker = sum(hit.astype(jnp.float32) for hit in hits).astype(jnp.bfloat16)
    mixer = sum(jnp.where(hit, piece_probs[:, k : k + 1], 0.0) for k, hit in enumerate(hits))
    pieces = normed.reshape(tok_rows * PARTS, model_width // PARTS)
    doubled = contract_rows(picker, pieces).astype(jnp.bfloat16)
    doubled = doubled.reshape(2 * experts, capacity * PARTS, model_width // PARTS)
    arrived = lax.all_to_all(doubled, ALL, split_axis=0, concat_axis=0, tiled=True)
    arrived, fetches[0] = lax.optimization_barrier((arrived, fetches[0]))
    half_parts = expert_half(arrived, expert_gate, expert_up, expert_down, capacity)
    half_parts, fetches[1] = lax.optimization_barrier((half_parts, fetches[1]))
    returned = lax.all_to_all(half_parts, ALL, split_axis=0, concat_axis=0, tiled=True)
    gate_up_weight = assemble([draft_gate, draft_up], fetches[:2], 1)
    returned, gate_up_weight, draft_down = lax.optimization_barrier(
        (returned, gate_up_weight, draft_down)
    )
    fetches.append(fetch_half(draft_down))
    returned = returned.reshape(lines, model_width // PARTS)
    first = mixer.astype(jnp.bfloat16)
    rest = mixer - first.astype(jnp.float32)
    second = rest.astype(jnp.bfloat16)
    third = (rest - second.astype(jnp.float32)).astype(jnp.bfloat16)
    mixed = jnp.dot(
        jnp.concatenate([first, second, third], axis=0),
        returned,
        preferred_element_type=jnp.float32,
    )
    moe_out = jnp.sum(mixed.reshape(3, tok_rows * PARTS, -1), axis=0).reshape(tok_rows, model_width)
    top_state = (as_float + moe_out).astype(jnp.bfloat16)
    units = draft_gate.shape[1]
    half_width = model_width // 2
    norm_gain = draft_gain.astype(jnp.float32)
    segments = segment_ids[0]
    row_size = lax.axis_size(ROW)
    row_start = lax.axis_index(ROW) * tok_rows
    seg_pad = jnp.concatenate([segments, jnp.full((STEPS,), -1, jnp.int32)], axis=0)
    own_segments = lax.dynamic_slice_in_dim(segments, row_start, tok_rows, 0)
    loss_scale = 1.0 / math.sqrt(token_count)
    following = lax.ppermute(
        top_state, ROW, [(i, (i + row_size - 1) % row_size) for i in range(row_size)]
    )
    high_pad = jnp.concatenate([top_state, following], axis=0)
    draft_state = top_state
    saved_steps, forward_rows = [], []
    latest = None
    for step_index in range(STEPS):
        floats_in, inv_in = normalize(draft_state)
        draft_norm = spread((floats_in * inv_in * norm_gain).astype(jnp.bfloat16), latest)
        if step_index == 1:
            draft_norm, gate_up_rows_weight = lax.optimization_barrier(
                (draft_norm, with_layout_constraint(gate_up_weight.T, Layout((0, 1))))
            )
        if step_index == 0:
            draft_norm, fetches[2] = lax.optimization_barrier((draft_norm, fetches[2]))
            down_weight = assemble([draft_down], fetches[2:], 0)
        pres = jnp.split(
            jnp.dot(draft_norm, gate_up_weight, preferred_element_type=jnp.float32), 4, axis=1
        )
        acts = jnp.concatenate(
            [jax.nn.silu(pres[0]) * pres[1], jax.nn.silu(pres[2]) * pres[3]], axis=1
        ).astype(jnp.bfloat16)
        packed = packs(draft_norm, [acts])
        acts, *packed = lax.optimization_barrier((acts, *packed))
        partial = jnp.dot(acts, down_weight, preferred_element_type=jnp.float32)
        latest = Exchange(packed)
        forward_rows.append(latest)
        summed = collect(partial, latest)
        new_state = (floats_in + summed).astype(jnp.bfloat16)
        saved_steps.append((draft_state, pres, new_state))
        draft_state = new_state
    carried = jnp.zeros((tok_rows, model_width), jnp.float32)
    backward_rows = []
    for step_index in reversed(range(STEPS)):
        state_in, pres, state_out = saved_steps[step_index]
        ahead = step_index + 1
        target_rows = high_pad[ahead : ahead + tok_rows]
        same_doc = lax.dynamic_slice_in_dim(seg_pad, row_start + ahead, tok_rows, 0) == own_segments
        grad_state = carried + loss_scale * jnp.where(
            same_doc[:, None], state_out.astype(jnp.float32) - target_rows.astype(jnp.float32), 0.0
        )
        own_rows = grad_state.astype(jnp.bfloat16)
        grad_full = spread(own_rows, latest)
        if step_index == 0:
            own_half, far_half = halves(own_rows)
            others = [swap(own_half, 1), swap(far_half, 2), swap(far_half, 3)]
            grad_full, *others = lax.optimization_barrier((grad_full, *others))
            other_grads = spread(jnp.concatenate(others, axis=0), None)
        grad_act = jnp.split(contract_cols(grad_full, down_weight), 2, axis=1)
        gate_up_grads = []
        for block, block_grad in enumerate(grad_act):
            silu_value, silu_slope = silu_terms(pres[2 * block])
            gate_up_grads.append(block_grad * pres[2 * block + 1] * silu_slope)
            gate_up_grads.append(block_grad * silu_value)
        gate_up_grads = jnp.concatenate(gate_up_grads, axis=1).astype(jnp.bfloat16)
        if step_index == 0:
            own_block, far_block = jnp.split(gate_up_grads, 2, axis=1)
            gate_up_shares = [own_block, swap(far_block, 1), swap(own_block, 2), swap(far_block, 3)]
            break
        packed = packs(grad_full, [gate_up_grads])
        gate_up_grads, *packed = lax.optimization_barrier((gate_up_grads, *packed))
        partial = jnp.dot(gate_up_grads, gate_up_rows_weight, preferred_element_type=jnp.float32)
        latest = Exchange(packed)
        backward_rows.append(latest)
        grad_norm = collect(partial, latest)
        floats_in, inv_in = normalize(state_in)
        weighted = grad_norm * norm_gain
        grad_in = inv_in * weighted - floats_in * inv_in * inv_in * inv_in * jnp.mean(
            floats_in * weighted, axis=-1, keepdims=True
        )
        carried = grad_state + grad_in
    gate_up, down = 0.0, 0.0
    for forward, backward in zip(reversed(forward_rows), backward_rows):
        wide, act_rows = jnp.split(forward.gathered(), [half_width], axis=1)
        grads, gate_up_rows = jnp.split(backward.gathered(), [half_width], axis=1)
        gate_up = gate_up + contract_rows(wide, gate_up_rows)
        down = down + contract_rows(act_rows, grads)
    wide = jnp.concatenate([rows[:, :half_width] for rows in forward_rows[0].rows], axis=0)
    gate_up = gate_up + contract_rows(wide, jnp.concatenate(gate_up_shares, axis=0))
    core = lax.axis_index("core")
    quarter = half_width // 2

    def add_cores(partial, axis):
        mine = lax.dynamic_slice_in_dim(partial, core * quarter, quarter, axis)
        sent = lax.dynamic_slice_in_dim(partial, (1 - core) * quarter, quarter, axis)
        return mine, lax.ppermute(sent.astype(jnp.bfloat16), "core", SWAP)

    mine, received = add_cores(gate_up, 0)
    grad_gate = mine[:, :units] + received[:, :units].astype(jnp.float32)
    grad_up = mine[:, units:] + received[:, units:].astype(jnp.float32)
    other_grads, grad_gate, grad_up = lax.optimization_barrier((other_grads, grad_gate, grad_up))
    own_acts, *other_acts = [rows[:, half_width:] for rows in forward_rows[0].rows]
    other_acts = jnp.stack([acts.reshape(-1, tok_rows, units) for acts in other_acts], axis=1)
    down = down + contract_rows(own_acts, halves(grad_full)[0])
    down = down + contract_rows(other_acts.reshape(-1, units), other_grads)
    mine, received = add_cores(down, 1)
    grad_down = mine + received.astype(jnp.float32)
    return (draft_state, grad_gate, grad_up, grad_down)


def solution(mesh):
    fine = Mesh(mesh.devices.reshape(2, 2, 2, 4, 4), ALL)
    dp = ("y_lo", "core")
    return jax.shard_map(
        on_device,
        mesh=fine,
        in_specs=(
            P(ALL, None),
            P(),
            P(None, ALL),
            P(None, ALL),
            P(ALL, None),
            P(ALL, None),
            P(dp, None),
            P(),
            P(None, ROW),
            P(None, ROW),
            P(ROW, None),
        ),
        out_specs=(
            P(ALL, None),
            P(dp, ROW),
            P(dp, ROW),
            P(ROW, dp),
        ),
        check_vma=False,
    )
```

```python
import functools
import math

import jax
import jax.numpy as jnp
from jax import lax
from jax.experimental import pallas as pl
from jax.experimental.layout import Layout, with_layout_constraint
from jax.experimental.pallas import tpu as pltpu
from jax.sharding import Mesh, PartitionSpec as P

STEPS = 3
PARTS = 4
EPSILON = 1e-06

ALL = ("y_lo", "core", "y_hi", "z", "x")
ROW = ("y_hi", "z", "x")
PLANE = ("z", "x")
SWAP = [(0, 1), (1, 0)]


def normalize(incoming):
    as_float = incoming.astype(jnp.float32)
    inv_rms = lax.rsqrt(jnp.mean(as_float * as_float, axis=-1, keepdims=True) + EPSILON)
    return (as_float, inv_rms)


def silu_terms(gate_pre):
    sigmoid_v = jax.nn.sigmoid(gate_pre)
    return (gate_pre * sigmoid_v, sigmoid_v * (1.0 + gate_pre * (1.0 - sigmoid_v)))


def contract_rows(left_side, right_side):
    return lax.dot_general(
        left_side, right_side, (((0,), (0,)), ((), ())), preferred_element_type=jnp.float32
    )


def contract_cols(left_side, right_side):
    return lax.dot_general(
        left_side, right_side, (((1,), (1,)), ((), ())), preferred_element_type=jnp.float32
    )


def expert_kernel(x_ref, gate_hbm, up_hbm, down_hbm, out_ref, gate, up, down, wide, rows, sems):
    copies = [
        pltpu.make_async_copy(source, target, sems.at[i])
        for i, (source, target) in enumerate(((gate_hbm, gate), (up_hbm, up), (down_hbm, down)))
    ]
    for copy in copies:
        copy.start()
    sources, pieces, run = x_ref.shape
    capacity = rows.shape[0] // sources
    parts = pieces // capacity
    lanes = wide.shape[-1]
    for lane in range(run // lanes):
        columns = pl.ds(lane * lanes, lanes)
        wide[lane] = x_ref[:, :, columns].reshape(sources * pieces, lanes).astype(jnp.float32)
        for piece in range(pieces):
            slot, part = divmod(piece, parts)
            rows[
                pl.ds(slot * sources, sources), pl.ds(part * run + lane * lanes, lanes)
            ] = wide[lane, pl.ds(piece, sources, stride=pieces), :].astype(jnp.bfloat16)
    copies[0].wait()
    gate_pre = jnp.dot(rows[...], gate[...], preferred_element_type=jnp.float32)
    copies[1].wait()
    up_pre = jnp.dot(rows[...], up[...], preferred_element_type=jnp.float32)
    act = (gate_pre * jax.nn.sigmoid(gate_pre) * up_pre).astype(jnp.bfloat16)
    copies[2].wait()
    for part in range(parts):
        result = jnp.dot(
            act, down[:, pl.ds(part * run, run)], preferred_element_type=jnp.float32
        )
        for slot in range(capacity):
            for lane in range(run // lanes):
                wide[lane, pl.ds(slot * parts + part, sources, stride=pieces), :] = result[
                    slot * sources : (slot + 1) * sources, lane * lanes : (lane + 1) * lanes
                ]
    for lane in range(run // lanes):
        out_ref[:, :, pl.ds(lane * lanes, lanes)] = (
            wide[lane].astype(jnp.bfloat16).reshape(sources, pieces, lanes)
        )


def expert_half(arrived, w_gate, w_up, w_down, capacity):
    sources, pieces, run = arrived.shape
    width = w_gate.shape[0]
    whole = pl.BlockSpec(memory_space=pltpu.VMEM)
    far = pl.BlockSpec(memory_space=pl.ANY)
    return pl.pallas_call(
        expert_kernel,
        out_shape=jax.ShapeDtypeStruct(arrived.shape, jnp.bfloat16),
        in_specs=[whole, far, far, far],
        out_specs=whole,
        scratch_shapes=[
            pltpu.VMEM(w_gate.shape, jnp.bfloat16),
            pltpu.VMEM(w_up.shape, jnp.bfloat16),
            pltpu.VMEM(w_down.shape, jnp.bfloat16),
            pltpu.VMEM((run // 128, sources * pieces, 128), jnp.float32),
            pltpu.VMEM((sources * capacity, width), jnp.bfloat16),
            pltpu.SemaphoreType.DMA((3,)),
        ],
        compiler_params=pltpu.CompilerParams(vmem_limit_bytes=56 * 1024 * 1024),
        cost_estimate=pl.CostEstimate(
            flops=6 * sources * capacity * width * w_gate.shape[1],
            bytes_accessed=3 * w_gate.size * 2,
            transcendentals=0,
        ),
    )(arrived, w_gate, w_up, w_down)


def spread(incoming, beside):
    members = lax.axis_size("z") * lax.axis_size("x")
    copies = jnp.broadcast_to(incoming[None], (members,) + incoming.shape)
    gathered = lax.all_to_all(copies, PLANE, split_axis=0, concat_axis=0, tiled=True)
    gathered = gathered.reshape((-1, incoming.shape[-1]))
    return gathered if beside is None else beside.beside_gather(gathered)


def collect(incoming, beside, product=None):
    members = lax.axis_size("z") * lax.axis_size("x")
    parts = incoming.astype(jnp.bfloat16).reshape((members, -1, incoming.shape[-1]))
    received = lax.all_to_all(parts, PLANE, split_axis=0, concat_axis=0, tiled=True)
    if product is not None:
        received, product = lax.optimization_barrier((received, product))
    total = jnp.sum(beside.beside_sum(received).astype(jnp.float32), axis=0)
    return total if product is None else (total, product)


def halves(incoming):
    width = incoming.shape[1] // 2
    y_lo = lax.axis_index("y_lo")
    own = lax.dynamic_slice_in_dim(incoming, y_lo * width, width, 1)
    far = lax.dynamic_slice_in_dim(incoming, (1 - y_lo) * width, width, 1)
    return own, far


def swap(rows, mask):
    return lax.ppermute(rows, ("y_lo", "y_hi"), [(i, i ^ mask) for i in range(4)])


def pack_kernel(y_lo_ref, wide_ref, *refs):
    blocks, outs = refs[:-4], refs[-4:]
    half = wide_ref.shape[1] // 2
    for mask, out in enumerate(outs):
        start = pl.multiple_of((y_lo_ref[0] ^ (mask // 2)) * half, half)
        out[:, :half] = wide_ref[:, pl.ds(start, half)]
        width = half
        for block in blocks:
            size = block.shape[1] // 2
            first = mask % 2 * size
            out[:, width : width + size] = block[:, first : first + size]
            width += size


def packs(wide, blocks):
    rows = wide.shape[0]
    width = (wide.shape[1] + sum(block.shape[1] for block in blocks)) // 2
    whole = pl.BlockSpec(memory_space=pltpu.VMEM)
    out = jax.ShapeDtypeStruct((rows, width), jnp.bfloat16)
    return pl.pallas_call(
        pack_kernel,
        out_shape=[out] * 4,
        in_specs=[pl.BlockSpec(memory_space=pltpu.SMEM)] + [whole] * (1 + len(blocks)),
        out_specs=[whole] * 4,
        compiler_params=pltpu.CompilerParams(vmem_limit_bytes=8 * 1024 * 1024),
        cost_estimate=pl.CostEstimate(
            flops=0, bytes_accessed=12 * rows * width, transcendentals=0
        ),
    )(lax.axis_index("y_lo").astype(jnp.int32).reshape(1), wide, *blocks)


class Exchange:
    def __init__(self, packed):
        own, far_y_hi, *self.later = packed
        self.rows = [own, swap(far_y_hi, 1)]

    def beside_sum(self, received):
        received, self.rows[1], *self.later = lax.optimization_barrier(
            (received, self.rows[1], *self.later)
        )
        self.rows += [swap(self.later[0], 2), swap(self.later[1], 3)]
        return received

    def beside_gather(self, gathered):
        gathered, *self.rows[2:] = lax.optimization_barrier((gathered, *self.rows[2:]))
        return gathered

    def gathered(self):
        return jnp.concatenate(self.rows, axis=0)


def fetch_half(weight):
    half = weight.shape[0] // 2
    core = lax.axis_index("core")
    mine = lax.dynamic_slice_in_dim(weight, core * half, half, 0)
    return lax.ppermute(mine, ("y_lo", "y_hi"), [(0, 3), (3, 0), (1, 2), (2, 1)])


def assemble_kernel(axis, core_ref, *refs):
    out, sems = refs[-2:]
    count = (len(refs) - 2) // 3
    size = refs[0].shape[axis]
    half = refs[count].shape[0]
    core = core_ref[0]
    places = []

    def place(source, block, start):
        rows = source.shape[0]
        if axis == 1:
            target = out.at[pl.ds(start, rows), pl.ds(block * size, size)]
        else:
            target = out.at[pl.ds(block * size + start, rows), :]
        places.append((source, target))

    for i in range(count):
        place(refs[i], i, 0)
        place(refs[count + i], count + i, pl.multiple_of(core * half, half))
        place(refs[2 * count + i], count + i, pl.multiple_of((1 - core) * half, half))
    copies = [
        pltpu.make_async_copy(source, target, sems.at[k])
        for k, (source, target) in enumerate(places)
    ]
    for copy in copies:
        copy.start()
    for copy in copies:
        copy.wait()


def assemble(owns, fetched, axis):
    swapped = [lax.ppermute(half, "core", SWAP) for half in fetched]
    shape = list(owns[0].shape)
    shape[axis] *= 2 * len(owns)
    far = pl.BlockSpec(memory_space=pl.ANY)
    parts = [*owns, *fetched, *swapped]
    return pl.pallas_call(
        functools.partial(assemble_kernel, axis),
        out_shape=jax.ShapeDtypeStruct(tuple(shape), jnp.bfloat16),
        in_specs=[pl.BlockSpec(memory_space=pltpu.SMEM)] + [far] * len(parts),
        out_specs=pl.BlockSpec(memory_space=pltpu.VMEM),
        scratch_shapes=[pltpu.SemaphoreType.DMA((len(parts),))],
        compiler_params=pltpu.CompilerParams(vmem_limit_bytes=20 * 1024 * 1024),
        cost_estimate=pl.CostEstimate(
            flops=0, bytes_accessed=4 * math.prod(shape), transcendentals=0
        ),
    )(lax.axis_index("core").astype(jnp.int32).reshape(1), *parts)


def on_device(
    hidden_in,
    router_weight,
    expert_gate,
    expert_up,
    expert_down,
    expert_ids,
    segment_ids,
    draft_gain,
    draft_gate,
    draft_up,
    draft_down,
):
    tok_rows = hidden_in.shape[0]
    model_width = hidden_in.shape[1]
    top_count = expert_ids.shape[1]
    experts = router_weight.shape[1]
    capacity = 2 * ((tok_rows * top_count + experts - 1) // experts)
    token_count = tok_rows * lax.axis_size(ALL)
    fetches = [fetch_half(weight) for weight in (draft_gate, draft_up, draft_down)]
    as_float, inv_rms = normalize(hidden_in)
    normed = (as_float * inv_rms).astype(jnp.bfloat16)
    logits = jnp.dot(normed, router_weight, preferred_element_type=jnp.float32)
    chosen = jnp.take_along_axis(logits, expert_ids, axis=1)
    weights = jnp.exp(chosen)
    route_probs = weights / jnp.sum(weights, axis=1, keepdims=True)
    flat_ids = expert_ids.reshape(-1)
    choice_range = jnp.arange(flat_ids.shape[0], dtype=jnp.int32)
    earlier = (flat_ids[:, None] == flat_ids[None, :]) & (
        choice_range[None, :] < choice_range[:, None]
    )
    slots = flat_ids * capacity + jnp.sum(earlier.astype(jnp.int32), axis=1)
    lines = experts * 2 * capacity * PARTS
    line = jnp.arange(lines, dtype=jnp.int32)
    line_slot = line // (2 * capacity * PARTS) * capacity + line // PARTS % capacity
    piece_slots = jnp.repeat(slots.reshape(tok_rows, top_count), PARTS, axis=0)
    piece_probs = jnp.repeat(route_probs, PARTS, axis=0)
    piece_part = jnp.arange(tok_rows * PARTS, dtype=jnp.int32) % PARTS
    same_part = piece_part[:, None] == (line % PARTS)[None, :]
    hits = [same_part & (piece_slots[:, k : k + 1] == line_slot[None, :]) for k in range(top_count)]
    picker = sum(hit.astype(jnp.float32) for hit in hits).astype(jnp.bfloat16)
    mixer = sum(jnp.where(hit, piece_probs[:, k : k + 1], 0.0) for k, hit in enumerate(hits))
    pieces = normed.reshape(tok_rows * PARTS, model_width // PARTS)
    doubled = contract_rows(picker, pieces).astype(jnp.bfloat16)
    doubled = doubled.reshape(2 * experts, capacity * PARTS, model_width // PARTS)
    arrived = lax.all_to_all(doubled, ALL, split_axis=0, concat_axis=0, tiled=True)
    arrived, fetches[0] = lax.optimization_barrier((arrived, fetches[0]))
    half_parts = expert_half(arrived, expert_gate, expert_up, expert_down, capacity)
    half_parts, fetches[1] = lax.optimization_barrier((half_parts, fetches[1]))
    returned = lax.all_to_all(half_parts, ALL, split_axis=0, concat_axis=0, tiled=True)
    gate_up_weight = assemble([draft_gate, draft_up], fetches[:2], 1)
    returned, gate_up_weight = lax.optimization_barrier((returned, gate_up_weight))
    returned = returned.reshape(lines, model_width // PARTS)
    first = mixer.astype(jnp.bfloat16)
    rest = mixer - first.astype(jnp.float32)
    second = rest.astype(jnp.bfloat16)
    third = (rest - second.astype(jnp.float32)).astype(jnp.bfloat16)
    mixed = jnp.dot(
        jnp.concatenate([first, second, third], axis=0),
        returned,
        preferred_element_type=jnp.float32,
    )
    moe_out = jnp.sum(mixed.reshape(3, tok_rows * PARTS, -1), axis=0).reshape(tok_rows, model_width)
    top_state = (as_float + moe_out).astype(jnp.bfloat16)
    units = draft_gate.shape[1]
    half_width = model_width // 2
    norm_gain = draft_gain.astype(jnp.float32)
    segments = segment_ids[0]
    row_size = lax.axis_size(ROW)
    row_start = lax.axis_index(ROW) * tok_rows
    seg_pad = jnp.concatenate([segments, jnp.full((STEPS,), -1, jnp.int32)], axis=0)
    own_segments = lax.dynamic_slice_in_dim(segments, row_start, tok_rows, 0)
    loss_scale = 1.0 / math.sqrt(token_count)
    following = lax.ppermute(
        top_state, ROW, [(i, (i + row_size - 1) % row_size) for i in range(row_size)]
    )
    high_pad = jnp.concatenate([top_state, following], axis=0)
    draft_state = top_state
    saved_steps, forward_rows = [], []
    latest = None
    for step_index in range(STEPS):
        floats_in, inv_in = normalize(draft_state)
        draft_norm = spread((floats_in * inv_in * norm_gain).astype(jnp.bfloat16), latest)
        if step_index == 1:
            draft_norm, gate_up_rows_weight = lax.optimization_barrier(
                (draft_norm, with_layout_constraint(gate_up_weight.T, Layout((0, 1))))
            )
        if step_index == 0:
            draft_norm, fetches[2] = lax.optimization_barrier((draft_norm, fetches[2]))
            down_weight = assemble([draft_down], fetches[2:], 0)
        pres = jnp.split(
            jnp.dot(draft_norm, gate_up_weight, preferred_element_type=jnp.float32), 4, axis=1
        )
        acts = jnp.concatenate(
            [jax.nn.silu(pres[0]) * pres[1], jax.nn.silu(pres[2]) * pres[3]], axis=1
        ).astype(jnp.bfloat16)
        packed = packs(draft_norm, [acts])
        acts, *packed = lax.optimization_barrier((acts, *packed))
        partial = jnp.dot(acts, down_weight, preferred_element_type=jnp.float32)
        latest = Exchange(packed)
        forward_rows.append(latest)
        summed = collect(partial, latest)
        new_state = (floats_in + summed).astype(jnp.bfloat16)
        saved_steps.append((draft_state, pres, new_state))
        draft_state = new_state
    carried = jnp.zeros((tok_rows, model_width), jnp.float32)
    backward_rows = []
    for step_index in reversed(range(STEPS)):
        state_in, pres, state_out = saved_steps[step_index]
        ahead = step_index + 1
        target_rows = high_pad[ahead : ahead + tok_rows]
        same_doc = lax.dynamic_slice_in_dim(seg_pad, row_start + ahead, tok_rows, 0) == own_segments
        grad_state = carried + loss_scale * jnp.where(
            same_doc[:, None], state_out.astype(jnp.float32) - target_rows.astype(jnp.float32), 0.0
        )
        own_rows = grad_state.astype(jnp.bfloat16)
        grad_full = spread(own_rows, latest)
        if step_index == 0:
            own_half, far_half = halves(own_rows)
            others = [swap(own_half, 1), swap(far_half, 2), swap(far_half, 3)]
            grad_full, *others = lax.optimization_barrier((grad_full, *others))
            other_grads = spread(jnp.concatenate(others, axis=0), None)
        grad_act = jnp.split(contract_cols(grad_full, down_weight), 2, axis=1)
        gate_up_grads = []
        for block, block_grad in enumerate(grad_act):
            silu_value, silu_slope = silu_terms(pres[2 * block])
            gate_up_grads.append(block_grad * pres[2 * block + 1] * silu_slope)
            gate_up_grads.append(block_grad * silu_value)
        gate_up_grads = jnp.concatenate(gate_up_grads, axis=1).astype(jnp.bfloat16)
        if step_index == 0:
            own_block, far_block = jnp.split(gate_up_grads, 2, axis=1)
            gate_up_shares = [own_block, swap(far_block, 1), swap(own_block, 2), swap(far_block, 3)]
            break
        packed = packs(grad_full, [gate_up_grads])
        gate_up_grads, *packed = lax.optimization_barrier((gate_up_grads, *packed))
        partial = jnp.dot(gate_up_grads, gate_up_rows_weight, preferred_element_type=jnp.float32)
        latest = Exchange(packed)
        backward_rows.append(latest)
        if step_index == STEPS - 1:
            grad_norm = collect(partial, latest)
        else:
            wide = forward_rows[-1].gathered()[:, :half_width]
            gate_up = contract_rows(wide, backward_rows[0].gathered()[:, half_width:])
            grad_norm, gate_up = collect(partial, latest, gate_up)
        floats_in, inv_in = normalize(state_in)
        weighted = grad_norm * norm_gain
        grad_in = inv_in * weighted - floats_in * inv_in * inv_in * inv_in * jnp.mean(
            floats_in * weighted, axis=-1, keepdims=True
        )
        carried = grad_state + grad_in
    down = 0.0
    for forward, backward in zip(reversed(forward_rows), backward_rows):
        wide, act_rows = jnp.split(forward.gathered(), [half_width], axis=1)
        grads, gate_up_rows = jnp.split(backward.gathered(), [half_width], axis=1)
        if backward is not backward_rows[0]:
            gate_up = gate_up + contract_rows(wide, gate_up_rows)
        down = down + contract_rows(act_rows, grads)
    wide = jnp.concatenate([rows[:, :half_width] for rows in forward_rows[0].rows], axis=0)
    gate_up = gate_up + contract_rows(wide, jnp.concatenate(gate_up_shares, axis=0))
    core = lax.axis_index("core")
    quarter = half_width // 2

    def add_cores(partial, axis):
        mine = lax.dynamic_slice_in_dim(partial, core * quarter, quarter, axis)
        sent = lax.dynamic_slice_in_dim(partial, (1 - core) * quarter, quarter, axis)
        return mine, lax.ppermute(sent.astype(jnp.bfloat16), "core", SWAP)

    mine, received = add_cores(gate_up, 0)
    grad_gate = mine[:, :units] + received[:, :units].astype(jnp.float32)
    grad_up = mine[:, units:] + received[:, units:].astype(jnp.float32)
    other_grads, grad_gate, grad_up = lax.optimization_barrier((other_grads, grad_gate, grad_up))
    own_acts, *other_acts = [rows[:, half_width:] for rows in forward_rows[0].rows]
    other_acts = jnp.stack([acts.reshape(-1, tok_rows, units) for acts in other_acts], axis=1)
    down = down + contract_rows(own_acts, halves(grad_full)[0])
    down = down + contract_rows(other_acts.reshape(-1, units), other_grads)
    mine, received = add_cores(down, 1)
    grad_down = mine + received.astype(jnp.float32)
    return (draft_state, grad_gate, grad_up, grad_down)


def solution(mesh):
    fine = Mesh(mesh.devices.reshape(2, 2, 2, 4, 4), ALL)
    dp = ("y_lo", "core")
    return jax.shard_map(
        on_device,
        mesh=fine,
        in_specs=(
            P(ALL, None),
            P(),
            P(None, ALL),
            P(None, ALL),
            P(ALL, None),
            P(ALL, None),
            P(dp, None),
            P(),
            P(None, ROW),
            P(None, ROW),
            P(ROW, None),
        ),
        out_specs=(
            P(ALL, None),
            P(dp, ROW),
            P(dp, ROW),
            P(ROW, dp),
        ),
        check_vma=False,
    )
```

```python
import functools
import math

import jax
import jax.numpy as jnp
from jax import lax
from jax.experimental import pallas as pl
from jax.experimental.layout import Layout, with_layout_constraint
from jax.experimental.pallas import tpu as pltpu
from jax.sharding import Mesh, PartitionSpec as P

STEPS = 3
PARTS = 4
EPSILON = 1e-06

ALL = ("y_lo", "core", "y_hi", "z", "x")
ROW = ("y_hi", "z", "x")
PLANE = ("z", "x")
SWAP = [(0, 1), (1, 0)]


def normalize(incoming):
    as_float = incoming.astype(jnp.float32)
    inv_rms = lax.rsqrt(jnp.mean(as_float * as_float, axis=-1, keepdims=True) + EPSILON)
    return (as_float, inv_rms)


def silu_terms(gate_pre):
    sigmoid_v = jax.nn.sigmoid(gate_pre)
    return (gate_pre * sigmoid_v, sigmoid_v * (1.0 + gate_pre * (1.0 - sigmoid_v)))


def contract_rows(left_side, right_side):
    return lax.dot_general(
        left_side, right_side, (((0,), (0,)), ((), ())), preferred_element_type=jnp.float32
    )


def contract_cols(left_side, right_side):
    return lax.dot_general(
        left_side, right_side, (((1,), (1,)), ((), ())), preferred_element_type=jnp.float32
    )


def expert_kernel(x_ref, gate_hbm, up_hbm, down_hbm, out_ref, gate, up, down, wide, rows, sems):
    copies = [
        pltpu.make_async_copy(source, target, sems.at[i])
        for i, (source, target) in enumerate(((gate_hbm, gate), (up_hbm, up), (down_hbm, down)))
    ]
    for copy in copies:
        copy.start()
    sources, pieces, run = x_ref.shape
    capacity = rows.shape[0] // sources
    parts = pieces // capacity
    lanes = wide.shape[-1]
    for lane in range(run // lanes):
        columns = pl.ds(lane * lanes, lanes)
        wide[lane] = x_ref[:, :, columns].reshape(sources * pieces, lanes).astype(jnp.float32)
        for piece in range(pieces):
            slot, part = divmod(piece, parts)
            rows[
                pl.ds(slot * sources, sources), pl.ds(part * run + lane * lanes, lanes)
            ] = wide[lane, pl.ds(piece, sources, stride=pieces), :].astype(jnp.bfloat16)
    copies[0].wait()
    gate_pre = jnp.dot(rows[...], gate[...], preferred_element_type=jnp.float32)
    copies[1].wait()
    up_pre = jnp.dot(rows[...], up[...], preferred_element_type=jnp.float32)
    act = (gate_pre * jax.nn.sigmoid(gate_pre) * up_pre).astype(jnp.bfloat16)
    copies[2].wait()
    for part in range(parts):
        result = jnp.dot(
            act, down[:, pl.ds(part * run, run)], preferred_element_type=jnp.float32
        )
        for slot in range(capacity):
            for lane in range(run // lanes):
                wide[lane, pl.ds(slot * parts + part, sources, stride=pieces), :] = result[
                    slot * sources : (slot + 1) * sources, lane * lanes : (lane + 1) * lanes
                ]
    for lane in range(run // lanes):
        out_ref[:, :, pl.ds(lane * lanes, lanes)] = (
            wide[lane].astype(jnp.bfloat16).reshape(sources, pieces, lanes)
        )


def expert_half(arrived, w_gate, w_up, w_down, capacity):
    sources, pieces, run = arrived.shape
    width = w_gate.shape[0]
    whole = pl.BlockSpec(memory_space=pltpu.VMEM)
    far = pl.BlockSpec(memory_space=pl.ANY)
    return pl.pallas_call(
        expert_kernel,
        out_shape=jax.ShapeDtypeStruct(arrived.shape, jnp.bfloat16),
        in_specs=[whole, far, far, far],
        out_specs=whole,
        scratch_shapes=[
            pltpu.VMEM(w_gate.shape, jnp.bfloat16),
            pltpu.VMEM(w_up.shape, jnp.bfloat16),
            pltpu.VMEM(w_down.shape, jnp.bfloat16),
            pltpu.VMEM((run // 128, sources * pieces, 128), jnp.float32),
            pltpu.VMEM((sources * capacity, width), jnp.bfloat16),
            pltpu.SemaphoreType.DMA((3,)),
        ],
        compiler_params=pltpu.CompilerParams(vmem_limit_bytes=56 * 1024 * 1024),
        cost_estimate=pl.CostEstimate(
            flops=6 * sources * capacity * width * w_gate.shape[1],
            bytes_accessed=3 * w_gate.size * 2,
            transcendentals=0,
        ),
    )(arrived, w_gate, w_up, w_down)


def spread(incoming, beside):
    members = lax.axis_size("z") * lax.axis_size("x")
    copies = jnp.broadcast_to(incoming[None], (members,) + incoming.shape)
    gathered = lax.all_to_all(copies, PLANE, split_axis=0, concat_axis=0, tiled=True)
    gathered = gathered.reshape((-1, incoming.shape[-1]))
    return gathered if beside is None else beside.beside_gather(gathered)


def collect(incoming, beside, product=None):
    members = lax.axis_size("z") * lax.axis_size("x")
    parts = incoming.astype(jnp.bfloat16).reshape((members, -1, incoming.shape[-1]))
    received = lax.all_to_all(parts, PLANE, split_axis=0, concat_axis=0, tiled=True)
    if product is not None:
        received, product = lax.optimization_barrier((received, product))
    total = jnp.sum(beside.beside_sum(received).astype(jnp.float32), axis=0)
    return total if product is None else (total, product)


def halves(incoming):
    width = incoming.shape[1] // 2
    y_lo = lax.axis_index("y_lo")
    own = lax.dynamic_slice_in_dim(incoming, y_lo * width, width, 1)
    far = lax.dynamic_slice_in_dim(incoming, (1 - y_lo) * width, width, 1)
    return own, far


def swap(rows, mask):
    return lax.ppermute(rows, ("y_lo", "y_hi"), [(i, i ^ mask) for i in range(4)])


def pack_kernel(y_lo_ref, wide_ref, *refs):
    blocks, outs = refs[:-4], refs[-4:]
    half = wide_ref.shape[1] // 2
    for mask, out in enumerate(outs):
        start = pl.multiple_of((y_lo_ref[0] ^ (mask // 2)) * half, half)
        out[:, :half] = wide_ref[:, pl.ds(start, half)]
        width = half
        for block in blocks:
            size = block.shape[1] // 2
            first = mask % 2 * size
            out[:, width : width + size] = block[:, first : first + size]
            width += size


def packs(wide, blocks):
    rows = wide.shape[0]
    width = (wide.shape[1] + sum(block.shape[1] for block in blocks)) // 2
    whole = pl.BlockSpec(memory_space=pltpu.VMEM)
    out = jax.ShapeDtypeStruct((rows, width), jnp.bfloat16)
    return pl.pallas_call(
        pack_kernel,
        out_shape=[out] * 4,
        in_specs=[pl.BlockSpec(memory_space=pltpu.SMEM)] + [whole] * (1 + len(blocks)),
        out_specs=[whole] * 4,
        compiler_params=pltpu.CompilerParams(vmem_limit_bytes=8 * 1024 * 1024),
        cost_estimate=pl.CostEstimate(
            flops=0, bytes_accessed=12 * rows * width, transcendentals=0
        ),
    )(lax.axis_index("y_lo").astype(jnp.int32).reshape(1), wide, *blocks)


class Exchange:
    def __init__(self, packed):
        own, far_y_hi, *self.later = packed
        self.rows = [own, swap(far_y_hi, 1)]

    def beside_sum(self, received):
        received, self.rows[1], *self.later = lax.optimization_barrier(
            (received, self.rows[1], *self.later)
        )
        self.rows += [swap(self.later[0], 2), swap(self.later[1], 3)]
        return received

    def beside_gather(self, gathered):
        gathered, *self.rows[2:] = lax.optimization_barrier((gathered, *self.rows[2:]))
        return gathered

    def gathered(self):
        return jnp.concatenate(self.rows, axis=0)


def fetch_half(weight, pieces=1):
    half = weight.shape[0] // 2
    core = lax.axis_index("core")
    mine = lax.dynamic_slice_in_dim(weight, core * half, half, 0)
    return [
        lax.ppermute(piece, ("y_lo", "y_hi"), [(0, 3), (3, 0), (1, 2), (2, 1)])
        for piece in jnp.split(mine, pieces, axis=0)
    ]


def assemble_kernel(axis, core_ref, *refs):
    out, sems = refs[-2:]
    count = (len(refs) - 2) // 3
    size = refs[0].shape[axis]
    half = refs[count].shape[0]
    core = core_ref[0]
    places = []

    def place(source, block, start):
        rows = source.shape[0]
        if axis == 1:
            target = out.at[pl.ds(start, rows), pl.ds(block * size, size)]
        else:
            target = out.at[pl.ds(block * size + start, rows), :]
        places.append((source, target))

    for i in range(count):
        place(refs[i], i, 0)
        place(refs[count + i], count + i, pl.multiple_of(core * half, half))
        place(refs[2 * count + i], count + i, pl.multiple_of((1 - core) * half, half))
    copies = [
        pltpu.make_async_copy(source, target, sems.at[k])
        for k, (source, target) in enumerate(places)
    ]
    for copy in copies:
        copy.start()
    for copy in copies:
        copy.wait()


def assemble(owns, fetched, axis):
    swapped = [lax.ppermute(half, "core", SWAP) for half in fetched]
    shape = list(owns[0].shape)
    shape[axis] *= 2 * len(owns)
    far = pl.BlockSpec(memory_space=pl.ANY)
    parts = [*owns, *fetched, *swapped]
    return pl.pallas_call(
        functools.partial(assemble_kernel, axis),
        out_shape=jax.ShapeDtypeStruct(tuple(shape), jnp.bfloat16),
        in_specs=[pl.BlockSpec(memory_space=pltpu.SMEM)] + [far] * len(parts),
        out_specs=pl.BlockSpec(memory_space=pltpu.VMEM),
        scratch_shapes=[pltpu.SemaphoreType.DMA((len(parts),))],
        compiler_params=pltpu.CompilerParams(vmem_limit_bytes=20 * 1024 * 1024),
        cost_estimate=pl.CostEstimate(
            flops=0, bytes_accessed=4 * math.prod(shape), transcendentals=0
        ),
    )(lax.axis_index("core").astype(jnp.int32).reshape(1), *parts)


def on_device(
    hidden_in,
    router_weight,
    expert_gate,
    expert_up,
    expert_down,
    expert_ids,
    segment_ids,
    draft_gain,
    draft_gate,
    draft_up,
    draft_down,
):
    tok_rows = hidden_in.shape[0]
    model_width = hidden_in.shape[1]
    top_count = expert_ids.shape[1]
    experts = router_weight.shape[1]
    capacity = 2 * ((tok_rows * top_count + experts - 1) // experts)
    token_count = tok_rows * lax.axis_size(ALL)
    up_first, up_rest = fetch_half(draft_up, 2)
    fetches = [*fetch_half(draft_gate), None, *fetch_half(draft_down)]
    as_float, inv_rms = normalize(hidden_in)
    normed = (as_float * inv_rms).astype(jnp.bfloat16)
    logits = jnp.dot(normed, router_weight, preferred_element_type=jnp.float32)
    chosen = jnp.take_along_axis(logits, expert_ids, axis=1)
    weights = jnp.exp(chosen)
    route_probs = weights / jnp.sum(weights, axis=1, keepdims=True)
    flat_ids = expert_ids.reshape(-1)
    choice_range = jnp.arange(flat_ids.shape[0], dtype=jnp.int32)
    earlier = (flat_ids[:, None] == flat_ids[None, :]) & (
        choice_range[None, :] < choice_range[:, None]
    )
    slots = flat_ids * capacity + jnp.sum(earlier.astype(jnp.int32), axis=1)
    lines = experts * 2 * capacity * PARTS
    line = jnp.arange(lines, dtype=jnp.int32)
    line_slot = line // (2 * capacity * PARTS) * capacity + line // PARTS % capacity
    piece_slots = jnp.repeat(slots.reshape(tok_rows, top_count), PARTS, axis=0)
    piece_probs = jnp.repeat(route_probs, PARTS, axis=0)
    piece_part = jnp.arange(tok_rows * PARTS, dtype=jnp.int32) % PARTS
    same_part = piece_part[:, None] == (line % PARTS)[None, :]
    hits = [same_part & (piece_slots[:, k : k + 1] == line_slot[None, :]) for k in range(top_count)]
    picker = sum(hit.astype(jnp.float32) for hit in hits).astype(jnp.bfloat16)
    mixer = sum(jnp.where(hit, piece_probs[:, k : k + 1], 0.0) for k, hit in enumerate(hits))
    pieces = normed.reshape(tok_rows * PARTS, model_width // PARTS)
    doubled = contract_rows(picker, pieces).astype(jnp.bfloat16)
    doubled = doubled.reshape(2 * experts, capacity * PARTS, model_width // PARTS)
    arrived = lax.all_to_all(doubled, ALL, split_axis=0, concat_axis=0, tiled=True)
    arrived, fetches[0] = lax.optimization_barrier((arrived, fetches[0]))
    half_parts = expert_half(arrived, expert_gate, expert_up, expert_down, capacity)
    half_parts, up_first = lax.optimization_barrier((half_parts, up_first))
    fetches[1] = jnp.concatenate([up_first, up_rest], axis=0)
    returned = lax.all_to_all(half_parts, ALL, split_axis=0, concat_axis=0, tiled=True)
    gate_up_weight = assemble([draft_gate, draft_up], fetches[:2], 1)
    returned, gate_up_weight = lax.optimization_barrier((returned, gate_up_weight))
    returned = returned.reshape(lines, model_width // PARTS)
    first = mixer.astype(jnp.bfloat16)
    rest = mixer - first.astype(jnp.float32)
    second = rest.astype(jnp.bfloat16)
    third = (rest - second.astype(jnp.float32)).astype(jnp.bfloat16)
    mixed = jnp.dot(
        jnp.concatenate([first, second, third], axis=0),
        returned,
        preferred_element_type=jnp.float32,
    )
    moe_out = jnp.sum(mixed.reshape(3, tok_rows * PARTS, -1), axis=0).reshape(tok_rows, model_width)
    top_state = (as_float + moe_out).astype(jnp.bfloat16)
    units = draft_gate.shape[1]
    half_width = model_width // 2
    norm_gain = draft_gain.astype(jnp.float32)
    segments = segment_ids[0]
    row_size = lax.axis_size(ROW)
    row_start = lax.axis_index(ROW) * tok_rows
    seg_pad = jnp.concatenate([segments, jnp.full((STEPS,), -1, jnp.int32)], axis=0)
    own_segments = lax.dynamic_slice_in_dim(segments, row_start, tok_rows, 0)
    loss_scale = 1.0 / math.sqrt(token_count)
    following = lax.ppermute(
        top_state, ROW, [(i, (i + row_size - 1) % row_size) for i in range(row_size)]
    )
    high_pad = jnp.concatenate([top_state, following], axis=0)
    draft_state = top_state
    saved_steps, forward_rows = [], []
    latest = None
    for step_index in range(STEPS):
        floats_in, inv_in = normalize(draft_state)
        draft_norm = spread((floats_in * inv_in * norm_gain).astype(jnp.bfloat16), latest)
        if step_index == 1:
            draft_norm, gate_up_rows_weight = lax.optimization_barrier(
                (draft_norm, with_layout_constraint(gate_up_weight.T, Layout((0, 1))))
            )
        if step_index == 0:
            draft_norm, fetches[2] = lax.optimization_barrier((draft_norm, fetches[2]))
            down_weight = assemble([draft_down], fetches[2:], 0)
        pres = jnp.split(
            jnp.dot(draft_norm, gate_up_weight, preferred_element_type=jnp.float32), 4, axis=1
        )
        acts = jnp.concatenate(
            [jax.nn.silu(pres[0]) * pres[1], jax.nn.silu(pres[2]) * pres[3]], axis=1
        ).astype(jnp.bfloat16)
        packed = packs(draft_norm, [acts])
        acts, *packed = lax.optimization_barrier((acts, *packed))
        partial = jnp.dot(acts, down_weight, preferred_element_type=jnp.float32)
        latest = Exchange(packed)
        forward_rows.append(latest)
        summed = collect(partial, latest)
        new_state = (floats_in + summed).astype(jnp.bfloat16)
        saved_steps.append((draft_state, pres, new_state))
        draft_state = new_state
    carried = jnp.zeros((tok_rows, model_width), jnp.float32)
    backward_rows = []
    for step_index in reversed(range(STEPS)):
        state_in, pres, state_out = saved_steps[step_index]
        ahead = step_index + 1
        target_rows = high_pad[ahead : ahead + tok_rows]
        same_doc = lax.dynamic_slice_in_dim(seg_pad, row_start + ahead, tok_rows, 0) == own_segments
        grad_state = carried + loss_scale * jnp.where(
            same_doc[:, None], state_out.astype(jnp.float32) - target_rows.astype(jnp.float32), 0.0
        )
        own_rows = grad_state.astype(jnp.bfloat16)
        grad_full = spread(own_rows, latest)
        if step_index == 0:
            own_half, far_half = halves(own_rows)
            others = [swap(own_half, 1), swap(far_half, 2), swap(far_half, 3)]
            grad_full, *others = lax.optimization_barrier((grad_full, *others))
            other_grads = spread(jnp.concatenate(others, axis=0), None)
        grad_act = jnp.split(contract_cols(grad_full, down_weight), 2, axis=1)
        gate_up_grads = []
        for block, block_grad in enumerate(grad_act):
            silu_value, silu_slope = silu_terms(pres[2 * block])
            gate_up_grads.append(block_grad * pres[2 * block + 1] * silu_slope)
            gate_up_grads.append(block_grad * silu_value)
        gate_up_grads = jnp.concatenate(gate_up_grads, axis=1).astype(jnp.bfloat16)
        if step_index == 0:
            own_block, far_block = jnp.split(gate_up_grads, 2, axis=1)
            gate_up_shares = [own_block, swap(far_block, 1), swap(own_block, 2), swap(far_block, 3)]
            break
        packed = packs(grad_full, [gate_up_grads])
        gate_up_grads, *packed = lax.optimization_barrier((gate_up_grads, *packed))
        partial = jnp.dot(gate_up_grads, gate_up_rows_weight, preferred_element_type=jnp.float32)
        latest = Exchange(packed)
        backward_rows.append(latest)
        if step_index == STEPS - 1:
            grad_norm = collect(partial, latest)
        else:
            wide = forward_rows[-1].gathered()[:, :half_width]
            gate_up = contract_rows(wide, backward_rows[0].gathered()[:, half_width:])
            grad_norm, gate_up = collect(partial, latest, gate_up)
        floats_in, inv_in = normalize(state_in)
        weighted = grad_norm * norm_gain
        grad_in = inv_in * weighted - floats_in * inv_in * inv_in * inv_in * jnp.mean(
            floats_in * weighted, axis=-1, keepdims=True
        )
        carried = grad_state + grad_in
    down = 0.0
    for forward, backward in zip(reversed(forward_rows), backward_rows):
        wide, act_rows = jnp.split(forward.gathered(), [half_width], axis=1)
        grads, gate_up_rows = jnp.split(backward.gathered(), [half_width], axis=1)
        if backward is not backward_rows[0]:
            gate_up = gate_up + contract_rows(wide, gate_up_rows)
        down = down + contract_rows(act_rows, grads)
    wide = jnp.concatenate([rows[:, :half_width] for rows in forward_rows[0].rows], axis=0)
    gate_up = gate_up + contract_rows(wide, jnp.concatenate(gate_up_shares, axis=0))
    core = lax.axis_index("core")
    quarter = half_width // 2

    def add_cores(partial, axis):
        mine = lax.dynamic_slice_in_dim(partial, core * quarter, quarter, axis)
        sent = lax.dynamic_slice_in_dim(partial, (1 - core) * quarter, quarter, axis)
        return mine, lax.ppermute(sent.astype(jnp.bfloat16), "core", SWAP)

    mine, received = add_cores(gate_up, 0)
    grad_gate = mine[:, :units] + received[:, :units].astype(jnp.float32)
    grad_up = mine[:, units:] + received[:, units:].astype(jnp.float32)
    other_grads, grad_gate, grad_up = lax.optimization_barrier((other_grads, grad_gate, grad_up))
    own_acts, *other_acts = [rows[:, half_width:] for rows in forward_rows[0].rows]
    other_acts = jnp.stack([acts.reshape(-1, tok_rows, units) for acts in other_acts], axis=1)
    down = down + contract_rows(own_acts, halves(grad_full)[0])
    down = down + contract_rows(other_acts.reshape(-1, units), other_grads)
    mine, received = add_cores(down, 1)
    grad_down = mine + received.astype(jnp.float32)
    return (draft_state, grad_gate, grad_up, grad_down)


def solution(mesh):
    fine = Mesh(mesh.devices.reshape(2, 2, 2, 4, 4), ALL)
    dp = ("y_lo", "core")
    return jax.shard_map(
        on_device,
        mesh=fine,
        in_specs=(
            P(ALL, None),
            P(),
            P(None, ALL),
            P(None, ALL),
            P(ALL, None),
            P(ALL, None),
            P(dp, None),
            P(),
            P(None, ROW),
            P(None, ROW),
            P(ROW, None),
        ),
        out_specs=(
            P(ALL, None),
            P(dp, ROW),
            P(dp, ROW),
            P(ROW, dp),
        ),
        check_vma=False,
    )
```

```python
import functools
import math

import jax
import jax.numpy as jnp
from jax import lax
from jax.experimental import pallas as pl
from jax.experimental.layout import Layout, with_layout_constraint
from jax.experimental.pallas import tpu as pltpu
from jax.sharding import Mesh, PartitionSpec as P

STEPS = 3
PARTS = 4
EPSILON = 1e-06

ALL = ("y_lo", "core", "y_hi", "z", "x")
ROW = ("y_hi", "z", "x")
PLANE = ("z", "x")
SWAP = [(0, 1), (1, 0)]


def normalize(incoming):
    as_float = incoming.astype(jnp.float32)
    inv_rms = lax.rsqrt(jnp.mean(as_float * as_float, axis=-1, keepdims=True) + EPSILON)
    return (as_float, inv_rms)


def silu_terms(gate_pre):
    sigmoid_v = jax.nn.sigmoid(gate_pre)
    return (gate_pre * sigmoid_v, sigmoid_v * (1.0 + gate_pre * (1.0 - sigmoid_v)))


def contract_rows(left_side, right_side):
    return lax.dot_general(
        left_side, right_side, (((0,), (0,)), ((), ())), preferred_element_type=jnp.float32
    )


def contract_cols(left_side, right_side):
    return lax.dot_general(
        left_side, right_side, (((1,), (1,)), ((), ())), preferred_element_type=jnp.float32
    )


def expert_kernel(x_ref, gate_hbm, up_hbm, down_hbm, out_ref, gate, up, down, wide, rows, sems):
    copies = [
        pltpu.make_async_copy(source, target, sems.at[i])
        for i, (source, target) in enumerate(((gate_hbm, gate), (up_hbm, up), (down_hbm, down)))
    ]
    for copy in copies:
        copy.start()
    sources, pieces, run = x_ref.shape
    capacity = rows.shape[0] // sources
    parts = pieces // capacity
    lanes = wide.shape[-1]
    for lane in range(run // lanes):
        columns = pl.ds(lane * lanes, lanes)
        wide[lane] = x_ref[:, :, columns].reshape(sources * pieces, lanes).astype(jnp.float32)
        for piece in range(pieces):
            slot, part = divmod(piece, parts)
            rows[
                pl.ds(slot * sources, sources), pl.ds(part * run + lane * lanes, lanes)
            ] = wide[lane, pl.ds(piece, sources, stride=pieces), :].astype(jnp.bfloat16)
    copies[0].wait()
    gate_pre = jnp.dot(rows[...], gate[...], preferred_element_type=jnp.float32)
    copies[1].wait()
    up_pre = jnp.dot(rows[...], up[...], preferred_element_type=jnp.float32)
    act = (gate_pre * jax.nn.sigmoid(gate_pre) * up_pre).astype(jnp.bfloat16)
    copies[2].wait()
    for part in range(parts):
        result = jnp.dot(
            act, down[:, pl.ds(part * run, run)], preferred_element_type=jnp.float32
        )
        for slot in range(capacity):
            for lane in range(run // lanes):
                wide[lane, pl.ds(slot * parts + part, sources, stride=pieces), :] = result[
                    slot * sources : (slot + 1) * sources, lane * lanes : (lane + 1) * lanes
                ]
    for lane in range(run // lanes):
        out_ref[:, :, pl.ds(lane * lanes, lanes)] = (
            wide[lane].astype(jnp.bfloat16).reshape(sources, pieces, lanes)
        )


def expert_half(arrived, w_gate, w_up, w_down, capacity):
    sources, pieces, run = arrived.shape
    width = w_gate.shape[0]
    whole = pl.BlockSpec(memory_space=pltpu.VMEM)
    far = pl.BlockSpec(memory_space=pl.ANY)
    return pl.pallas_call(
        expert_kernel,
        out_shape=jax.ShapeDtypeStruct(arrived.shape, jnp.bfloat16),
        in_specs=[whole, far, far, far],
        out_specs=whole,
        scratch_shapes=[
            pltpu.VMEM(w_gate.shape, jnp.bfloat16),
            pltpu.VMEM(w_up.shape, jnp.bfloat16),
            pltpu.VMEM(w_down.shape, jnp.bfloat16),
            pltpu.VMEM((run // 128, sources * pieces, 128), jnp.float32),
            pltpu.VMEM((sources * capacity, width), jnp.bfloat16),
            pltpu.SemaphoreType.DMA((3,)),
        ],
        compiler_params=pltpu.CompilerParams(vmem_limit_bytes=56 * 1024 * 1024),
        cost_estimate=pl.CostEstimate(
            flops=6 * sources * capacity * width * w_gate.shape[1],
            bytes_accessed=3 * w_gate.size * 2,
            transcendentals=0,
        ),
    )(arrived, w_gate, w_up, w_down)


def spread(incoming, beside):
    members = lax.axis_size("z") * lax.axis_size("x")
    copies = jnp.broadcast_to(incoming[None], (members,) + incoming.shape)
    gathered = lax.all_to_all(copies, PLANE, split_axis=0, concat_axis=0, tiled=True)
    gathered = gathered.reshape((-1, incoming.shape[-1]))
    return gathered if beside is None else beside.beside_gather(gathered)


def collect(incoming, beside, product=None):
    members = lax.axis_size("z") * lax.axis_size("x")
    parts = incoming.astype(jnp.bfloat16).reshape((members, -1, incoming.shape[-1]))
    received = lax.all_to_all(parts, PLANE, split_axis=0, concat_axis=0, tiled=True)
    if product is not None:
        received, product = lax.optimization_barrier((received, product))
    total = jnp.sum(beside.beside_sum(received).astype(jnp.float32), axis=0)
    return total if product is None else (total, product)


def halves(incoming):
    width = incoming.shape[1] // 2
    y_lo = lax.axis_index("y_lo")
    own = lax.dynamic_slice_in_dim(incoming, y_lo * width, width, 1)
    far = lax.dynamic_slice_in_dim(incoming, (1 - y_lo) * width, width, 1)
    return own, far


def swap(rows, mask):
    return lax.ppermute(rows, ("y_lo", "y_hi"), [(i, i ^ mask) for i in range(4)])


def pack_kernel(y_lo_ref, wide_ref, *refs):
    blocks, outs = refs[:-4], refs[-4:]
    half = wide_ref.shape[1] // 2
    for mask, out in enumerate(outs):
        start = pl.multiple_of((y_lo_ref[0] ^ (mask // 2)) * half, half)
        out[:, :half] = wide_ref[:, pl.ds(start, half)]
        width = half
        for block in blocks:
            size = block.shape[1] // 2
            first = mask % 2 * size
            out[:, width : width + size] = block[:, first : first + size]
            width += size


def packs(wide, blocks):
    rows = wide.shape[0]
    width = (wide.shape[1] + sum(block.shape[1] for block in blocks)) // 2
    whole = pl.BlockSpec(memory_space=pltpu.VMEM)
    out = jax.ShapeDtypeStruct((rows, width), jnp.bfloat16)
    return pl.pallas_call(
        pack_kernel,
        out_shape=[out] * 4,
        in_specs=[pl.BlockSpec(memory_space=pltpu.SMEM)] + [whole] * (1 + len(blocks)),
        out_specs=[whole] * 4,
        compiler_params=pltpu.CompilerParams(vmem_limit_bytes=8 * 1024 * 1024),
        cost_estimate=pl.CostEstimate(
            flops=0, bytes_accessed=12 * rows * width, transcendentals=0
        ),
    )(lax.axis_index("y_lo").astype(jnp.int32).reshape(1), wide, *blocks)


class Exchange:
    def __init__(self, packed):
        own, far_y_hi, *self.later = packed
        self.rows = [own, swap(far_y_hi, 1)]

    def beside_sum(self, received):
        received, self.rows[1], *self.later = lax.optimization_barrier(
            (received, self.rows[1], *self.later)
        )
        self.rows += [swap(self.later[0], 2), swap(self.later[1], 3)]
        return received

    def beside_gather(self, gathered):
        gathered, *self.rows[2:] = lax.optimization_barrier((gathered, *self.rows[2:]))
        return gathered

    def gathered(self):
        return jnp.concatenate(self.rows, axis=0)


def fetch_half(weight):
    half = weight.shape[0] // 2
    core = lax.axis_index("core")
    mine = lax.dynamic_slice_in_dim(weight, core * half, half, 0)
    return lax.ppermute(mine, ("y_lo", "y_hi"), [(0, 3), (3, 0), (1, 2), (2, 1)])


def assemble_kernel(axis, core_ref, *refs):
    out, sems = refs[-2:]
    count = (len(refs) - 2) // 3
    size = refs[0].shape[axis]
    half = refs[count].shape[0]
    core = core_ref[0]
    places = []

    def place(source, block, start):
        rows = source.shape[0]
        if axis == 1:
            target = out.at[pl.ds(start, rows), pl.ds(block * size, size)]
        else:
            target = out.at[pl.ds(block * size + start, rows), :]
        places.append((source, target))

    for i in range(count):
        place(refs[i], i, 0)
        place(refs[count + i], count + i, pl.multiple_of(core * half, half))
        place(refs[2 * count + i], count + i, pl.multiple_of((1 - core) * half, half))
    copies = [
        pltpu.make_async_copy(source, target, sems.at[k])
        for k, (source, target) in enumerate(places)
    ]
    for copy in copies:
        copy.start()
    for copy in copies:
        copy.wait()


def assemble(owns, fetched, axis):
    swapped = [lax.ppermute(half, "core", SWAP) for half in fetched]
    shape = list(owns[0].shape)
    shape[axis] *= 2 * len(owns)
    far = pl.BlockSpec(memory_space=pl.ANY)
    parts = [*owns, *fetched, *swapped]
    return pl.pallas_call(
        functools.partial(assemble_kernel, axis),
        out_shape=jax.ShapeDtypeStruct(tuple(shape), jnp.bfloat16),
        in_specs=[pl.BlockSpec(memory_space=pltpu.SMEM)] + [far] * len(parts),
        out_specs=pl.BlockSpec(memory_space=pltpu.VMEM),
        scratch_shapes=[pltpu.SemaphoreType.DMA((len(parts),))],
        compiler_params=pltpu.CompilerParams(vmem_limit_bytes=20 * 1024 * 1024),
        cost_estimate=pl.CostEstimate(
            flops=0, bytes_accessed=4 * math.prod(shape), transcendentals=0
        ),
    )(lax.axis_index("core").astype(jnp.int32).reshape(1), *parts)


def on_device(
    hidden_in,
    router_weight,
    expert_gate,
    expert_up,
    expert_down,
    expert_ids,
    segment_ids,
    draft_gain,
    draft_gate,
    draft_up,
    draft_down,
):
    tok_rows = hidden_in.shape[0]
    model_width = hidden_in.shape[1]
    top_count = expert_ids.shape[1]
    experts = router_weight.shape[1]
    capacity = 2 * ((tok_rows * top_count + experts - 1) // experts)
    token_count = tok_rows * lax.axis_size(ALL)
    fetches = [fetch_half(weight) for weight in (draft_gate, draft_up, draft_down)]
    as_float, inv_rms = normalize(hidden_in)
    normed = (as_float * inv_rms).astype(jnp.bfloat16)
    logits = jnp.dot(normed, router_weight, preferred_element_type=jnp.float32)
    chosen = jnp.take_along_axis(logits, expert_ids, axis=1)
    weights = jnp.exp(chosen)
    route_probs = weights / jnp.sum(weights, axis=1, keepdims=True)
    flat_ids = expert_ids.reshape(-1)
    choice_range = jnp.arange(flat_ids.shape[0], dtype=jnp.int32)
    earlier = (flat_ids[:, None] == flat_ids[None, :]) & (
        choice_range[None, :] < choice_range[:, None]
    )
    slots = flat_ids * capacity + jnp.sum(earlier.astype(jnp.int32), axis=1)
    lines = experts * 2 * capacity * PARTS
    line = jnp.arange(lines, dtype=jnp.int32)
    line_slot = line // (2 * capacity * PARTS) * capacity + line // PARTS % capacity
    piece_slots = jnp.repeat(slots.reshape(tok_rows, top_count), PARTS, axis=0)
    piece_probs = jnp.repeat(route_probs, PARTS, axis=0)
    piece_part = jnp.arange(tok_rows * PARTS, dtype=jnp.int32) % PARTS
    same_part = piece_part[:, None] == (line % PARTS)[None, :]
    hits = [same_part & (piece_slots[:, k : k + 1] == line_slot[None, :]) for k in range(top_count)]
    picker = sum(hit.astype(jnp.float32) for hit in hits).astype(jnp.bfloat16)
    mixer = sum(jnp.where(hit, piece_probs[:, k : k + 1], 0.0) for k, hit in enumerate(hits))
    pieces = normed.reshape(tok_rows * PARTS, model_width // PARTS)
    doubled = contract_rows(picker, pieces).astype(jnp.bfloat16)
    doubled = doubled.reshape(2 * experts, capacity * PARTS, model_width // PARTS)
    arrived = lax.all_to_all(doubled, ALL, split_axis=0, concat_axis=0, tiled=True)
    arrived, fetches[0] = lax.optimization_barrier((arrived, fetches[0]))
    half_parts = expert_half(arrived, expert_gate, expert_up, expert_down, capacity)
    half_parts, fetches[1] = lax.optimization_barrier((half_parts, fetches[1]))
    returned = lax.all_to_all(half_parts, ALL, split_axis=0, concat_axis=0, tiled=True)
    gate_up_weight = assemble([draft_gate, draft_up], fetches[:2], 1)
    returned, gate_up_weight = lax.optimization_barrier((returned, gate_up_weight))
    returned = returned.reshape(lines, model_width // PARTS)
    first = mixer.astype(jnp.bfloat16)
    rest = mixer - first.astype(jnp.float32)
    second = rest.astype(jnp.bfloat16)
    third = (rest - second.astype(jnp.float32)).astype(jnp.bfloat16)
    mixed = jnp.dot(
        jnp.concatenate([first, second, third], axis=0),
        returned,
        preferred_element_type=jnp.float32,
    )
    moe_out = jnp.sum(mixed.reshape(3, tok_rows * PARTS, -1), axis=0).reshape(tok_rows, model_width)
    top_state = (as_float + moe_out).astype(jnp.bfloat16)
    units = draft_gate.shape[1]
    half_width = model_width // 2
    norm_gain = draft_gain.astype(jnp.float32)
    segments = segment_ids[0]
    row_size = lax.axis_size(ROW)
    row_start = lax.axis_index(ROW) * tok_rows
    seg_pad = jnp.concatenate([segments, jnp.full((STEPS,), -1, jnp.int32)], axis=0)
    own_segments = lax.dynamic_slice_in_dim(segments, row_start, tok_rows, 0)
    loss_scale = 1.0 / math.sqrt(token_count)
    following = lax.ppermute(
        top_state, ROW, [(i, (i + row_size - 1) % row_size) for i in range(row_size)]
    )
    draft_state = top_state
    saved_steps, forward_rows = [], []
    latest = None
    for step_index in range(STEPS):
        floats_in, inv_in = normalize(draft_state)
        draft_norm = spread((floats_in * inv_in * norm_gain).astype(jnp.bfloat16), latest)
        if step_index == 1:
            draft_norm, gate_up_rows_weight = lax.optimization_barrier(
                (draft_norm, with_layout_constraint(gate_up_weight.T, Layout((0, 1))))
            )
        if step_index == 0:
            draft_norm, fetches[2], following = lax.optimization_barrier(
                (draft_norm, fetches[2], following)
            )
            high_pad = jnp.concatenate([top_state, following], axis=0)
            down_weight = assemble([draft_down], fetches[2:], 0)
        pres = jnp.split(
            jnp.dot(draft_norm, gate_up_weight, preferred_element_type=jnp.float32), 4, axis=1
        )
        acts = jnp.concatenate(
            [jax.nn.silu(pres[0]) * pres[1], jax.nn.silu(pres[2]) * pres[3]], axis=1
        ).astype(jnp.bfloat16)
        packed = packs(draft_norm, [acts])
        acts, *packed = lax.optimization_barrier((acts, *packed))
        partial = jnp.dot(acts, down_weight, preferred_element_type=jnp.float32)
        latest = Exchange(packed)
        forward_rows.append(latest)
        summed = collect(partial, latest)
        new_state = (floats_in + summed).astype(jnp.bfloat16)
        saved_steps.append((draft_state, pres, new_state))
        draft_state = new_state
    carried = jnp.zeros((tok_rows, model_width), jnp.float32)
    backward_rows = []
    for step_index in reversed(range(STEPS)):
        state_in, pres, state_out = saved_steps[step_index]
        ahead = step_index + 1
        target_rows = high_pad[ahead : ahead + tok_rows]
        same_doc = lax.dynamic_slice_in_dim(seg_pad, row_start + ahead, tok_rows, 0) == own_segments
        grad_state = carried + loss_scale * jnp.where(
            same_doc[:, None], state_out.astype(jnp.float32) - target_rows.astype(jnp.float32), 0.0
        )
        own_rows = grad_state.astype(jnp.bfloat16)
        grad_full = spread(own_rows, latest)
        if step_index == 0:
            own_half, far_half = halves(own_rows)
            others = [swap(own_half, 1), swap(far_half, 2), swap(far_half, 3)]
            grad_full, *others = lax.optimization_barrier((grad_full, *others))
            other_grads = spread(jnp.concatenate(others, axis=0), None)
        grad_act = jnp.split(contract_cols(grad_full, down_weight), 2, axis=1)
        gate_up_grads = []
        for block, block_grad in enumerate(grad_act):
            silu_value, silu_slope = silu_terms(pres[2 * block])
            gate_up_grads.append(block_grad * pres[2 * block + 1] * silu_slope)
            gate_up_grads.append(block_grad * silu_value)
        gate_up_grads = jnp.concatenate(gate_up_grads, axis=1).astype(jnp.bfloat16)
        if step_index == 0:
            own_block, far_block = jnp.split(gate_up_grads, 2, axis=1)
            gate_up_shares = [own_block, swap(far_block, 1), swap(own_block, 2), swap(far_block, 3)]
            break
        packed = packs(grad_full, [gate_up_grads])
        gate_up_grads, *packed = lax.optimization_barrier((gate_up_grads, *packed))
        partial = jnp.dot(gate_up_grads, gate_up_rows_weight, preferred_element_type=jnp.float32)
        latest = Exchange(packed)
        backward_rows.append(latest)
        if step_index == STEPS - 1:
            grad_norm = collect(partial, latest)
        else:
            wide = forward_rows[-1].gathered()[:, :half_width]
            gate_up = contract_rows(wide, backward_rows[0].gathered()[:, half_width:])
            grad_norm, gate_up = collect(partial, latest, gate_up)
        floats_in, inv_in = normalize(state_in)
        weighted = grad_norm * norm_gain
        grad_in = inv_in * weighted - floats_in * inv_in * inv_in * inv_in * jnp.mean(
            floats_in * weighted, axis=-1, keepdims=True
        )
        carried = grad_state + grad_in
    down = 0.0
    for forward, backward in zip(reversed(forward_rows), backward_rows):
        wide, act_rows = jnp.split(forward.gathered(), [half_width], axis=1)
        grads, gate_up_rows = jnp.split(backward.gathered(), [half_width], axis=1)
        if backward is not backward_rows[0]:
            gate_up = gate_up + contract_rows(wide, gate_up_rows)
        down = down + contract_rows(act_rows, grads)
    wide = jnp.concatenate([rows[:, :half_width] for rows in forward_rows[0].rows], axis=0)
    gate_up = gate_up + contract_rows(wide, jnp.concatenate(gate_up_shares, axis=0))
    core = lax.axis_index("core")
    quarter = half_width // 2

    def add_cores(partial, axis):
        mine = lax.dynamic_slice_in_dim(partial, core * quarter, quarter, axis)
        sent = lax.dynamic_slice_in_dim(partial, (1 - core) * quarter, quarter, axis)
        return mine, lax.ppermute(sent.astype(jnp.bfloat16), "core", SWAP)

    mine, received = add_cores(gate_up, 0)
    grad_gate = mine[:, :units] + received[:, :units].astype(jnp.float32)
    grad_up = mine[:, units:] + received[:, units:].astype(jnp.float32)
    other_grads, grad_gate, grad_up = lax.optimization_barrier((other_grads, grad_gate, grad_up))
    own_acts, *other_acts = [rows[:, half_width:] for rows in forward_rows[0].rows]
    other_acts = jnp.stack([acts.reshape(-1, tok_rows, units) for acts in other_acts], axis=1)
    down = down + contract_rows(own_acts, halves(grad_full)[0])
    down = down + contract_rows(other_acts.reshape(-1, units), other_grads)
    mine, received = add_cores(down, 1)
    grad_down = mine + received.astype(jnp.float32)
    return (draft_state, grad_gate, grad_up, grad_down)


def solution(mesh):
    fine = Mesh(mesh.devices.reshape(2, 2, 2, 4, 4), ALL)
    dp = ("y_lo", "core")
    return jax.shard_map(
        on_device,
        mesh=fine,
        in_specs=(
            P(ALL, None),
            P(),
            P(None, ALL),
            P(None, ALL),
            P(ALL, None),
            P(ALL, None),
            P(dp, None),
            P(),
            P(None, ROW),
            P(None, ROW),
            P(ROW, None),
        ),
        out_specs=(
            P(ALL, None),
            P(dp, ROW),
            P(dp, ROW),
            P(ROW, dp),
        ),
        check_vma=False,
    )
```
